32 devices in a mesh: seq: 4 (over y, x), fsdp: 8 (over z, core).
Axes of the slice: x: 2, y: 2, z: 4, core: 2. Of those that a mesh axis runs over, the one named last changes fastest.
Arguments:
- hidden_in: bfloat16 [8, 1024, 2048], P('fsdp', 'seq'), may hold values from -6 to 6
- segments: int32 [8, 1024], P('fsdp'), may hold values from 0 to 2, as said below
- out_grad: bfloat16 [8, 1024, 2048], P('fsdp', 'seq'), may hold values from -6 to 6
- norm1_gain: bfloat16 [2048], P(('seq', 'fsdp')), may hold values from 0.25 to 1.75
- w_query: bfloat16 [2048, 1024], P(('seq', 'fsdp')), may hold values from -0.125 to 0.125
- w_keyval: bfloat16 [2048, 512], P(('seq', 'fsdp')), may hold values from -0.125 to 0.125
- w_attn_out: bfloat16 [1024, 2048], P(('seq', 'fsdp')), may hold values from -0.75 to 0.75
- w_gate_z: bfloat16 [2048, 3072], P(('seq', 'fsdp')), may hold values from -0.125 to 0.125
- w_ssm_x: bfloat16 [2048, 3072], P(('seq', 'fsdp')), may hold values from -0.125 to 0.125
- w_ssm_bc: bfloat16 [2048, 512], P(('seq', 'fsdp')), may hold values from -0.125 to 0.125
- w_ssm_dt: bfloat16 [2048, 48], P(('seq', 'fsdp')), may hold values from -0.0625 to 0.0625
- conv_taps: bfloat16 [3584, 5], P(('seq', 'fsdp')), may hold values from -0.59765625 to 0.59765625
- a_log: float32 [48], replicated, may hold values from 0 to 1.4
- dt_bias: float32 [48], replicated, may hold values from -6 to -3
- skip_gain: float32 [48], replicated, may hold values from 0.5 to 1.5
- ssm_gain: bfloat16 [3072], P(('seq', 'fsdp')), may hold values from 0.25 to 1.75
- w_ssm_out: bfloat16 [3072, 2048], P(('seq', 'fsdp')), may hold values from -0.109375 to 0.109375
- norm2_gain: bfloat16 [2048], P(('seq', 'fsdp')), may hold values from 0.25 to 1.75
- w_ff_gate: bfloat16 [2048, 4096], P(('seq', 'fsdp')), may hold values from -0.125 to 0.125
- w_ff_up: bfloat16 [2048, 4096], P(('seq', 'fsdp')), may hold values from -0.125 to 0.125
- w_ff_down: bfloat16 [4096, 2048], P(('seq', 'fsdp')), may hold values from -0.09375 to 0.09375
Outputs:
- layer_out: bfloat16 [8, 1024, 2048], P('fsdp', 'seq')
- grad_in: bfloat16 [8, 1024, 2048], P('fsdp', 'seq')
- grad_norm1_gain: float32 [2048], P(('seq', 'fsdp'))
- grad_w_query: float32 [2048, 1024], P(('seq', 'fsdp'))
- grad_w_keyval: float32 [2048, 512], P(('seq', 'fsdp'))
- grad_w_attn_out: float32 [1024, 2048], P(('seq', 'fsdp'))
- grad_w_gate_z: float32 [2048, 3072], P(('seq', 'fsdp'))
- grad_w_ssm_x: float32 [2048, 3072], P(('seq', 'fsdp'))
- grad_w_ssm_bc: float32 [2048, 512], P(('seq', 'fsdp'))
- grad_w_ssm_dt: float32 [2048, 48], P(('seq', 'fsdp'))
- grad_conv_taps: float32 [3584, 5], P(('seq', 'fsdp'))
- grad_a_log: float32 [48], replicated
- grad_dt_bias: float32 [48], replicated
- grad_skip_gain: float32 [48], replicated
- grad_ssm_gain: float32 [3072], P(('seq', 'fsdp'))
- grad_w_ssm_out: float32 [3072, 2048], P(('seq', 'fsdp'))
- grad_norm2_gain: float32 [2048], P(('seq', 'fsdp'))
- grad_w_ff_gate: float32 [2048, 4096], P(('seq', 'fsdp'))
- grad_w_ff_up: float32 [2048, 4096], P(('seq', 'fsdp'))
- grad_w_ff_down: float32 [4096, 2048], P(('seq', 'fsdp'))
The draws below stay inside these ranges and needn't reach their ends.
Inputs may be any that keep to these rules, and one draw needn't show every extreme that they name: `segments`: along each row the ids never fall: documents 0, 1 and 2 in this order, each of one token or more; document 1 covers all but 1 to max(1, 64) tokens at each end of the row.
All inputs are finite; a program needn't handle non-finite values.
Results may differ from the reference program's by a relative error of at most 0.018.
Values may be sent and summed in bfloat16 or wider, within the bound.
No kernel may reach another device: no remote copies, remote signals or barrier semaphores. Data moves between devices by JAX's collectives and lax.ppermute only.
A program may use at most 448 MiB of HBM per device.

```python
import jax
import jax.numpy as jnp
from jax import lax

D = 2048
HEADS = 8
KV_HEADS = 2
HEAD_DIM = 128
SSM_HEADS = 48
SSM_DIM = 64
STATE = 256
CONV = 4
FF = 4096
LENGTH = 1024
SEQS = 8
DSSM = 3072
XBC = 3584


def draw_segments(key, part):
    key = jax.random.fold_in(key, 7)
    first_key, last_key = jax.random.split(key)
    margin = max(LENGTH // 16, 1)
    starts = jax.random.randint(first_key, (SEQS, 1), 1, margin + 1)
    finish = LENGTH - jax.random.randint(last_key, (SEQS, 1), 1, margin + 1)
    places = jnp.arange(LENGTH, dtype=jnp.int32)[None, :]
    return (places >= starts).astype(jnp.int32) + (places >= finish).astype(jnp.int32)


def shard_levels(own_key, extent, shards, low, largest):
    def one(position, parts):
        heights = jax.random.uniform(jax.random.fold_in(jax.random.fold_in(own_key, 6), position), (parts,), jnp.float32, low / len(shards), largest / len(shards))
        return jnp.repeat(jnp.exp(heights), extent[position] // parts).reshape((-1,) + (1,) * (len(extent) - position - 1))

    level = one(*shards[0])
    for cut in shards[1:]:
        level = level * one(*cut)
    return level


def gaussian(key, extent, width, bound, shards=(), held_as=jnp.bfloat16):
    drawn = jax.random.normal(key, extent, jnp.float32) * width
    if len(shards) > 0:
        drawn = shard_levels(key, extent, shards, -0.22, 0.18) * drawn
    return jnp.clip(drawn, min=-bound, max=bound).astype(held_as)


def setup_inputs(seed: int = 0) -> dict:
    key_of = jax.random.split(jax.random.key(seed), 22)
    hidden_in = gaussian(key_of[0], (SEQS, LENGTH, D), 1.0, 6.0, ((0, 8), (1, 4)))
    segments = draw_segments(jax.random.fold_in(key_of[21], 71), 0)
    out_grad = gaussian(key_of[2], (SEQS, LENGTH, D), 1.0, 6.0, ((0, 8), (1, 4)))
    norm1_gain = jnp.clip(1.0 + 0.15 * jax.random.normal(key_of[3], (D,), jnp.float32), 0.25, 1.75).astype(jnp.bfloat16)
    w_query = gaussian(key_of[4], (D, HEADS * HEAD_DIM), D ** -0.5, 0.125, ((0, 32),))
    w_keyval = gaussian(key_of[5], (D, 2 * KV_HEADS * HEAD_DIM), D ** -0.5, 0.125, ((0, 32),))
    w_attn_out = gaussian(key_of[6], (HEADS * HEAD_DIM, D), (HEADS * HEAD_DIM // 16) ** -0.5, 0.75, ((0, 32),))
    w_gate_z = gaussian(key_of[7], (D, DSSM), D ** -0.5, 0.125, ((0, 32),))
    w_ssm_x = gaussian(key_of[8], (D, DSSM), D ** -0.5, 0.125, ((0, 32),))
    w_ssm_bc = gaussian(key_of[9], (D, 2 * STATE), D ** -0.5, 0.125, ((0, 32),))
    w_ssm_dt = gaussian(key_of[10], (D, SSM_HEADS), (4 * D) ** -0.5, 0.0625, ((0, 32),))
    conv_taps = jnp.clip(jax.random.uniform(key_of[11], (XBC, CONV + 1), jnp.float32, -0.59765625, 0.59765625) * shard_levels(key_of[11], (XBC, CONV + 1), ((0, 32),), -0.4, 0.0), -0.59765625, 0.59765625).astype(jnp.bfloat16)
    a_log = jnp.clip(jax.random.uniform(key_of[12], (SSM_HEADS,), jnp.float32, 0.0, 1.4), 0.0, 1.4)
    dt_bias = jnp.clip(jax.random.uniform(key_of[13], (SSM_HEADS,), jnp.float32, -6.0, -3.0), -6.0, -3.0)
    skip_gain = jnp.clip(jax.random.uniform(key_of[14], (SSM_HEADS,), jnp.float32, 0.5, 1.5), 0.5, 1.5)
    ssm_gain = jnp.clip(1.0 + 0.15 * jax.random.normal(key_of[15], (DSSM,), jnp.float32), 0.25, 1.75).astype(jnp.bfloat16)
    w_ssm_out = gaussian(key_of[16], (DSSM, D), DSSM ** -0.5, 0.109375, ((0, 32),))
    norm2_gain = jnp.clip(1.0 + 0.15 * jax.random.normal(key_of[17], (D,), jnp.float32), 0.25, 1.75).astype(jnp.bfloat16)
    w_ff_gate = gaussian(key_of[18], (D, FF), D ** -0.5, 0.125, ((0, 32),))
    w_ff_up = gaussian(key_of[19], (D, FF), D ** -0.5, 0.125, ((0, 32),))
    w_ff_down = gaussian(key_of[20], (FF, D), FF ** -0.5, 0.09375, ((0, 32),))
    return dict(hidden_in=hidden_in, segments=segments, out_grad=out_grad, norm1_gain=norm1_gain, w_query=w_query, w_keyval=w_keyval, w_attn_out=w_attn_out, w_gate_z=w_gate_z, w_ssm_x=w_ssm_x, w_ssm_bc=w_ssm_bc, w_ssm_dt=w_ssm_dt, conv_taps=conv_taps, a_log=a_log, dt_bias=dt_bias, skip_gain=skip_gain, ssm_gain=ssm_gain, w_ssm_out=w_ssm_out, norm2_gain=norm2_gain, w_ff_gate=w_ff_gate, w_ff_up=w_ff_up, w_ff_down=w_ff_down)


@jax.custom_vjp
def low(v):
    return lax.optimization_barrier(v.astype(jnp.bfloat16)).astype(jnp.float32)

@jax.custom_vjp
def low_back(v):
    return v

def low_keep(v):
    return (low(v), None)

def low_pass(kept, grad):
    return (grad,)

def back_keep(v):
    return (v, None)

def back_low(kept, grad):
    return (low(grad),)
low.defvjp(low_keep, low_pass)
low_back.defvjp(back_keep, back_low)
epsilon = 1e-05
rope_base = 10000.0
masked_score = -1e+30

def matmul(left_op, right_op):
    return jnp.dot(left_op, right_op, precision=lax.Precision.HIGHEST, preferred_element_type=jnp.float32)

def rms_scale(row_data, gain_vec):
    return row_data * lax.rsqrt(lax.optimization_barrier(jnp.mean(row_data * row_data, axis=-1, keepdims=True)) + epsilon) * gain_vec

def gated_norm(ssm_vals, gate_vals, gain_vec):
    return rms_scale(ssm_vals * jax.nn.silu(gate_vals), gain_vec)

def swiglu(gate_vals, up_vals):
    return jax.nn.silu(gate_vals) * up_vals

def rope_tables(length, head_dim):
    half_dim = head_dim // 2
    frequency = rope_base ** (-jnp.arange(half_dim, dtype=jnp.float32) / half_dim)
    angles = jnp.arange(length, dtype=jnp.float32)[:, None] * frequency[None, :]
    return (jnp.cos(angles)[:, None, :], jnp.sin(angles)[:, None, :])

def rotate(values, cosine, sine_part, turn_sign):
    half_dim = values.shape[-1] // 2
    lower_half = values[..., :half_dim]
    upper_half = values[..., half_dim:]
    return jnp.concatenate([lower_half * cosine - turn_sign * upper_half * sine_part, upper_half * cosine + turn_sign * lower_half * sine_part], axis=-1)

def causal_conv(signal, conv_weights, seg_row):
    length = signal.shape[0]
    taps_count = conv_weights.shape[1] - 1
    padded = jnp.pad(signal, ((taps_count - 1, 0), (0, 0)))
    seg_padded = jnp.pad(seg_row, (taps_count - 1, 0), constant_values=-1)
    result = jnp.zeros_like(signal) + conv_weights[:, taps_count][None, :]
    for offset in range(taps_count):
        same_doc = (seg_padded[offset:offset + length] == seg_row).astype(signal.dtype)
        result = result + padded[offset:offset + length] * same_doc[:, None] * conv_weights[:, offset][None, :]
    return jax.nn.silu(result)

def step_chain(dt_raw, bias_vec, alog_vec):
    dt_step = jax.nn.softplus(dt_raw + bias_vec[None, :])
    return (dt_step, jnp.cumsum(dt_step * jnp.exp(alog_vec)[None, :], axis=0))

def block_mask(row_start, block_rows, seg_row):
    length = seg_row.shape[0]
    row_pos = row_start + jnp.arange(block_rows, dtype=jnp.int32)
    col_pos = jnp.arange(length, dtype=jnp.int32)
    row_seg = lax.dynamic_slice_in_dim(seg_row, row_start, block_rows, 0)
    return (row_pos[:, None] >= col_pos[None, :]) & (row_seg[:, None] == seg_row[None, :])

def decay_block(decay_sum, row_start, block_rows, allowed):
    sum_rows = lax.dynamic_slice_in_dim(decay_sum, row_start, block_rows, 0)
    spread_gap = sum_rows.T[:, :, None] - decay_sum.T[:, None, :]
    mask_all = allowed[None, :, :]
    return jnp.where(mask_all, jnp.exp(-jnp.where(mask_all, spread_gap, 0.0)), 0.0)

def block_starts(length, block_rows):
    return jnp.arange(length // block_rows, dtype=jnp.int32) * block_rows

def attend_sequence(seq_items):
    q_seq, k_seq, v_seq, seg_row = seq_items
    cosine, sine_part = rope_tables(LENGTH, HEAD_DIM)
    q_rot = low(rotate(q_seq, cosine, sine_part, 1.0))
    k_rot = low(rotate(k_seq, cosine, sine_part, 1.0))
    block_rows = min(512, LENGTH)
    score_scale = HEAD_DIM ** (-0.5)

    def one_block(row_start):
        q_blk = lax.dynamic_slice_in_dim(q_rot, row_start, block_rows, 0)
        scores = low_back(jnp.einsum('qhd,khd->hqk', q_blk, k_rot, precision=lax.Precision.HIGHEST) * score_scale)
        allowed = block_mask(row_start, block_rows, seg_row)
        scores = jnp.where(allowed[None], scores, masked_score)
        prob_vals = jax.nn.softmax(scores, axis=-1)
        mixed = jnp.einsum('hqk,khd->qhd', low(prob_vals), v_seq, precision=lax.Precision.HIGHEST)
        return low(low_back(mixed))
    outputs = lax.map(jax.checkpoint(one_block), block_starts(LENGTH, block_rows))
    return outputs.reshape(LENGTH, HEADS * HEAD_DIM)

def ssd_sequence(x_seq, bc_seq, dt_seq, seg_row, conv_taps, a_log, dt_bias, skip_gain):
    mixed_x = causal_conv(x_seq, conv_taps[:DSSM], seg_row)
    mixed_bc = causal_conv(bc_seq, conv_taps[DSSM:], seg_row)
    in_b = low(mixed_bc[:, :STATE])
    out_c = low(mixed_bc[:, STATE:])
    dt_step, decay_sum = step_chain(dt_seq, dt_bias, a_log)
    heads_x = mixed_x.reshape(LENGTH, SSM_HEADS, SSM_DIM)
    scaled_x = low(heads_x * dt_step[:, :, None])
    block_rows = min(512, LENGTH)

    def one_block(row_start):
        allowed = block_mask(row_start, block_rows, seg_row)
        c_blk = lax.dynamic_slice_in_dim(out_c, row_start, block_rows, 0)
        intersection = matmul(c_blk, in_b.T)
        per_head = low_back(jnp.broadcast_to(intersection[None], (SSM_HEADS, block_rows, LENGTH)))
        decay = decay_block(decay_sum, row_start, block_rows, allowed)
        ssm_weights = low(per_head * decay)
        mixed = jnp.einsum('hqk,khd->qhd', ssm_weights, scaled_x, precision=lax.Precision.HIGHEST)
        x_blk = lax.dynamic_slice_in_dim(heads_x, row_start, block_rows, 0)
        return low(low_back(mixed + skip_gain[None, :, None] * x_blk))
    outputs = lax.map(jax.checkpoint(one_block), block_starts(LENGTH, block_rows))
    return outputs.reshape(LENGTH, DSSM)

def layer(hidden, params, segments):
    norm1_gain, w_query, w_keyval, w_attn_out, w_gate_z, w_ssm_x, w_ssm_bc, w_ssm_dt, conv_taps, a_log, dt_bias, skip_gain, ssm_gain, w_ssm_out, norm2_gain, w_ff_gate, w_ff_up, w_ff_down = params
    total_rows = SEQS * LENGTH
    flat = hidden.reshape(total_rows, D)
    normed = low(rms_scale(flat, norm1_gain))
    queries = low(low_back(matmul(normed, w_query)))
    keyval = low(low_back(matmul(normed, w_keyval)))
    gate_z = low_back(matmul(normed, w_gate_z))
    ssm_x = low(low_back(matmul(normed, w_ssm_x)))
    ssm_bc = low(low_back(matmul(normed, w_ssm_bc)))
    ssm_dt = low(low_back(matmul(normed, w_ssm_dt)))
    group_size = HEADS // KV_HEADS
    kv_width = KV_HEADS * HEAD_DIM
    key_rep = low_back(jnp.repeat(keyval[:, :kv_width].reshape(total_rows, KV_HEADS, HEAD_DIM), group_size, axis=1))
    val_rep = low_back(jnp.repeat(keyval[:, kv_width:].reshape(total_rows, KV_HEADS, HEAD_DIM), group_size, axis=1))
    head_shape = (SEQS, LENGTH, HEADS, HEAD_DIM)
    attn_rows = lax.map(attend_sequence, (queries.reshape(head_shape), key_rep.reshape(head_shape), val_rep.reshape(head_shape), segments))

    def ssd_item(seq_items):
        return ssd_sequence(seq_items[0], seq_items[1], seq_items[2], seq_items[3], conv_taps, a_log, dt_bias, skip_gain)
    ssm_rows = lax.map(ssd_item, (ssm_x.reshape(SEQS, LENGTH, DSSM), ssm_bc.reshape(SEQS, LENGTH, 2 * STATE), ssm_dt.reshape(SEQS, LENGTH, SSM_HEADS), segments))
    attn_out = low_back(matmul(attn_rows.reshape(total_rows, HEADS * HEAD_DIM), w_attn_out))
    ssm_in = low(gated_norm(ssm_rows.reshape(total_rows, DSSM), gate_z, ssm_gain))
    ssm_out = low_back(matmul(ssm_in, w_ssm_out))
    middle = flat + attn_out + ssm_out
    normed2 = low(rms_scale(middle, norm2_gain))
    gate_ff = low_back(matmul(normed2, w_ff_gate))
    up_ff = low_back(matmul(normed2, w_ff_up))
    act = low(swiglu(gate_ff, up_ff))
    ff_out = low_back(matmul(act, w_ff_down))
    return (middle + ff_out).reshape(SEQS, LENGTH, D)

def reference(hidden_in, segments, out_grad, norm1_gain, w_query, w_keyval, w_attn_out, w_gate_z, w_ssm_x, w_ssm_bc, w_ssm_dt, conv_taps, a_log, dt_bias, skip_gain, ssm_gain, w_ssm_out, norm2_gain, w_ff_gate, w_ff_up, w_ff_down):
    params = tuple((argument_array.astype(jnp.float32) for argument_array in (norm1_gain, w_query, w_keyval, w_attn_out, w_gate_z, w_ssm_x, w_ssm_bc, w_ssm_dt, conv_taps, a_log, dt_bias, skip_gain, ssm_gain, w_ssm_out, norm2_gain, w_ff_gate, w_ff_up, w_ff_down)))

    def wrapped(hidden, weights):
        return layer(hidden, weights, segments)
    result, pullback = jax.vjp(wrapped, hidden_in.astype(jnp.float32), params)
    grad_hidden, grads = pullback(out_grad.astype(jnp.float32))
    return (result.astype(jnp.bfloat16), grad_hidden.astype(jnp.bfloat16), grads[0], grads[1], grads[2], grads[3], grads[4], grads[5], grads[6], grads[7], grads[8], grads[9], grads[10], grads[11], grads[12], grads[13], grads[14], grads[15], grads[16], grads[17])
```

```python
import functools

import jax
import jax.numpy as jnp
from jax import lax
from jax.sharding import PartitionSpec as P

HEADS = 8
KV_HEADS = 2
HEAD_DIM = 128
SSM_DIM = 64
STATE = 256


epsilon = 1e-05
rope_base = 10000.0
masked_score = -1e30


def mat_product(left_op, right_op):
    return jnp.dot(left_op, right_op, preferred_element_type=jnp.float32)


def weight_grad(left_op, right_op):
    return lax.dot_general(
        left_op, right_op, (((0,), (0,)), ((), ())), preferred_element_type=jnp.float32
    )


def input_grad(grad_rows, weights):
    return lax.dot_general(
        grad_rows, weights, (((1,), (1,)), ((), ())), preferred_element_type=jnp.float32
    )


def rms_scale(row_data, gain_vec):
    return (
        row_data
        * lax.rsqrt(jnp.mean(row_data * row_data, axis=-1, keepdims=True) + epsilon)
        * gain_vec
    )


def gated_norm(ssm_vals, gate_vals, gain_vec):
    return rms_scale(ssm_vals * jax.nn.silu(gate_vals), gain_vec)


def swiglu(gate_vals, up_vals):
    return jax.nn.silu(gate_vals) * up_vals


def rope_tables(length, head_dim):
    half_dim = head_dim // 2
    frequency = rope_base ** (-jnp.arange(half_dim, dtype=jnp.float32) / half_dim)
    angles = jnp.arange(length, dtype=jnp.float32)[:, None] * frequency[None, :]
    return (jnp.cos(angles)[:, None, :], jnp.sin(angles)[:, None, :])


def rotate(values, cosine, sine_part, turn_sign):
    half_dim = values.shape[-1] // 2
    lower_half = values[..., :half_dim]
    upper_half = values[..., half_dim:]
    return jnp.concatenate(
        [
            lower_half * cosine - turn_sign * upper_half * sine_part,
            upper_half * cosine + turn_sign * lower_half * sine_part,
        ],
        axis=-1,
    )


def causal_conv(signal, conv_weights, seg_row):
    length = signal.shape[0]
    taps_count = conv_weights.shape[1] - 1
    padded = jnp.pad(signal, ((taps_count - 1, 0), (0, 0)))
    seg_padded = jnp.pad(seg_row, (taps_count - 1, 0), constant_values=-1)
    result = jnp.zeros_like(signal) + conv_weights[:, taps_count][None, :]
    for offset in range(taps_count):
        same_doc = (seg_padded[offset : offset + length] == seg_row).astype(signal.dtype)
        result = (
            result
            + padded[offset : offset + length]
            * same_doc[:, None]
            * conv_weights[:, offset][None, :]
        )
    return jax.nn.silu(result)


def step_chain(dt_raw, bias_vec, alog_vec):
    dt_step = jax.nn.softplus(dt_raw + bias_vec[None, :])
    return (dt_step, jnp.cumsum(dt_step * jnp.exp(alog_vec)[None, :], axis=0))


def block_mask(row_start, block_rows, seg_row):
    length = seg_row.shape[0]
    row_pos = row_start + jnp.arange(block_rows, dtype=jnp.int32)
    col_pos = jnp.arange(length, dtype=jnp.int32)
    row_seg = lax.dynamic_slice_in_dim(seg_row, row_start, block_rows, 0)
    return (row_pos[:, None] >= col_pos[None, :]) & (row_seg[:, None] == seg_row[None, :])


def decay_block(decay_sum, row_start, block_rows, allowed):
    sum_rows = lax.dynamic_slice_in_dim(decay_sum, row_start, block_rows, 0)
    spread_gap = sum_rows.T[:, :, None] - decay_sum.T[:, None, :]
    mask_all = allowed[None, :, :]
    return jnp.where(mask_all, jnp.exp(-jnp.where(mask_all, spread_gap, 0.0)), 0.0)


def block_starts(length, block_rows):
    return jnp.arange(length // block_rows, dtype=jnp.int32) * block_rows


def rotated_heads(q_seq, k_seq, v_seq, cosine, sine_part):
    length = q_seq.shape[0]
    head_shape = (length, q_seq.shape[1] // HEAD_DIM, HEAD_DIM)
    q_rot = rotate(q_seq.astype(jnp.float32).reshape(head_shape), cosine, sine_part, 1.0).astype(
        jnp.bfloat16
    )
    k_rot = rotate(k_seq.astype(jnp.float32).reshape(head_shape), cosine, sine_part, 1.0).astype(
        jnp.bfloat16
    )
    return (q_rot, k_rot, v_seq.reshape(head_shape))


def masked_scores(q_blk, k_rot, row_start, block_rows, seg_row):
    scores = jnp.einsum(
        "qhd,khd->hqk", q_blk, k_rot, preferred_element_type=jnp.float32
    ) * HEAD_DIM ** (-0.5)
    allowed = block_mask(row_start, block_rows, seg_row)
    return jnp.where(allowed[None], scores, masked_score)


def attend_forward(q_seq, k_seq, v_seq, seg_row, cosine, sine_part):
    length = q_seq.shape[0]
    head_count = q_seq.shape[1] // HEAD_DIM
    q_rot, k_rot, v_arr = rotated_heads(q_seq, k_seq, v_seq, cosine, sine_part)
    block_rows = min(512, length)

    def one_block(row_start):
        q_blk = lax.dynamic_slice_in_dim(q_rot, row_start, block_rows, 0)
        scores = masked_scores(q_blk, k_rot, row_start, block_rows, seg_row)
        row_max = jnp.max(scores, axis=-1, keepdims=True)
        exponent = jnp.exp(scores - row_max)
        row_total = jnp.sum(exponent, axis=-1, keepdims=True)
        prob_low = (exponent / row_total).astype(jnp.bfloat16)
        out_blk = jnp.einsum("hqk,khd->qhd", prob_low, v_arr, preferred_element_type=jnp.float32)
        return (out_blk.astype(jnp.bfloat16), (row_max + jnp.log(row_total))[..., 0])

    out_blocks, lse_seq = lax.map(one_block, block_starts(length, block_rows))
    return (out_blocks.reshape(length, head_count * HEAD_DIM), lse_seq)


def attend_backward(q_seq, k_seq, v_seq, seg_row, lse_seq, grad_out, cosine, sine_part):
    length = q_seq.shape[0]
    head_count = q_seq.shape[1] // HEAD_DIM
    q_rot, k_rot, v_arr = rotated_heads(q_seq, k_seq, v_seq, cosine, sine_part)
    grad_arr = grad_out.reshape(length, head_count, HEAD_DIM)
    block_rows = min(512, length)
    score_scale = HEAD_DIM ** (-0.5)

    def one_block(carry, block_inputs):
        grad_key, grad_val = carry
        row_start, lse_blk = block_inputs
        q_blk = lax.dynamic_slice_in_dim(q_rot, row_start, block_rows, 0)
        g_blk = lax.dynamic_slice_in_dim(grad_arr, row_start, block_rows, 0)
        scores = masked_scores(q_blk, k_rot, row_start, block_rows, seg_row)
        prob_vals = jnp.exp(scores - lse_blk[..., None])
        grad_probs = jnp.einsum("qhd,khd->hqk", g_blk, v_arr, preferred_element_type=jnp.float32)
        inner = jnp.sum(grad_probs * prob_vals, axis=-1, keepdims=True)
        grad_scores = (prob_vals * (grad_probs - inner)).astype(jnp.bfloat16)
        grad_q_blk = (
            jnp.einsum("hqk,khd->qhd", grad_scores, k_rot, preferred_element_type=jnp.float32)
            * score_scale
        )
        grad_key = (
            grad_key
            + jnp.einsum("hqk,qhd->khd", grad_scores, q_blk, preferred_element_type=jnp.float32)
            * score_scale
        )
        grad_val = grad_val + jnp.einsum(
            "hqk,qhd->khd",
            prob_vals.astype(jnp.bfloat16),
            g_blk,
            preferred_element_type=jnp.float32,
        )
        return ((grad_key, grad_val), grad_q_blk)

    zero_heads = jnp.zeros((length, head_count, HEAD_DIM), jnp.float32)
    (grad_key, grad_val), grad_query = lax.scan(
        one_block, (zero_heads, zero_heads), (block_starts(length, block_rows), lse_seq)
    )
    grad_query = rotate(grad_query.reshape(length, head_count, HEAD_DIM), cosine, sine_part, -1.0)
    grad_key = rotate(grad_key, cosine, sine_part, -1.0)
    flat_shape = (length, head_count * HEAD_DIM)
    return (
        grad_query.reshape(flat_shape).astype(jnp.bfloat16),
        grad_key.reshape(flat_shape).astype(jnp.bfloat16),
        grad_val.reshape(flat_shape).astype(jnp.bfloat16),
    )


def ssd_forward(x_seq, bc_seq, dt_seq, seg_row, ssm_params):
    x_taps, bc_taps, a_local, bias_local, skip_local = ssm_params
    length = x_seq.shape[0]
    head_count = dt_seq.shape[1]
    mixed_x = causal_conv(x_seq.astype(jnp.float32), x_taps, seg_row)
    mixed_bc = causal_conv(bc_seq.astype(jnp.float32), bc_taps, seg_row)
    dt_step, decay_sum = step_chain(dt_seq.astype(jnp.float32), bias_local, a_local)
    in_b = mixed_bc[:, :STATE].astype(jnp.bfloat16)
    out_c = mixed_bc[:, STATE:].astype(jnp.bfloat16)
    heads_x = mixed_x.reshape(length, head_count, SSM_DIM)
    scaled_x = (heads_x * dt_step[:, :, None]).astype(jnp.bfloat16)
    block_rows = min(512, length)

    def one_block(row_start):
        allowed = block_mask(row_start, block_rows, seg_row)
        c_blk = lax.dynamic_slice_in_dim(out_c, row_start, block_rows, 0)
        intersection = jnp.einsum("qn,kn->qk", c_blk, in_b, preferred_element_type=jnp.float32)
        decay = decay_block(decay_sum, row_start, block_rows, allowed)
        ssm_weights = (intersection[None] * decay).astype(jnp.bfloat16)
        mixed = jnp.einsum(
            "hqk,khd->qhd", ssm_weights, scaled_x, preferred_element_type=jnp.float32
        )
        x_blk = lax.dynamic_slice_in_dim(heads_x, row_start, block_rows, 0)
        return (mixed + skip_local[None, :, None] * x_blk).astype(jnp.bfloat16)

    outputs = lax.map(one_block, block_starts(length, block_rows))
    return outputs.reshape(length, head_count * SSM_DIM)


def ssd_backward(x_seq, bc_seq, dt_seq, seg_row, grad_y, ssm_params):
    x_taps, bc_taps, a_local, bias_local, skip_local = ssm_params
    length = x_seq.shape[0]
    head_count = dt_seq.shape[1]
    block_rows = min(512, length)

    def conv_piece(signal, conv_weights):
        return causal_conv(signal, conv_weights, seg_row)

    mixed_x, pull_x = jax.vjp(conv_piece, x_seq.astype(jnp.float32), x_taps)
    mixed_bc, pull_bc = jax.vjp(conv_piece, bc_seq.astype(jnp.float32), bc_taps)
    (dt_step, decay_sum), pull_step = jax.vjp(
        step_chain, dt_seq.astype(jnp.float32), bias_local, a_local
    )
    in_b = mixed_bc[:, :STATE].astype(jnp.bfloat16)
    out_c = mixed_bc[:, STATE:].astype(jnp.bfloat16)
    heads_x = mixed_x.reshape(length, head_count, SSM_DIM)
    scaled_x = (heads_x * dt_step[:, :, None]).astype(jnp.bfloat16)
    grad_arr = grad_y.reshape(length, head_count, SSM_DIM)

    def one_block(carry, row_start):
        grad_b, grad_scaled, grad_cum = carry
        allowed = block_mask(row_start, block_rows, seg_row)
        c_blk = lax.dynamic_slice_in_dim(out_c, row_start, block_rows, 0)
        g_blk = lax.dynamic_slice_in_dim(grad_arr, row_start, block_rows, 0)
        intersection = jnp.einsum("qn,kn->qk", c_blk, in_b, preferred_element_type=jnp.float32)
        decay = decay_block(decay_sum, row_start, block_rows, allowed)
        ssm_weights = intersection[None] * decay
        grad_w = jnp.einsum("qhd,khd->hqk", g_blk, scaled_x, preferred_element_type=jnp.float32)
        grad_scaled = grad_scaled + jnp.einsum(
            "hqk,qhd->khd",
            ssm_weights.astype(jnp.bfloat16),
            g_blk,
            preferred_element_type=jnp.float32,
        )
        product = grad_w * ssm_weights
        grad_cum = grad_cum + jnp.sum(product, axis=1).T
        row_part = -jnp.sum(product, axis=2).T
        grad_intersection = (grad_w * decay).astype(jnp.bfloat16)
        grad_c_blk = jnp.sum(
            jnp.einsum("hqk,kn->hqn", grad_intersection, in_b, preferred_element_type=jnp.float32),
            axis=0,
        )
        grad_b = grad_b + jnp.sum(
            jnp.einsum("hqk,qn->hkn", grad_intersection, c_blk, preferred_element_type=jnp.float32),
            axis=0,
        )
        return ((grad_b, grad_scaled, grad_cum), (grad_c_blk, row_part))

    carry_init = (
        jnp.zeros((length, STATE), jnp.float32),
        jnp.zeros((length, head_count, SSM_DIM), jnp.float32),
        jnp.zeros((length, head_count), jnp.float32),
    )
    (grad_b, grad_scaled, grad_cum), (grad_c_blocks, row_parts) = lax.scan(
        one_block, carry_init, block_starts(length, block_rows)
    )
    grad_c = grad_c_blocks.reshape(length, STATE)
    grad_cum = grad_cum + row_parts.reshape(length, head_count)
    grad_y_f32 = grad_arr.astype(jnp.float32)
    grad_skip = jnp.sum(grad_y_f32 * heads_x, axis=(0, 2))
    grad_heads_x = skip_local[None, :, None] * grad_y_f32 + grad_scaled * dt_step[:, :, None]
    grad_step = jnp.sum(grad_scaled * heads_x, axis=2)
    grad_dt_raw, grad_bias, grad_alog = pull_step((grad_step, grad_cum))
    grad_x_in, grad_x_taps = pull_x(grad_heads_x.reshape(length, head_count * SSM_DIM))
    grad_bc_in, grad_bc_taps = pull_bc(jnp.concatenate([grad_b, grad_c], axis=1))
    return (
        grad_x_in.astype(jnp.bfloat16),
        grad_dt_raw.astype(jnp.bfloat16),
        grad_bc_in,
        grad_x_taps,
        grad_bc_taps,
        grad_alog,
        grad_bias,
        grad_skip,
    )


def swap_seq(value, bit, count):
    return lax.ppermute(value, "seq", [(place, place ^ bit) for place in range(count)])


def shift_fsdp(value, step, count):
    pairs = [
        (place, place + step) for place in range(count) if 0 <= place + step < count
    ]
    return lax.ppermute(value, "fsdp", pairs)


def seq_bits(count):
    bits = []
    bit = 1
    while bit < count:
        bits.append(bit)
        bit *= 2
    return bits


def block_order(bits):
    order = [0]
    for bit in bits:
        order = order + [place ^ bit for place in order]
    return order


def rows_gather(rows, count):
    half = rows.shape[0] // 2
    bits = seq_bits(count)
    parts = []
    for piece, order in ((rows[:half], bits), (rows[half:], bits[::-1])):
        for bit in order:
            piece = jnp.concatenate([piece, swap_seq(piece, bit, count)], axis=0)
        parts.append(piece)
    return jnp.concatenate(parts, axis=0)


def rows_scatter(partial, count):
    half = partial.shape[0] // 2
    bits = seq_bits(count)
    parts = []
    for piece, order in ((partial[:half], bits), (partial[half:], bits[::-1])):
        piece = piece.astype(jnp.float32)
        for bit in order[::-1]:
            keep = piece.shape[0] // 2
            came = swap_seq(piece[keep:].astype(jnp.bfloat16), bit, count)
            piece = piece[:keep] + came.astype(jnp.float32)
        parts.append(piece)
    return jnp.concatenate(parts, axis=0)


def relative_rows(rank, count):
    bits = seq_bits(count)
    upper = jnp.asarray(block_order(bits), jnp.int32) ^ rank
    lower = jnp.asarray(block_order(bits[::-1]), jnp.int32) ^ rank
    return jnp.concatenate([upper * 2, lower * 2 + 1])


def true_rows(rank, count):
    bits = seq_bits(count)
    upper = block_order(bits)
    lower = block_order(bits[::-1])
    place_upper = [upper.index(block) for block in range(count)]
    place_lower = [count + lower.index(block) for block in range(count)]
    blocks = jnp.arange(count, dtype=jnp.int32) ^ rank
    table_upper = jnp.asarray(place_upper, jnp.int32)[blocks]
    table_lower = jnp.asarray(place_lower, jnp.int32)[blocks]
    return jnp.stack([table_upper, table_lower], axis=1).reshape(-1)


def reorder(value, table):
    pieces = table.shape[0]
    rows = value.shape[0] // pieces
    return jnp.concatenate(
        [
            lax.dynamic_slice_in_dim(value, table[place] * rows, rows, 0)
            for place in range(pieces)
        ],
        axis=0,
    )


def seq_pieces(value, count):
    return [value] + [swap_seq(value, bit, count) for bit in range(1, count)]


def seq_sum(value, count):
    bits = seq_bits(count)
    orders = (block_order(bits), block_order(bits[::-1]))
    total = value.reshape(2 * count, -1)
    for bit in range(1, count):
        came = swap_seq(value, bit, count).reshape(2 * count, -1)
        places = [
            half * count + order.index(block ^ bit)
            for half, order in enumerate(orders)
            for block in order
        ]
        total = total + jnp.concatenate([came[place : place + 1] for place in places])
    return total.reshape(-1)


def seq_stack(value, rank, count):
    result = jnp.zeros((count,) + value.shape, value.dtype)
    for bit, piece in enumerate(seq_pieces(value, count)):
        result = lax.dynamic_update_index_in_dim(result, piece, rank ^ bit, 0)
    return result


def seq_reduce_blocks(blocks, rank, count):
    total = lax.dynamic_index_in_dim(blocks, rank, 0, False).astype(jnp.float32)
    for bit in range(1, count):
        block = lax.dynamic_index_in_dim(blocks, rank ^ bit, 0, False)
        total = total + swap_seq(block, bit, count).astype(jnp.float32)
    return total


def small_gather(vector, seq_count, fsdp_count):
    rank = lax.axis_index("seq")
    place = lax.axis_index("fsdp")
    chips = fsdp_count // 2
    by_seq = seq_stack(vector, rank, seq_count)
    other = lax.ppermute(by_seq, "fsdp", [(spot, spot ^ 1) for spot in range(fsdp_count)])
    core = place % 2
    pair = jnp.where(core == 0, jnp.stack([by_seq, other]), jnp.stack([other, by_seq]))
    line = [shift_fsdp(pair, 2 * step, fsdp_count) for step in range(chips - 1, 0, -1)]
    line.append(pair)
    line += [shift_fsdp(pair, -2 * step, fsdp_count) for step in range(1, chips)]
    chip_rows = lax.dynamic_slice_in_dim(jnp.stack(line), chips - 1 - place // 2, chips, 0)
    return chip_rows.reshape(fsdp_count, seq_count, -1).transpose(1, 0, 2)


def small_scatter(vectors, seq_count, fsdp_count):
    rank = lax.axis_index("seq")
    place = lax.axis_index("fsdp")
    chips = fsdp_count // 2
    rows = seq_reduce_blocks(vectors, rank, seq_count).reshape(chips, 2, -1)
    core = place % 2
    away = lax.dynamic_index_in_dim(rows, 1 - core, 1, False)
    kept = lax.dynamic_index_in_dim(rows, core, 1, False)
    kept = kept + lax.ppermute(away, "fsdp", [(spot, spot ^ 1) for spot in range(fsdp_count)])
    chip = place // 2
    total = lax.dynamic_index_in_dim(kept, chip, 0, False)
    for step in range(1, chips):
        ahead = lax.dynamic_index_in_dim(kept, jnp.minimum(chip + step, chips - 1), 0, False)
        behind = lax.dynamic_index_in_dim(kept, jnp.maximum(chip - step, 0), 0, False)
        total = total + shift_fsdp(ahead, 2 * step, fsdp_count)
        total = total + shift_fsdp(behind, -2 * step, fsdp_count)
    return total


def norm_forward(rows, gain):
    scale = lax.rsqrt(jnp.mean(rows * rows, axis=-1, keepdims=True) + epsilon)
    return ((rows * scale * gain).astype(jnp.bfloat16), scale)


def norm_backward(rows, scale, gain, cotangent):
    weighted = cotangent * gain
    inner = jnp.mean(rows * weighted, axis=-1, keepdims=True)
    grad_rows = scale * weighted - rows * (scale * scale * scale * inner)
    return (grad_rows, jnp.sum(cotangent * rows * scale, axis=0))


def columns_to_owners(blocks):
    arrived = lax.all_to_all(blocks, "seq", split_axis=0, concat_axis=0, tiled=True)
    return arrived.transpose(1, 0, 2).astype(jnp.float32)


def body(
    seq_count,
    fsdp_count,
    hidden_in,
    segments,
    out_grad,
    norm1_gain,
    w_query,
    w_keyval,
    w_attn_out,
    w_gate_z,
    w_ssm_x,
    w_ssm_bc,
    w_ssm_dt,
    conv_taps,
    a_log,
    dt_bias,
    skip_gain,
    ssm_gain,
    w_ssm_out,
    norm2_gain,
    w_ff_gate,
    w_ff_up,
    w_ff_down,
):
    f32, bf16 = jnp.float32, jnp.bfloat16
    batch, block_len, model_width = hidden_in.shape
    length = block_len * seq_count
    rank = lax.axis_index("seq")
    seg_row = segments[0]
    heads_local = HEADS // seq_count
    group_size = HEADS // KV_HEADS
    q_width = w_query.shape[1] // seq_count
    z_width = w_gate_z.shape[1] // seq_count
    x_width = w_ssm_x.shape[1] // seq_count
    bc_width = w_ssm_bc.shape[1] // seq_count
    dt_width = w_ssm_dt.shape[1] // seq_count
    ff_width = w_ff_gate.shape[1] // seq_count
    kv_total = w_keyval.shape[1] // 2
    heads_total = a_log.shape[0]
    dssm = w_ssm_x.shape[1]
    row_piece = w_query.shape[0]
    used = q_width + 2 * HEAD_DIM + x_width + bc_width + dt_width
    pad_width = -used % 128

    sends = []
    for target in range(seq_count):
        kv_head = target * heads_local // group_size
        sends.append(
            jnp.concatenate(
                [
                    w_query[:, target * q_width : (target + 1) * q_width],
                    w_keyval[:, kv_head * HEAD_DIM : (kv_head + 1) * HEAD_DIM],
                    w_keyval[:, kv_total + kv_head * HEAD_DIM : kv_total + (kv_head + 1) * HEAD_DIM],
                    w_ssm_x[:, target * x_width : (target + 1) * x_width],
                    w_ssm_bc[:, target * bc_width : (target + 1) * bc_width],
                    w_ssm_dt[:, target * dt_width : (target + 1) * dt_width],
                    jnp.zeros((row_piece, pad_width), bf16),
                    w_gate_z[:, target * z_width : (target + 1) * z_width],
                ],
                axis=1,
            )
        )
    mixer_piece = lax.all_to_all(jnp.stack(sends), "seq", split_axis=0, concat_axis=0, tiled=True)
    mixer_w = lax.all_gather(mixer_piece, "fsdp", axis=1, tiled=True).reshape(model_width, -1)
    out_piece = jnp.concatenate([w_attn_out, w_ssm_out], axis=0)
    out_w = lax.all_gather(out_piece, "fsdp", axis=0)
    attn_out_w = out_w[:, : w_attn_out.shape[0]].reshape(-1, model_width)
    ssm_out_w = out_w[:, w_attn_out.shape[0] :].reshape(-1, model_width)
    ff_sends = jnp.stack(
        [
            jnp.concatenate(
                [
                    w_ff_gate[:, target * ff_width : (target + 1) * ff_width],
                    w_ff_up[:, target * ff_width : (target + 1) * ff_width],
                ],
                axis=1,
            )
            for target in range(seq_count)
        ]
    )
    ff_piece = lax.all_to_all(ff_sends, "seq", split_axis=0, concat_axis=0, tiled=True)
    ff_w = lax.all_gather(ff_piece, "fsdp", axis=1, tiled=True).reshape(model_width, -1)
    down_w = lax.all_gather(w_ff_down, "fsdp", axis=0, tiled=True)

    taps_rows, taps_width = conv_taps.shape
    gains = jnp.concatenate([norm1_gain, norm2_gain, ssm_gain, conv_taps.reshape(-1)])
    gain_count = norm1_gain.shape[0]
    ssm_count = ssm_gain.shape[0]
    gathered = small_gather(gains, seq_count, fsdp_count).astype(f32)
    gain1 = gathered[:, :, :gain_count].reshape(-1)
    gain2 = gathered[:, :, gain_count : 2 * gain_count].reshape(-1)
    gain_ssm = gathered[:, :, 2 * gain_count : 2 * gain_count + ssm_count].reshape(seq_count, -1)
    gain_ssm = lax.dynamic_index_in_dim(gain_ssm, rank, 0, False)
    taps_full = gathered[:, :, 2 * gain_count + ssm_count :].reshape(-1, taps_width)
    x_taps = lax.dynamic_slice_in_dim(taps_full, rank * x_width, x_width, 0)
    bc_taps = taps_full[dssm:]
    a_local = lax.dynamic_slice_in_dim(a_log, rank * dt_width, dt_width, 0)
    bias_local = lax.dynamic_slice_in_dim(dt_bias, rank * dt_width, dt_width, 0)
    skip_local = lax.dynamic_slice_in_dim(skip_gain, rank * dt_width, dt_width, 0)
    ssm_params = (x_taps, bc_taps, a_local, bias_local, skip_local)

    to_relative = relative_rows(rank, seq_count)
    to_true = true_rows(rank, seq_count)

    own_in = hidden_in.reshape(block_len, model_width)
    all_in = rows_gather(own_in, seq_count)
    normed, _ = norm_forward(all_in.astype(f32), gain1)
    narrow_width = used + pad_width
    narrow = mat_product(normed, mixer_w[:, :narrow_width]).astype(bf16)
    gate_z = mat_product(normed, mixer_w[:, narrow_width:])
    narrow_true = reorder(narrow, to_true)
    edges = [0]
    for width in (q_width, HEAD_DIM, HEAD_DIM, x_width, bc_width, dt_width):
        edges.append(edges[-1] + width)
    q_seq, k_one, v_one, x_seq, bc_own, dt_seq = (
        narrow_true[:, edges[part] : edges[part + 1]] for part in range(6)
    )
    bc_seq = seq_stack(bc_own, rank, seq_count).transpose(1, 0, 2).reshape(length, -1)
    k_seq = jnp.tile(k_one, (1, heads_local))
    v_seq = jnp.tile(v_one, (1, heads_local))
    cosine, sine_part = rope_tables(length, HEAD_DIM)
    attn_true, lse_seq = attend_forward(q_seq, k_seq, v_seq, seg_row, cosine, sine_part)
    ssm_true = ssd_forward(x_seq, bc_seq, dt_seq, seg_row, ssm_params)
    heads_rel = reorder(jnp.concatenate([attn_true, ssm_true], axis=1), to_relative)
    attn_rel = heads_rel[:, :q_width]
    ssm_rel = heads_rel[:, q_width:].astype(f32)
    gate_sig = jax.nn.sigmoid(gate_z)
    gate_silu = gate_z * gate_sig
    gated = ssm_rel * gate_silu
    square_sum = seq_sum(jnp.sum(gated * gated, axis=1), seq_count)
    gated_scale = lax.rsqrt(square_sum / dssm + epsilon)[:, None]
    ssm_in = (gated * gated_scale * gain_ssm).astype(bf16)
    out_partial = mat_product(attn_rel, attn_out_w) + mat_product(ssm_in, ssm_out_w)
    xin = own_in.astype(f32)
    middle = xin + rows_scatter(out_partial, seq_count)

    own_normed2, scale2 = norm_forward(middle, gain2)
    normed2 = rows_gather(own_normed2, seq_count)
    grad_own = out_grad.reshape(block_len, model_width)
    grad_ff = rows_gather(grad_own, seq_count)
    gate_ff = mat_product(normed2, ff_w[:, :ff_width])
    up_ff = mat_product(normed2, ff_w[:, ff_width:])
    ff_sig = jax.nn.sigmoid(gate_ff)
    ff_silu = gate_ff * ff_sig
    act = (ff_silu * up_ff).astype(bf16)
    layer_out = middle + rows_scatter(mat_product(act, down_w), seq_count)
    grad_w_down = weight_grad(act, grad_ff).astype(bf16)
    grad_act = input_grad(grad_ff, down_w)
    grad_gate_ff = grad_act * up_ff * (ff_sig + ff_silu * (1.0 - ff_sig))
    grad_up_ff = grad_act * ff_silu
    grad_pair = jnp.concatenate([grad_gate_ff.astype(bf16), grad_up_ff.astype(bf16)], axis=1)
    grad_w_ff = weight_grad(normed2, grad_pair).astype(bf16)
    grad_normed2 = rows_scatter(input_grad(grad_pair, ff_w), seq_count)
    grad_middle_norm, grad_gain2 = norm_backward(middle, scale2, gain2, grad_normed2)
    grad_middle = grad_own.astype(f32) + grad_middle_norm
    grad_w_down = lax.psum_scatter(grad_w_down, "fsdp", scatter_dimension=0, tiled=True)
    grad_w_ff = lax.psum_scatter(
        grad_w_ff.reshape(seq_count, -1, 2 * ff_width), "fsdp", scatter_dimension=1, tiled=True
    )

    grad_mix = rows_gather(grad_middle.astype(bf16), seq_count)
    grad_w_attn = weight_grad(attn_rel, grad_mix).astype(bf16)
    grad_w_ssm = weight_grad(ssm_in, grad_mix).astype(bf16)
    grad_attn = input_grad(grad_mix, attn_out_w).astype(bf16)
    grad_ssm_in = input_grad(grad_mix, ssm_out_w)
    weighted = grad_ssm_in * gain_ssm
    inner = seq_sum(jnp.sum(gated * weighted, axis=1), seq_count)[:, None] / dssm
    grad_gated = gated_scale * weighted - gated * (
        gated_scale * gated_scale * gated_scale * inner
    )
    grad_gain_ssm = jnp.sum(grad_ssm_in * gated * gated_scale, axis=0)
    grad_ssm = (grad_gated * gate_silu).astype(bf16)
    grad_z = (grad_gated * ssm_rel * (gate_sig + gate_silu * (1.0 - gate_sig))).astype(bf16)
    grads_true = reorder(jnp.concatenate([grad_attn, grad_ssm], axis=1), to_true)
    grad_q, grad_k, grad_v = attend_backward(
        q_seq, k_seq, v_seq, seg_row, lse_seq, grads_true[:, :q_width], cosine, sine_part
    )
    (
        grad_x,
        grad_dt,
        grad_bc_part,
        grad_x_taps,
        grad_bc_taps,
        grad_alog,
        grad_bias,
        grad_skip,
    ) = ssd_backward(x_seq, bc_seq, dt_seq, seg_row, grads_true[:, q_width:], ssm_params)
    grad_k = jnp.sum(grad_k.reshape(length, heads_local, HEAD_DIM).astype(f32), axis=1)
    grad_v = jnp.sum(grad_v.reshape(length, heads_local, HEAD_DIM).astype(f32), axis=1)
    bc_blocks = grad_bc_part.astype(bf16).reshape(length, seq_count, bc_width).transpose(1, 0, 2)
    grad_bc = seq_reduce_blocks(bc_blocks, rank, seq_count).astype(bf16)
    grad_narrow = reorder(
        jnp.concatenate(
            [
                grad_q,
                grad_k.astype(bf16),
                grad_v.astype(bf16),
                grad_x,
                grad_bc,
                grad_dt,
                jnp.zeros((length, pad_width), bf16),
            ],
            axis=1,
        ),
        to_relative,
    )
    grad_w_z = weight_grad(normed, grad_z).astype(bf16)
    grad_w_narrow = weight_grad(normed, grad_narrow).astype(bf16)
    grad_normed = input_grad(grad_narrow, mixer_w[:, :narrow_width]) + input_grad(
        grad_z, mixer_w[:, narrow_width:]
    )
    grad_normed = rows_scatter(grad_normed, seq_count)
    _, scale1 = norm_forward(xin, gain1)
    grad_in_norm, grad_gain1 = norm_backward(xin, scale1, gain1, grad_normed)
    grad_in = grad_middle + grad_in_norm
    out_grads = jnp.concatenate(
        [
            grad_w_attn.reshape(fsdp_count, -1, model_width),
            grad_w_ssm.reshape(fsdp_count, -1, model_width),
        ],
        axis=1,
    )
    out_grads = lax.psum_scatter(out_grads, "fsdp", scatter_dimension=0, tiled=True)[0]
    grad_w_z = lax.psum_scatter(
        grad_w_z.reshape(seq_count, -1, z_width), "fsdp", scatter_dimension=1, tiled=True
    )
    grad_w_narrow = lax.psum_scatter(
        grad_w_narrow.reshape(seq_count, -1, narrow_width),
        "fsdp",
        scatter_dimension=1,
        tiled=True,
    )

    per_device = (seq_count, fsdp_count, -1)
    x_conv = lax.dynamic_update_slice_in_dim(
        jnp.zeros((dssm, taps_width), f32), grad_x_taps, rank * x_width, 0
    )
    conv_grads = jnp.concatenate([x_conv, grad_bc_taps], axis=0).reshape(per_device)
    ssm_grads = lax.dynamic_update_index_in_dim(
        jnp.zeros((seq_count, z_width), f32), grad_gain_ssm, rank, 0
    ).reshape(per_device)
    head_grads = lax.dynamic_update_slice(
        jnp.zeros((3, heads_total), f32),
        jnp.stack([grad_alog, grad_bias, grad_skip]),
        (jnp.int32(0), rank * dt_width),
    )
    head_grads = jnp.broadcast_to(
        head_grads.reshape(1, 1, -1), (seq_count, fsdp_count, 3 * heads_total)
    )
    small = small_scatter(
        jnp.concatenate(
            [
                grad_gain1.reshape(per_device),
                grad_gain2.reshape(per_device),
                ssm_grads,
                conv_grads,
                head_grads,
            ],
            axis=2,
        ),
        seq_count,
        fsdp_count,
    )
    small_edges = [0]
    for width in (gain_count, gain_count, ssm_count, taps_rows * taps_width, 3 * heads_total):
        small_edges.append(small_edges[-1] + width)
    out_gain1, out_gain2, out_ssm_gain, out_conv, out_heads = (
        small[small_edges[part] : small_edges[part + 1]] for part in range(5)
    )
    out_heads = out_heads.reshape(3, heads_total)

    ff_cols = columns_to_owners(grad_w_ff)
    z_cols = columns_to_owners(grad_w_z)
    narrow_cols = columns_to_owners(grad_w_narrow)
    q_cols, k_cols, v_cols, x_cols, bc_cols, dt_cols = (
        narrow_cols[:, :, edges[part] : edges[part + 1]] for part in range(6)
    )
    ranks_per_kv = group_size // heads_local
    kv_shape = (row_piece, KV_HEADS, ranks_per_kv, HEAD_DIM)
    k_cols = jnp.sum(k_cols.reshape(kv_shape), axis=2).reshape(row_piece, -1)
    v_cols = jnp.sum(v_cols.reshape(kv_shape), axis=2).reshape(row_piece, -1)
    attn_rows = w_attn_out.shape[0]
    return (
        layer_out.astype(bf16).reshape(batch, block_len, model_width),
        grad_in.astype(bf16).reshape(batch, block_len, model_width),
        out_gain1,
        q_cols.reshape(row_piece, -1),
        jnp.concatenate([k_cols, v_cols], axis=1),
        out_grads[:attn_rows].astype(f32),
        z_cols.reshape(row_piece, -1),
        x_cols.reshape(row_piece, -1),
        bc_cols.reshape(row_piece, -1),
        dt_cols.reshape(row_piece, -1),
        out_conv.reshape(taps_rows, taps_width),
        out_heads[0],
        out_heads[1],
        out_heads[2],
        out_ssm_gain,
        out_grads[attn_rows:].astype(f32),
        out_gain2,
        ff_cols[:, :, :ff_width].reshape(row_piece, -1),
        ff_cols[:, :, ff_width:].reshape(row_piece, -1),
        grad_w_down.astype(f32),
    )


def solution(mesh):
    in_specs = (
        P("fsdp", "seq", None),
        P("fsdp", None),
        P("fsdp", "seq", None),
        P(("seq", "fsdp")),
        P(("seq", "fsdp"), None),
        P(("seq", "fsdp"), None),
        P(("seq", "fsdp"), None),
        P(("seq", "fsdp"), None),
        P(("seq", "fsdp"), None),
        P(("seq", "fsdp"), None),
        P(("seq", "fsdp"), None),
        P(("seq", "fsdp"), None),
        P(),
        P(),
        P(),
        P(("seq", "fsdp")),
        P(("seq", "fsdp"), None),
        P(("seq", "fsdp")),
        P(("seq", "fsdp"), None),
        P(("seq", "fsdp"), None),
        P(("seq", "fsdp"), None),
    )
    out_specs = (
        P("fsdp", "seq", None),
        P("fsdp", "seq", None),
        P(("seq", "fsdp")),
        P(("seq", "fsdp"), None),
        P(("seq", "fsdp"), None),
        P(("seq", "fsdp"), None),
        P(("seq", "fsdp"), None),
        P(("seq", "fsdp"), None),
        P(("seq", "fsdp"), None),
        P(("seq", "fsdp"), None),
        P(("seq", "fsdp"), None),
        P(),
        P(),
        P(),
        P(("seq", "fsdp")),
        P(("seq", "fsdp"), None),
        P(("seq", "fsdp")),
        P(("seq", "fsdp"), None),
        P(("seq", "fsdp"), None),
        P(("seq", "fsdp"), None),
    )
    step = functools.partial(body, mesh.shape["seq"], mesh.shape["fsdp"])
    return jax.shard_map(step, mesh=mesh, in_specs=in_specs, out_specs=out_specs, check_vma=False)
```

```python
import functools

import jax
import jax.numpy as jnp
from jax import lax
from jax.experimental import pallas as pl
from jax.experimental.layout import Layout, with_layout_constraint
from jax.experimental.pallas import tpu as pltpu
from jax.sharding import PartitionSpec as P

HEADS = 8
KV_HEADS = 2
HEAD_DIM = 128
SSM_DIM = 64
STATE = 256
BLOCK = 256
LANES = 128
KERNEL_VMEM = 56 * 1024 * 1024


epsilon = 1e-05
rope_base = 10000.0
masked_score = -1e30


def mat_product(left_op, right_op):
    return jnp.dot(left_op, right_op, preferred_element_type=jnp.float32)


def weight_grad(left_op, right_op):
    return lax.dot_general(
        left_op, right_op, (((0,), (0,)), ((), ())), preferred_element_type=jnp.float32
    )


def input_grad(grad_rows, weights):
    return lax.dot_general(
        grad_rows, weights, (((1,), (1,)), ((), ())), preferred_element_type=jnp.float32
    )


def dot_plain(left_op, right_op):
    return jnp.dot(left_op, right_op, preferred_element_type=jnp.float32)


def dot_exact(left_op, right_op):
    return jnp.dot(
        left_op, right_op, precision=lax.Precision.HIGHEST, preferred_element_type=jnp.float32
    )


def dot_rows(left_op, right_op):
    return lax.dot_general(
        left_op, right_op, (((1,), (1,)), ((), ())), preferred_element_type=jnp.float32
    )


def dot_columns(left_op, right_op):
    return lax.dot_general(
        left_op, right_op, (((0,), (0,)), ((), ())), preferred_element_type=jnp.float32
    )


def iota_of(shape, axis):
    return lax.broadcasted_iota(jnp.int32, shape, axis)


def allowed_block(marks_ref, seg_row_ref, row_start, col_start, columns, diagonal):
    seg_col = marks_ref[pl.ds(row_start, BLOCK), 0:1]
    seg_row = seg_row_ref[0:1, pl.ds(col_start, columns)]
    same = seg_col == seg_row
    if diagonal:
        row_pos = row_start + iota_of((BLOCK, columns), 0)
        col_pos = col_start + iota_of((BLOCK, columns), 1)
        same = same & (row_pos >= col_pos)
    return same


def store_relative(order_ref, target, piece, row_start, column, values):
    rows, width = values.shape
    for part in range(rows // piece):
        place = row_start // piece + part
        start = pl.multiple_of(order_ref[place] * piece, piece)
        target[pl.ds(start, piece), column : column + width] = values[
            part * piece : (part + 1) * piece
        ]


def attention_load(pieces, order_ref, narrow_ref, cos_ref, sin_ref, q_s, k_s, v_s, q_width):
    length = narrow_ref.shape[0]
    piece = length // pieces
    for place in range(pieces):
        start = pl.multiple_of(order_ref[place] * piece, piece)
        rows = slice(place * piece, (place + 1) * piece)
        cosine = cos_ref[rows, :]
        sine = sin_ref[rows, :]
        for column in range(0, q_width + HEAD_DIM, HEAD_DIM):
            part = narrow_ref[pl.ds(start, piece), column : column + HEAD_DIM].astype(jnp.float32)
            turned = part * cosine + pltpu.roll(part, HEAD_DIM // 2, 1) * sine
            if column < q_width:
                q_s[rows, column : column + HEAD_DIM] = turned.astype(jnp.bfloat16)
            else:
                k_s[rows, :] = turned.astype(jnp.bfloat16)
        v_s[rows, :] = narrow_ref[
            pl.ds(start, piece), q_width + HEAD_DIM : q_width + 2 * HEAD_DIM
        ]


def attention_forward_kernel(
    q_width,
    pieces,
    order_ref,
    narrow_ref,
    cos_ref,
    sin_ref,
    marks_ref,
    seg_row_ref,
    out_ref,
    lse_ref,
    q_s,
    k_s,
    v_s,
):
    length = narrow_ref.shape[0]
    piece = length // pieces
    attention_load(pieces, order_ref, narrow_ref, cos_ref, sin_ref, q_s, k_s, v_s, q_width)
    for block in range(length // BLOCK):
        start = block * BLOCK
        columns = start + BLOCK
        allowed = allowed_block(marks_ref, seg_row_ref, start, 0, columns, True)
        for head in range(q_width // HEAD_DIM):
            lanes = slice(head * HEAD_DIM, (head + 1) * HEAD_DIM)
            scores = dot_rows(q_s[start : start + BLOCK, lanes], k_s[0:columns, :])
            scores = jnp.where(allowed, scores * HEAD_DIM ** (-0.5), masked_score)
            row_max = jnp.max(scores, axis=1, keepdims=True)
            exponent = jnp.exp(scores - row_max)
            total = jnp.sum(exponent, axis=1, keepdims=True)
            probs = (exponent * (1.0 / total)).astype(jnp.bfloat16)
            mixed = dot_plain(probs, v_s[0:columns, :]).astype(jnp.bfloat16)
            store_relative(order_ref, out_ref, piece, start, head * HEAD_DIM, mixed)
            lse_ref[start : start + BLOCK, head : head + 1] = row_max + jnp.log(total)


def attention_backward_kernel(
    q_width,
    pieces,
    order_ref,
    narrow_ref,
    grad_ref,
    cos_ref,
    sin_ref,
    marks_ref,
    seg_row_ref,
    lse_ref,
    out_ref,
    q_s,
    k_s,
    v_s,
    g_s,
    dk_s,
    dv_s,
):
    length = narrow_ref.shape[0]
    piece = length // pieces
    scale = HEAD_DIM ** (-0.5)
    attention_load(pieces, order_ref, narrow_ref, cos_ref, sin_ref, q_s, k_s, v_s, q_width)
    for place in range(pieces):
        rows = slice(place * piece, (place + 1) * piece)
        start = pl.multiple_of(order_ref[place] * piece, piece)
        g_s[rows, :] = grad_ref[pl.ds(start, piece), 0:q_width]
    dk_s[...] = jnp.zeros_like(dk_s)
    dv_s[...] = jnp.zeros_like(dv_s)
    for block in range(length // BLOCK):
        start = block * BLOCK
        columns = start + BLOCK
        rows = slice(start, columns)
        cosine = cos_ref[rows, :]
        sine = sin_ref[rows, :]
        allowed = allowed_block(marks_ref, seg_row_ref, start, 0, columns, True)
        for head in range(q_width // HEAD_DIM):
            lanes = slice(head * HEAD_DIM, (head + 1) * HEAD_DIM)
            q_blk = q_s[rows, lanes]
            g_blk = g_s[rows, lanes]
            scores = dot_rows(q_blk, k_s[0:columns, :])
            scores = jnp.where(allowed, scores * scale, masked_score)
            probs = jnp.exp(scores - lse_ref[rows, head : head + 1])
            grad_probs = dot_rows(g_blk, v_s[0:columns, :])
            inner = jnp.sum(grad_probs * probs, axis=1, keepdims=True)
            grad_scores = (probs * (grad_probs - inner)).astype(jnp.bfloat16)
            grad_q = dot_plain(grad_scores, k_s[0:columns, :]) * scale
            grad_q = grad_q * cosine - pltpu.roll(grad_q, HEAD_DIM // 2, 1) * sine
            store_relative(
                order_ref, out_ref, piece, start, head * HEAD_DIM, grad_q.astype(jnp.bfloat16)
            )
            dk_s[0:columns, :] += dot_columns(grad_scores, q_blk)
            dv_s[0:columns, :] += dot_columns(probs.astype(jnp.bfloat16), g_blk)
    for block in range(length // BLOCK):
        start = block * BLOCK
        rows = slice(start, start + BLOCK)
        grad_k = dk_s[rows, :] * scale
        grad_k = grad_k * cos_ref[rows, :] - pltpu.roll(grad_k, HEAD_DIM // 2, 1) * sin_ref[rows, :]
        store_relative(order_ref, out_ref, piece, start, q_width, grad_k.astype(jnp.bfloat16))
        store_relative(
            order_ref,
            out_ref,
            piece,
            start,
            q_width + HEAD_DIM,
            dv_s[rows, :].astype(jnp.bfloat16),
        )


def head_spread(width):
    heads = iota_of((LANES, width), 0)
    return (iota_of((LANES, width), 1) // SSM_DIM == heads).astype(jnp.float32)


def head_gather(width):
    heads = iota_of((width, LANES), 1)
    return (iota_of((width, LANES), 0) // SSM_DIM == heads).astype(jnp.float32)


def triangle(lower):
    rows = iota_of((BLOCK, BLOCK), 0)
    columns = iota_of((BLOCK, BLOCK), 1)
    return (rows >= columns if lower else rows <= columns).astype(jnp.float32)


def softplus(values):
    return jnp.maximum(values, 0.0) + jnp.log1p(jnp.exp(-jnp.abs(values)))


def conv_window(pad_ref, taps_ref, marks_ref, row_start, column):
    window = pad_ref[pl.ds(row_start, BLOCK + 8), column : column + LANES]
    total = jnp.broadcast_to(taps_ref[4:5, column : column + LANES], (BLOCK, LANES))
    shifted = []
    for tap in range(4):
        rows = window[5 + tap : 5 + tap + BLOCK]
        if tap < 3:
            rows = rows * marks_ref[pl.ds(row_start, BLOCK), 1 + tap : 2 + tap]
        shifted.append(rows)
        total = total + rows * taps_ref[tap : tap + 1, column : column + LANES]
    return total, shifted


def mixer_load(
    x_column,
    order_ref,
    narrow_ref,
    bc_ref,
    marks_ref,
    x_taps_ref,
    bc_taps_ref,
    heads_ref,
    x_pad,
    bc_pad,
    dt_s,
    a_s,
    a_row_s,
    a_wide,
    mixed_s,
    scaled_s,
    bc_s,
):
    length, width = mixed_s.shape
    count, _, bc_width = bc_ref.shape
    pieces = 2 * count
    piece = length // pieces
    dt_column = narrow_ref.shape[1] - LANES
    x_pad[0:8, :] = jnp.zeros((8, width), jnp.float32)
    bc_pad[0:8, :] = jnp.zeros((8, bc_pad.shape[1]), jnp.float32)
    for place in range(pieces):
        start = pl.multiple_of(order_ref[place] * piece, piece)
        rows = slice(place * piece, (place + 1) * piece)
        padded = slice(8 + place * piece, 8 + (place + 1) * piece)
        x_pad[padded, :] = narrow_ref[pl.ds(start, piece), x_column : x_column + width].astype(
            jnp.float32
        )
        for owner in range(count):
            source = order_ref[pieces + owner]
            owner_start = pl.multiple_of(
                order_ref[pieces + count + owner * pieces + place] * piece, piece
            )
            bc_pad[padded, owner * bc_width : (owner + 1) * bc_width] = bc_ref[
                source, pl.ds(owner_start, piece), :
            ].astype(jnp.float32)
        dt_s[rows, :] = narrow_ref[pl.ds(start, piece), dt_column : dt_column + LANES].astype(
            jnp.float32
        )
    spread = head_spread(width)
    lower = triangle(True)
    rate = jnp.exp(heads_ref[0:1, :])
    bias = heads_ref[1:2, :]

    def one_block(block, carry):
        start = pl.multiple_of(block * BLOCK, BLOCK)
        rows = pl.ds(start, BLOCK)
        step = softplus(dt_s[rows, :] + bias)
        decay_sum = dot_exact(lower, step * rate) + carry
        a_s[rows, :] = decay_sum
        a_row_s[block] = decay_sum.T
        a_wide[rows, :] = dot_exact(decay_sum, spread)
        step_wide = dot_exact(step, spread)
        for column in range(0, width, LANES):
            lanes = slice(column, column + LANES)
            total, _ = conv_window(x_pad, x_taps_ref, marks_ref, start, column)
            mixed = total * jax.nn.sigmoid(total)
            mixed_s[rows, lanes] = mixed
            scaled_s[rows, lanes] = (mixed * step_wide[:, lanes]).astype(jnp.bfloat16)
        for column in range(0, bc_pad.shape[1], LANES):
            total, _ = conv_window(bc_pad, bc_taps_ref, marks_ref, start, column)
            bc_s[rows, column : column + LANES] = (total * jax.nn.sigmoid(total)).astype(
                jnp.bfloat16
            )
        return decay_sum[BLOCK - 1 : BLOCK, :]

    lax.fori_loop(0, length // BLOCK, one_block, jnp.zeros((1, LANES), jnp.float32))


def half_lanes(values, half):
    lane = iota_of(values.shape, 1)
    keep = lane < SSM_DIM if half == 0 else lane >= SSM_DIM
    return jnp.where(keep, values, jnp.zeros_like(values))


def diagonal_decay(a_s, a_row_s, block, start, head):
    gap = a_row_s[block, head : head + 1, :] - a_s[pl.ds(start, BLOCK), head : head + 1]
    return jnp.exp(jnp.minimum(gap, 0.0))


def mixer_forward_kernel(
    x_column,
    order_ref,
    narrow_ref,
    bc_ref,
    marks_ref,
    seg_row_ref,
    x_taps_ref,
    bc_taps_ref,
    heads_ref,
    out_ref,
    x_pad,
    bc_pad,
    dt_s,
    a_s,
    a_row_s,
    a_wide,
    mixed_s,
    scaled_s,
    bc_s,
    weight_s,
    inter_s,
    total_s,
):
    length, width = mixed_s.shape
    piece = length // (2 * bc_ref.shape[0])
    mixer_load(
        x_column,
        order_ref,
        narrow_ref,
        bc_ref,
        marks_ref,
        x_taps_ref,
        bc_taps_ref,
        heads_ref,
        x_pad,
        bc_pad,
        dt_s,
        a_s,
        a_row_s,
        a_wide,
        mixed_s,
        scaled_s,
        bc_s,
    )
    skip_wide = dot_exact(jnp.broadcast_to(heads_ref[2:3, :], (8, LANES)), head_spread(width))

    def one_block(block, _):
        start = pl.multiple_of(block * BLOCK, BLOCK)
        rows = pl.ds(start, BLOCK)
        out_c = bc_s[rows, STATE : 2 * STATE]
        total_s[...] = jnp.zeros_like(total_s)
        first = a_wide[pl.ds(start, 8), :][0:1]

        def earlier(other, _):
            col_start = pl.multiple_of(other * BLOCK, BLOCK)
            columns = pl.ds(col_start, BLOCK)
            allowed = allowed_block(marks_ref, seg_row_ref, start, col_start, BLOCK, False)
            inter = dot_rows(out_c, bc_s[columns, 0:STATE])
            inter = jnp.where(allowed, inter, 0.0).astype(jnp.bfloat16)
            faded = scaled_s[columns, :].astype(jnp.float32) * jnp.exp(a_wide[columns, :] - first)
            total_s[...] += dot_plain(inter, faded.astype(jnp.bfloat16))
            return 0

        lax.fori_loop(0, block, earlier, 0)
        allowed = allowed_block(marks_ref, seg_row_ref, start, start, BLOCK, True)
        inter_s[...] = jnp.where(allowed, dot_rows(out_c, bc_s[rows, 0:STATE]), 0.0)
        for column in range(0, width, LANES):
            lanes = slice(column, column + LANES)
            scaled = scaled_s[rows, lanes]
            mixed = total_s[:, lanes] * jnp.exp(first[:, lanes] - a_wide[rows, lanes])
            for half in range(2):
                head = column // SSM_DIM + half
                decay = diagonal_decay(a_s, a_row_s, block, start, head)
                weights = (inter_s[...] * decay).astype(jnp.bfloat16)
                mixed = mixed + dot_plain(weights, half_lanes(scaled, half))
            mixed = mixed + skip_wide[0:1, lanes] * mixed_s[rows, lanes]
            weight_s[:, lanes] = mixed.astype(jnp.bfloat16)
        for part in range(BLOCK // piece):
            place = block * (BLOCK // piece) + part
            target = pl.multiple_of(order_ref[place] * piece, piece)
            out_ref[pl.ds(target, piece), :] = weight_s[part * piece : (part + 1) * piece, :]
        return 0

    lax.fori_loop(0, length // BLOCK, one_block, 0)


def mixer_backward_kernel(
    x_column,
    order_ref,
    narrow_ref,
    bc_ref,
    grad_ref,
    marks_ref,
    seg_row_ref,
    x_taps_ref,
    bc_taps_ref,
    heads_ref,
    gx_ref,
    gdt_ref,
    gbc_ref,
    gx_taps_ref,
    gbc_taps_ref,
    gheads_ref,
    x_pad,
    bc_pad,
    dt_s,
    a_s,
    a_row_s,
    a_wide,
    mixed_s,
    scaled_s,
    bc_s,
    grad_s,
    gscaled_s,
    gap_s,
    gbc_s,
    inter_s,
    gover_s,
    faded_s,
    gfaded_s,
    fade_s,
    edge_s,
    low_s,
):
    length, width = mixed_s.shape
    count, _, bc_width = bc_ref.shape
    pieces = 2 * count
    piece = length // pieces
    blocks = length // BLOCK
    mixer_load(
        x_column,
        order_ref,
        narrow_ref,
        bc_ref,
        marks_ref,
        x_taps_ref,
        bc_taps_ref,
        heads_ref,
        x_pad,
        bc_pad,
        dt_s,
        a_s,
        a_row_s,
        a_wide,
        mixed_s,
        scaled_s,
        bc_s,
    )
    for place in range(pieces):
        source = pl.multiple_of(order_ref[place] * piece, piece)
        grad_s[place * piece : (place + 1) * piece, :] = grad_ref[pl.ds(source, piece), :]
    gscaled_s[...] = jnp.zeros_like(gscaled_s)
    gap_s[...] = jnp.zeros_like(gap_s)
    gbc_s[...] = jnp.zeros_like(gbc_s)

    def one_block(block, _):
        start = pl.multiple_of(block * BLOCK, BLOCK)
        rows = pl.ds(start, BLOCK)
        out_c = bc_s[rows, STATE : 2 * STATE]
        allowed = allowed_block(marks_ref, seg_row_ref, start, start, BLOCK, True)
        inter_s[...] = jnp.where(allowed, dot_rows(out_c, bc_s[rows, 0:STATE]), 0.0)
        gover_s[...] = jnp.zeros_like(gover_s)
        for column in range(0, width, LANES):
            lanes = slice(column, column + LANES)
            scaled = scaled_s[rows, lanes]
            grad = grad_s[rows, lanes]
            row_side = jnp.zeros((BLOCK, LANES), jnp.float32)
            col_side = jnp.zeros((BLOCK, LANES), jnp.float32)
            for half in range(2):
                head = column // SSM_DIM + half
                decay = diagonal_decay(a_s, a_row_s, block, start, head)
                weights = (inter_s[...] * decay).astype(jnp.bfloat16)
                scaled_half = half_lanes(scaled, half)
                gover_s[...] += dot_rows(grad, scaled_half) * decay
                row_side = row_side + dot_plain(weights, scaled_half)
                col_side = col_side + dot_columns(weights, half_lanes(grad, half))
            gscaled_s[rows, lanes] += col_side
            gap_s[rows, lanes] += scaled.astype(jnp.float32) * col_side - grad.astype(
                jnp.float32
            ) * row_side
        gover = jnp.where(allowed, gover_s[...], 0.0).astype(jnp.bfloat16)
        gbc_s[rows, STATE : 2 * STATE] += dot_plain(gover, bc_s[rows, 0:STATE])
        gbc_s[rows, 0:STATE] += dot_columns(gover, out_c)
        first = a_wide[pl.ds(start, 8), :][0:1]
        gfaded_s[...] = (
            grad_s[rows, :].astype(jnp.float32) * jnp.exp(first - a_wide[rows, :])
        ).astype(jnp.bfloat16)

        def earlier(other, _):
            col_start = pl.multiple_of(other * BLOCK, BLOCK)
            columns = pl.ds(col_start, BLOCK)
            same = allowed_block(marks_ref, seg_row_ref, start, col_start, BLOCK, False)
            in_b = bc_s[columns, 0:STATE]
            inter = jnp.where(same, dot_rows(out_c, in_b), 0.0).astype(jnp.bfloat16)
            fade_s[...] = jnp.exp(a_wide[columns, :] - first)
            faded_s[...] = (scaled_s[columns, :].astype(jnp.float32) * fade_s[...]).astype(
                jnp.bfloat16
            )
            over = dot_rows(gfaded_s[...], faded_s[...])
            over = jnp.where(same, over, 0.0).astype(jnp.bfloat16)
            gbc_s[rows, STATE : 2 * STATE] += dot_plain(over, in_b)
            gbc_s[columns, 0:STATE] += dot_columns(over, out_c)
            gap_s[rows, :] -= gfaded_s[...].astype(jnp.float32) * dot_plain(inter, faded_s[...])
            col_side = dot_columns(inter, gfaded_s[...])
            gap_s[columns, :] += faded_s[...].astype(jnp.float32) * col_side
            gscaled_s[columns, :] += fade_s[...] * col_side
            return 0

        lax.fori_loop(0, block, earlier, 0)
        return 0

    lax.fori_loop(0, blocks, one_block, 0)

    spread = head_spread(width)
    gather = head_gather(width)
    upper = triangle(False)
    rate = jnp.exp(heads_ref[0:1, :])
    bias = heads_ref[1:2, :]
    skip_wide = dot_exact(jnp.broadcast_to(heads_ref[2:3, :], (8, LANES)), spread)
    gx_taps_ref[...] = jnp.zeros_like(gx_taps_ref)
    gbc_taps_ref[...] = jnp.zeros_like(gbc_taps_ref)
    gheads_ref[...] = jnp.zeros_like(gheads_ref)
    edge_s[...] = jnp.zeros_like(edge_s)

    def conv_back(pad_ref, taps_ref, gtaps_ref, start, column, shift, gmixed):
        rows = pl.ds(start, BLOCK)
        total, shifted = conv_window(pad_ref, taps_ref, marks_ref, start, column)
        sig = jax.nn.sigmoid(total)
        gtotal = gmixed * sig * (1.0 + total * (1.0 - sig))
        lanes = slice(column, column + LANES)
        for tap in range(4):
            gtaps_ref[tap : tap + 1, lanes] += jnp.sum(gtotal * shifted[tap], axis=0, keepdims=True)
        gtaps_ref[4:5, lanes] += jnp.sum(gtotal, axis=0, keepdims=True)
        wide = slice(shift + column, shift + column + LANES)
        window = jnp.concatenate([gtotal, edge_s[:, wide]], axis=0)
        edge_s[:, wide] = gtotal[0:8]
        result = gtotal * taps_ref[3:4, lanes]
        for tap in range(3):
            ahead = window[3 - tap : 3 - tap + BLOCK] * marks_ref[rows, 4 + tap : 5 + tap]
            result = result + ahead * taps_ref[tap : tap + 1, lanes]
        return result.astype(jnp.bfloat16)

    def last_block(index, carry):
        block = blocks - 1 - index
        start = pl.multiple_of(block * BLOCK, BLOCK)
        rows = pl.ds(start, BLOCK)
        raw = dt_s[rows, :] + bias
        step = softplus(raw)
        gsum = dot_exact(upper, dot_exact(gap_s[rows, :], gather)) + carry
        gstep = dot_exact(gscaled_s[rows, :] * mixed_s[rows, :], gather) + gsum * rate
        graw = gstep * jax.nn.sigmoid(raw)
        gheads_ref[0:1, :] += jnp.sum(gsum * step * rate, axis=0, keepdims=True)
        gheads_ref[1:2, :] += jnp.sum(graw, axis=0, keepdims=True)
        low_s[:, width : width + LANES] = graw.astype(jnp.bfloat16)
        step_wide = dot_exact(step, spread)
        skip_parts = []
        for column in range(0, width, LANES):
            lanes = slice(column, column + LANES)
            grad = grad_s[rows, lanes].astype(jnp.float32)
            skip_parts.append(jnp.sum(grad * mixed_s[rows, lanes], axis=0, keepdims=True))
            gmixed = skip_wide[0:1, lanes] * grad + gscaled_s[rows, lanes] * step_wide[:, lanes]
            low_s[:, lanes] = conv_back(
                x_pad, x_taps_ref, gx_taps_ref, start, column, 0, gmixed
            )
        skip_row = jnp.broadcast_to(jnp.concatenate(skip_parts, axis=1), (8, width))
        gheads_ref[2:3, :] += dot_exact(skip_row, gather)[0:1]
        for column in range(0, 2 * STATE, LANES):
            lanes = slice(column, column + LANES)
            low_s[:, width + LANES + column : width + 2 * LANES + column] = conv_back(
                bc_pad, bc_taps_ref, gbc_taps_ref, start, column, width, gbc_s[rows, lanes]
            )
        for part in range(BLOCK // piece):
            place = block * (BLOCK // piece) + part
            target = pl.multiple_of(order_ref[place] * piece, piece)
            gx_ref[pl.ds(target, piece), :] = low_s[part * piece : (part + 1) * piece, 0:width]
            gdt_ref[pl.ds(target, piece), :] = low_s[
                part * piece : (part + 1) * piece, width : width + LANES
            ]
            for owner in range(count):
                first = width + LANES + owner * bc_width
                owner_start = pl.multiple_of(
                    order_ref[pieces + count + owner * pieces + place] * piece, piece
                )
                gbc_ref[order_ref[pieces + owner], pl.ds(owner_start, piece), :] = low_s[
                    part * piece : (part + 1) * piece, first : first + bc_width
                ]
        return gsum[0:1, :]

    lax.fori_loop(0, blocks, last_block, jnp.zeros((1, LANES), jnp.float32))


def local_call(kernel, outs, scratch, flops, operands):
    moved = sum(part.size * part.dtype.itemsize for part in operands)
    moved += sum(part.size * part.dtype.itemsize for part in outs)
    return pl.pallas_call(
        kernel,
        out_shape=outs,
        in_specs=[pl.BlockSpec(memory_space=pltpu.SMEM)]
        + [pl.BlockSpec(memory_space=pltpu.VMEM)] * (len(operands) - 1),
        out_specs=[pl.BlockSpec(memory_space=pltpu.VMEM)] * len(outs),
        scratch_shapes=scratch,
        compiler_params=pltpu.CompilerParams(vmem_limit_bytes=KERNEL_VMEM),
        cost_estimate=pl.CostEstimate(flops=flops, bytes_accessed=moved, transcendentals=0),
    )(*operands)


def array_of(shape, dtype):
    return jax.ShapeDtypeStruct(shape, dtype)


def attention_forward(q_width, pieces, order, narrow, cosine, sine, marks, seg_row):
    length = narrow.shape[0]
    low = jnp.bfloat16
    return local_call(
        functools.partial(attention_forward_kernel, q_width, pieces),
        [array_of((length, q_width), low), array_of((length, 8), jnp.float32)],
        [
            pltpu.VMEM((length, q_width), low),
            pltpu.VMEM((length, HEAD_DIM), low),
            pltpu.VMEM((length, HEAD_DIM), low),
        ],
        3 * length * length * q_width,
        (order, narrow, cosine, sine, marks, seg_row),
    )


def attention_backward(q_width, pieces, order, narrow, grad, cosine, sine, marks, seg_row, lse):
    length = narrow.shape[0]
    low = jnp.bfloat16
    return local_call(
        functools.partial(attention_backward_kernel, q_width, pieces),
        [array_of((length, q_width + 2 * HEAD_DIM), low)],
        [
            pltpu.VMEM((length, q_width), low),
            pltpu.VMEM((length, HEAD_DIM), low),
            pltpu.VMEM((length, HEAD_DIM), low),
            pltpu.VMEM((length, q_width), low),
            pltpu.VMEM((length, HEAD_DIM), jnp.float32),
            pltpu.VMEM((length, HEAD_DIM), jnp.float32),
        ],
        6 * length * length * q_width,
        (order, narrow, grad, cosine, sine, marks, seg_row, lse),
    )[0]


def mixer_scratch(length, width):
    low, full = jnp.bfloat16, jnp.float32
    return [
        pltpu.VMEM((length + 8, width), full),
        pltpu.VMEM((length + 8, 2 * STATE), full),
        pltpu.VMEM((length, LANES), full),
        pltpu.VMEM((length, LANES), full),
        pltpu.VMEM((length // BLOCK, LANES, BLOCK), full),
        pltpu.VMEM((length, width), full),
        pltpu.VMEM((length, width), full),
        pltpu.VMEM((length, width), low),
        pltpu.VMEM((length, 2 * STATE), low),
    ]


def mixer_forward(x_column, width, order, narrow, bc, marks, seg_row, x_taps, bc_taps, heads):
    length = narrow.shape[0]
    low, full = jnp.bfloat16, jnp.float32
    return local_call(
        functools.partial(mixer_forward_kernel, x_column),
        [array_of((length, width), low)],
        mixer_scratch(length, width)
        + [
            pltpu.VMEM((BLOCK, width), low),
            pltpu.VMEM((BLOCK, BLOCK), full),
            pltpu.VMEM((BLOCK, width), full),
        ],
        4 * length * length * width,
        (order, narrow, bc, marks, seg_row, x_taps, bc_taps, heads),
    )[0]


def mixer_backward(x_column, width, order, narrow, bc, grad, marks, seg_row, x_taps, bc_taps, heads):
    length = narrow.shape[0]
    low, full = jnp.bfloat16, jnp.float32
    return local_call(
        functools.partial(mixer_backward_kernel, x_column),
        [
            array_of((length, width), low),
            array_of((length, LANES), low),
            array_of(bc.shape, low),
            array_of((8, width), full),
            array_of((8, 2 * STATE), full),
            array_of((8, LANES), full),
        ],
        mixer_scratch(length, width)
        + [
            pltpu.VMEM((length, width), low),
            pltpu.VMEM((length, width), full),
            pltpu.VMEM((length, width), full),
            pltpu.VMEM((length, 2 * STATE), full),
            pltpu.VMEM((BLOCK, BLOCK), full),
            pltpu.VMEM((BLOCK, BLOCK), full),
            pltpu.VMEM((BLOCK, width), low),
            pltpu.VMEM((BLOCK, width), low),
            pltpu.VMEM((BLOCK, width), full),
            pltpu.VMEM((8, width + 2 * STATE), full),
            pltpu.VMEM((BLOCK, width + LANES + 2 * STATE), low),
        ],
        10 * length * length * width,
        (order, narrow, bc, grad, marks, seg_row, x_taps, bc_taps, heads),
    )


def document_marks(seg_row):
    length = seg_row.shape[0]
    before = jnp.pad(seg_row, (3, 0), constant_values=-1)
    after = jnp.pad(seg_row, (0, 3), constant_values=-1)
    columns = [seg_row.astype(jnp.float32)]
    for tap in range(3):
        columns.append((before[tap : tap + length] == seg_row).astype(jnp.float32))
    for tap in range(3):
        columns.append((after[3 - tap : 3 - tap + length] == seg_row).astype(jnp.float32))
    columns.append(jnp.zeros((length,), jnp.float32))
    return jnp.stack(columns, axis=1)


def rope_wide(length):
    half_dim = HEAD_DIM // 2
    frequency = rope_base ** (-jnp.arange(half_dim, dtype=jnp.float32) / half_dim)
    angles = jnp.arange(length, dtype=jnp.float32)[:, None] * frequency[None, :]
    cosine, sine = jnp.cos(angles), jnp.sin(angles)
    return jnp.concatenate([cosine, cosine], axis=1), jnp.concatenate([-sine, sine], axis=1)


def swap_seq(value, bit, count):
    return lax.ppermute(value, "seq", [(place, place ^ bit) for place in range(count)])


def shift_fsdp(value, step, count):
    pairs = [
        (place, place + step) for place in range(count) if 0 <= place + step < count
    ]
    return lax.ppermute(value, "fsdp", pairs)


def seq_bits(count):
    bits = []
    bit = 1
    while bit < count:
        bits.append(bit)
        bit *= 2
    return bits


def block_order(bits):
    order = [0]
    for bit in bits:
        order = order + [place ^ bit for place in order]
    return order


def relative_order(count):
    bits = seq_bits(count)
    upper = [(0, block) for block in block_order(bits)]
    lower = [(1, block) for block in block_order(bits[::-1])]
    near = count // 2
    return upper[:near] + lower[:near] + upper[near:] + lower[near:]


def rows_gather(rows, count):
    half = rows.shape[0] // 2
    bits = seq_bits(count)
    near, far = [], []
    for piece, order in ((rows[:half], bits), (rows[half:], bits[::-1])):
        for bit in order[:-1]:
            piece = jnp.concatenate([piece, swap_seq(piece, bit, count)], axis=0)
        near.append(piece)
        far.append(swap_seq(piece, order[-1], count))
    return jnp.concatenate(near, axis=0), jnp.concatenate(far, axis=0)


def rows_scatter(near, far, count):
    half = near.shape[0] // 2
    bits = seq_bits(count)
    far = far.astype(jnp.bfloat16)
    parts = []
    for first, order in ((0, bits), (half, bits[::-1])):
        came = swap_seq(far[first : first + half], order[-1], count)
        piece = near[first : first + half] + came.astype(jnp.float32)
        for bit in order[:-1][::-1]:
            keep = piece.shape[0] // 2
            came = swap_seq(piece[keep:].astype(jnp.bfloat16), bit, count)
            piece = piece[:keep] + came.astype(jnp.float32)
        parts.append(piece)
    return jnp.concatenate(parts, axis=0)


def true_rows(rank, count):
    order = relative_order(count)
    blocks = jnp.arange(count, dtype=jnp.int32) ^ rank
    tables = [
        jnp.asarray([order.index((half, block)) for block in range(count)], jnp.int32)[blocks]
        for half in range(2)
    ]
    return jnp.stack(tables, axis=1).reshape(-1)


def seq_pieces(value, count):
    return [value] + [swap_seq(value, bit, count) for bit in range(1, count)]


def seq_sum(value, count):
    order = relative_order(count)
    total = value.reshape(2 * count, -1)
    for bit in range(1, count):
        came = swap_seq(value, bit, count).reshape(2 * count, -1)
        places = [order.index((half, block ^ bit)) for half, block in order]
        total = total + jnp.concatenate([came[place : place + 1] for place in places])
    return total.reshape(-1)


def seq_stack(value, rank, count):
    result = jnp.zeros((count,) + value.shape, value.dtype)
    for bit, piece in enumerate(seq_pieces(value, count)):
        result = lax.dynamic_update_index_in_dim(result, piece, rank ^ bit, 0)
    return result


def seq_reduce_blocks(blocks, rank, count):
    total = lax.dynamic_index_in_dim(blocks, rank, 0, False).astype(jnp.float32)
    for bit in range(1, count):
        block = lax.dynamic_index_in_dim(blocks, rank ^ bit, 0, False)
        total = total + swap_seq(block, bit, count).astype(jnp.float32)
    return total


def small_gather(vector, seq_count, fsdp_count):
    rank = lax.axis_index("seq")
    place = lax.axis_index("fsdp")
    chips = fsdp_count // 2
    by_seq = seq_stack(vector, rank, seq_count)
    other = lax.ppermute(by_seq, "fsdp", [(spot, spot ^ 1) for spot in range(fsdp_count)])
    core = place % 2
    pair = jnp.where(core == 0, jnp.stack([by_seq, other]), jnp.stack([other, by_seq]))
    line = [shift_fsdp(pair, 2 * step, fsdp_count) for step in range(chips - 1, 0, -1)]
    line.append(pair)
    line += [shift_fsdp(pair, -2 * step, fsdp_count) for step in range(1, chips)]
    chip_rows = lax.dynamic_slice_in_dim(jnp.stack(line), chips - 1 - place // 2, chips, 0)
    return chip_rows.reshape(fsdp_count, seq_count, -1).transpose(1, 0, 2)


def small_scatter(vectors, seq_count, fsdp_count):
    rank = lax.axis_index("seq")
    place = lax.axis_index("fsdp")
    chips = fsdp_count // 2
    rows = seq_reduce_blocks(vectors, rank, seq_count).reshape(chips, 2, -1)
    core = place % 2
    away = lax.dynamic_index_in_dim(rows, 1 - core, 1, False)
    kept = lax.dynamic_index_in_dim(rows, core, 1, False)
    kept = kept + lax.ppermute(away, "fsdp", [(spot, spot ^ 1) for spot in range(fsdp_count)])
    chip = place // 2
    total = lax.dynamic_index_in_dim(kept, chip, 0, False)
    for step in range(1, chips):
        ahead = lax.dynamic_index_in_dim(kept, jnp.minimum(chip + step, chips - 1), 0, False)
        behind = lax.dynamic_index_in_dim(kept, jnp.maximum(chip - step, 0), 0, False)
        total = total + shift_fsdp(ahead, 2 * step, fsdp_count)
        total = total + shift_fsdp(behind, -2 * step, fsdp_count)
    return total


def norm_forward(rows, gain):
    scale = lax.rsqrt(jnp.mean(rows * rows, axis=-1, keepdims=True) + epsilon)
    return ((rows * scale * gain).astype(jnp.bfloat16), scale)


def norm_backward(rows, scale, gain, cotangent):
    weighted = cotangent * gain
    inner = jnp.mean(rows * weighted, axis=-1, keepdims=True)
    grad_rows = scale * weighted - rows * (scale * scale * scale * inner)
    return (grad_rows, jnp.sum(cotangent * rows * scale, axis=0))


def columns_gather(blocks):
    arrived = lax.all_to_all(blocks, "seq", split_axis=0, concat_axis=0, tiled=True)
    columns = blocks.shape[2]
    return lax.all_gather(arrived, "fsdp", axis=1, tiled=True).reshape(-1, columns)


def columns_to_owners(blocks, count):
    blocks = with_layout_constraint(blocks, Layout(major_to_minor=(0, 1, 2)))
    arrived = lax.all_to_all(blocks, "seq", split_axis=0, concat_axis=0, tiled=True)
    return [arrived[place].astype(jnp.float32) for place in range(count)]


def side_by_side(parts, first, width):
    return jnp.concatenate([part[:, first : first + width] for part in parts], axis=1)


def body(
    seq_count,
    fsdp_count,
    hidden_in,
    segments,
    out_grad,
    norm1_gain,
    w_query,
    w_keyval,
    w_attn_out,
    w_gate_z,
    w_ssm_x,
    w_ssm_bc,
    w_ssm_dt,
    conv_taps,
    a_log,
    dt_bias,
    skip_gain,
    ssm_gain,
    w_ssm_out,
    norm2_gain,
    w_ff_gate,
    w_ff_up,
    w_ff_down,
):
    f32, bf16 = jnp.float32, jnp.bfloat16
    batch, block_len, model_width = hidden_in.shape
    length = block_len * seq_count
    rank = lax.axis_index("seq")
    seg_row = segments[0]
    heads_local = HEADS // seq_count
    group_size = HEADS // KV_HEADS
    q_width = w_query.shape[1] // seq_count
    z_width = w_gate_z.shape[1] // seq_count
    x_width = w_ssm_x.shape[1] // seq_count
    bc_width = w_ssm_bc.shape[1] // seq_count
    dt_width = w_ssm_dt.shape[1] // seq_count
    ff_width = w_ff_gate.shape[1] // seq_count
    kv_total = w_keyval.shape[1] // 2
    heads_total = a_log.shape[0]
    dssm = w_ssm_x.shape[1]
    row_piece = w_query.shape[0]
    bc_pad = -bc_width % LANES
    dt_pad = -dt_width % LANES

    sends = []
    for target in range(seq_count):
        kv_head = target * heads_local // group_size
        sends.append(
            jnp.concatenate(
                [
                    w_query[:, target * q_width : (target + 1) * q_width],
                    w_keyval[:, kv_head * HEAD_DIM : (kv_head + 1) * HEAD_DIM],
                    w_keyval[:, kv_total + kv_head * HEAD_DIM : kv_total + (kv_head + 1) * HEAD_DIM],
                    w_ssm_x[:, target * x_width : (target + 1) * x_width],
                    w_ssm_bc[:, target * bc_width : (target + 1) * bc_width],
                    jnp.zeros((row_piece, bc_pad), bf16),
                    w_ssm_dt[:, target * dt_width : (target + 1) * dt_width],
                    jnp.zeros((row_piece, dt_pad), bf16),
                ],
                axis=1,
            )
        )
    narrow_w = columns_gather(jnp.stack(sends))
    w_gate_z, w_ff_gate, w_ff_up, out_grad = lax.optimization_barrier(
        (w_gate_z, w_ff_gate, w_ff_up, out_grad)
    )
    z_w = columns_gather(
        jnp.stack(
            [
                w_gate_z[:, target * z_width : (target + 1) * z_width]
                for target in range(seq_count)
            ]
        )
    )
    out_piece = jnp.concatenate([w_attn_out, w_ssm_out], axis=0)
    out_w = lax.all_gather(out_piece, "fsdp", axis=0)

    taps_rows, taps_width = conv_taps.shape
    gains = jnp.concatenate([norm1_gain, norm2_gain, ssm_gain, conv_taps.reshape(-1)])
    gain_count = norm1_gain.shape[0]
    ssm_count = ssm_gain.shape[0]
    gathered = small_gather(gains, seq_count, fsdp_count).astype(f32)
    gain1 = gathered[:, :, :gain_count].reshape(-1)
    gain2 = gathered[:, :, gain_count : 2 * gain_count].reshape(-1)
    gain_ssm = gathered[:, :, 2 * gain_count : 2 * gain_count + ssm_count].reshape(seq_count, -1)
    gain_ssm = lax.dynamic_index_in_dim(gain_ssm, rank, 0, False)
    taps_full = gathered[:, :, 2 * gain_count + ssm_count :].reshape(-1, taps_width)
    taps_rows8 = jnp.pad(taps_full.T, ((0, 8 - taps_width), (0, 0)))
    x_taps = lax.dynamic_slice_in_dim(taps_rows8, rank * x_width, x_width, 1)
    bc_taps = taps_rows8[:, dssm:]
    head_rows = lax.dynamic_slice_in_dim(
        jnp.stack([a_log, dt_bias, skip_gain]), rank * dt_width, dt_width, 1
    )
    head_rows = jnp.pad(head_rows, ((0, 5), (0, dt_pad)))
    marks = document_marks(seg_row)
    seg_line = jnp.broadcast_to(seg_row.astype(f32)[None, :], (8, length))

    to_true = true_rows(rank, seq_count)
    ranks = jnp.arange(seq_count, dtype=jnp.int32)
    to_true = jnp.concatenate(
        [to_true, ranks ^ rank] + [true_rows(other, seq_count) for other in range(seq_count)]
    )
    pieces = 2 * seq_count

    own_in = hidden_in.reshape(block_len, model_width)
    all_in = jnp.concatenate(rows_gather(own_in, seq_count), axis=0)
    all_in, w_ff_gate, w_ff_up = lax.optimization_barrier((all_in, w_ff_gate, w_ff_up))
    ff_sends = jnp.stack(
        [
            jnp.concatenate(
                [
                    w_ff_gate[:, target * ff_width : (target + 1) * ff_width],
                    w_ff_up[:, target * ff_width : (target + 1) * ff_width],
                ],
                axis=1,
            )
            for target in range(seq_count)
        ]
    )
    ff_w = columns_gather(ff_sends)
    normed, _ = norm_forward(all_in.astype(f32), gain1)
    edges = [0]
    for width in (q_width, HEAD_DIM, HEAD_DIM, x_width, bc_width + bc_pad, dt_width + dt_pad):
        edges.append(edges[-1] + width)
    narrow = mat_product(normed, narrow_w).astype(bf16)
    bc_seq = jnp.stack(seq_pieces(narrow[:, edges[4] : edges[4] + bc_width], seq_count))
    cosine, sine = rope_wide(length)
    attn_rel, lse_seq = attention_forward(
        q_width, pieces, to_true, narrow, cosine, sine, marks, seg_line
    )
    bc_seq, attn_rel, out_grad, w_ff_down = lax.optimization_barrier(
        (bc_seq, attn_rel, out_grad, w_ff_down)
    )
    down_w = lax.all_gather(w_ff_down, "fsdp", axis=0, tiled=True)
    mixer_args = (x_taps, bc_taps, head_rows)
    ssm_rel = mixer_forward(
        edges[3], x_width, to_true, narrow, bc_seq, marks, seg_line, *mixer_args
    )
    ssm_rel, out_w, z_w = lax.optimization_barrier((ssm_rel, out_w, z_w))
    ssm_rel = ssm_rel.astype(f32)
    attn_out_w = out_w[:, : w_attn_out.shape[0]].reshape(-1, model_width)
    ssm_out_w = out_w[:, w_attn_out.shape[0] :].reshape(-1, model_width)
    gate_z = mat_product(normed, z_w)
    gate_sig = jax.nn.sigmoid(gate_z)
    gate_silu = gate_z * gate_sig
    gated = ssm_rel * gate_silu
    square_sum = seq_sum(jnp.sum(gated * gated, axis=1), seq_count)
    gated_scale = lax.rsqrt(square_sum / dssm + epsilon)[:, None]
    ssm_in = (gated * gated_scale * gain_ssm).astype(bf16)
    near = length // 2

    def out_product(first):
        rows = slice(first, first + near)
        return mat_product(attn_rel[rows], attn_out_w) + mat_product(ssm_in[rows], ssm_out_w)

    xin = own_in.astype(f32)
    middle = xin + rows_scatter(out_product(0), out_product(near), seq_count)

    own_normed2, scale2 = norm_forward(middle, gain2)
    normed2 = rows_gather(own_normed2, seq_count)
    grad_own = out_grad.reshape(block_len, model_width)
    grad_ff = rows_gather(grad_own, seq_count)
    acts, grad_pairs = [], []
    for part in range(2):
        gate_ff = mat_product(normed2[part], ff_w[:, :ff_width])
        up_ff = mat_product(normed2[part], ff_w[:, ff_width:])
        ff_sig = jax.nn.sigmoid(gate_ff)
        ff_silu = gate_ff * ff_sig
        acts.append((ff_silu * up_ff).astype(bf16))
        grad_act = input_grad(grad_ff[part], down_w)
        grad_gate_ff = grad_act * up_ff * (ff_sig + ff_silu * (1.0 - ff_sig))
        grad_up_ff = grad_act * ff_silu
        grad_pairs.append(
            jnp.concatenate([grad_gate_ff.astype(bf16), grad_up_ff.astype(bf16)], axis=1)
        )
    act = jnp.concatenate(acts, axis=0)
    grad_w_down = weight_grad(act, jnp.concatenate(grad_ff, axis=0)).astype(bf16)
    grad_w_ff = weight_grad(
        jnp.concatenate(normed2, axis=0), jnp.concatenate(grad_pairs, axis=0)
    ).astype(bf16)
    grad_normed2 = rows_scatter(
        input_grad(grad_pairs[0], ff_w), input_grad(grad_pairs[1], ff_w), seq_count
    )
    grad_w_down = lax.psum_scatter(grad_w_down, "fsdp", scatter_dimension=0, tiled=True)
    grad_normed2, grad_w_down, grad_w_ff = lax.optimization_barrier(
        (grad_normed2, grad_w_down, grad_w_ff)
    )
    grad_w_ff = lax.psum_scatter(
        grad_w_ff.reshape(seq_count, -1, 2 * ff_width), "fsdp", scatter_dimension=1, tiled=True
    )
    grad_middle_norm, grad_gain2 = norm_backward(middle, scale2, gain2, grad_normed2)
    grad_middle = grad_own.astype(f32) + grad_middle_norm

    grad_mix = jnp.concatenate(rows_gather(grad_middle.astype(bf16), seq_count), axis=0)
    grad_w_attn = weight_grad(attn_rel, grad_mix).astype(bf16)
    grad_w_ssm = weight_grad(ssm_in, grad_mix).astype(bf16)
    grad_attn = input_grad(grad_mix, attn_out_w).astype(bf16)
    grad_ssm_in = input_grad(grad_mix, ssm_out_w)
    weighted = grad_ssm_in * gain_ssm
    inner = seq_sum(jnp.sum(gated * weighted, axis=1), seq_count)[:, None] / dssm
    grad_gated = gated_scale * weighted - gated * (
        gated_scale * gated_scale * gated_scale * inner
    )
    grad_gain_ssm = jnp.sum(grad_ssm_in * gated * gated_scale, axis=0)
    grad_ssm = (grad_gated * gate_silu).astype(bf16)
    grad_z = (grad_gated * ssm_rel * (gate_sig + gate_silu * (1.0 - gate_sig))).astype(bf16)
    out_grads = jnp.concatenate(
        [
            grad_w_attn.reshape(fsdp_count, -1, model_width),
            grad_w_ssm.reshape(fsdp_count, -1, model_width),
        ],
        axis=1,
    )
    grad_w_z = weight_grad(normed, grad_z).astype(bf16)
    grad_attn, grad_ssm, out_grads, grad_w_z, grad_w_ff, act = lax.optimization_barrier(
        (grad_attn, grad_ssm, out_grads, grad_w_z, grad_w_ff, act)
    )
    out_grads = lax.psum_scatter(out_grads, "fsdp", scatter_dimension=0, tiled=True)[0]
    grad_w_z = lax.psum_scatter(
        grad_w_z.reshape(seq_count, -1, z_width), "fsdp", scatter_dimension=1, tiled=True
    )
    layer_out = middle + rows_scatter(
        mat_product(act[:near], down_w), mat_product(act[near:], down_w), seq_count
    )
    grad_x, grad_dt, grad_bc_part, grad_x_taps, grad_bc_taps, grad_heads = mixer_backward(
        edges[3], x_width, to_true, narrow, bc_seq, grad_ssm, marks, seg_line, *mixer_args
    )
    grad_bc = grad_bc_part[0].astype(f32)
    for bit in range(1, seq_count):
        grad_bc = grad_bc + swap_seq(grad_bc_part[bit], bit, seq_count).astype(f32)
    grad_bc = grad_bc.astype(bf16)
    grad_w_x = weight_grad(normed, grad_x).astype(bf16)
    grad_attn, out_grads, grad_w_x = lax.optimization_barrier((grad_attn, out_grads, grad_w_x))
    grad_w_x = lax.psum_scatter(
        grad_w_x.reshape(seq_count, -1, x_width), "fsdp", scatter_dimension=1, tiled=True
    )
    grad_qkv = attention_backward(
        q_width, pieces, to_true, narrow, grad_attn, cosine, sine, marks, seg_line, lse_seq
    )
    bc_zeros = jnp.zeros((length, bc_pad), bf16)
    grad_rest = jnp.concatenate([grad_qkv, grad_bc, bc_zeros, grad_dt], axis=1)
    grad_narrow = jnp.concatenate([grad_qkv, grad_x, grad_bc, bc_zeros, grad_dt], axis=1)
    grad_w_rest = weight_grad(normed, grad_rest).astype(bf16)
    grad_narrow, grad_w_rest, grad_w_z = lax.optimization_barrier(
        (grad_narrow, grad_w_rest, grad_w_z)
    )
    grad_w_rest = lax.psum_scatter(
        grad_w_rest.reshape(seq_count, -1, grad_rest.shape[1]),
        "fsdp",
        scatter_dimension=1,
        tiled=True,
    )

    def first_product(first):
        rows = slice(first, first + near)
        return input_grad(grad_narrow[rows], narrow_w) + input_grad(grad_z[rows], z_w)

    grad_normed = rows_scatter(first_product(0), first_product(near), seq_count)
    _, scale1 = norm_forward(xin, gain1)
    grad_in_norm, grad_gain1 = norm_backward(xin, scale1, gain1, grad_normed)
    grad_in = grad_middle + grad_in_norm

    per_device = (seq_count, fsdp_count, -1)
    x_conv = lax.dynamic_update_slice_in_dim(
        jnp.zeros((dssm, taps_width), f32), grad_x_taps[:taps_width].T, rank * x_width, 0
    )
    conv_grads = jnp.concatenate([x_conv, grad_bc_taps[:taps_width].T], axis=0).reshape(per_device)
    ssm_grads = lax.dynamic_update_index_in_dim(
        jnp.zeros((seq_count, z_width), f32), grad_gain_ssm, rank, 0
    ).reshape(per_device)
    head_grads = lax.dynamic_update_slice(
        jnp.zeros((3, heads_total), f32),
        grad_heads[:3, :dt_width],
        (jnp.int32(0), rank * dt_width),
    )
    head_grads = jnp.broadcast_to(
        head_grads.reshape(1, 1, -1), (seq_count, fsdp_count, 3 * heads_total)
    )
    small = small_scatter(
        jnp.concatenate(
            [
                grad_gain1.reshape(per_device),
                grad_gain2.reshape(per_device),
                ssm_grads,
                conv_grads,
                head_grads,
            ],
            axis=2,
        ),
        seq_count,
        fsdp_count,
    )
    small_edges = [0]
    for width in (gain_count, gain_count, ssm_count, taps_rows * taps_width, 3 * heads_total):
        small_edges.append(small_edges[-1] + width)
    out_gain1, out_gain2, out_ssm_gain, out_conv, out_heads = (
        small[small_edges[part] : small_edges[part + 1]] for part in range(5)
    )
    out_heads = out_heads.reshape(3, heads_total)

    ff_cols = columns_to_owners(grad_w_ff, seq_count)
    z_cols = columns_to_owners(grad_w_z, seq_count)
    x_cols = columns_to_owners(grad_w_x, seq_count)
    rest_cols = columns_to_owners(grad_w_rest, seq_count)
    bc_first = edges[3]
    dt_first = bc_first + bc_width + bc_pad
    ranks_per_kv = group_size // heads_local
    kv_cols = []
    for first in (edges[1], edges[2]):
        for head in range(KV_HEADS):
            shares = rest_cols[head * ranks_per_kv : (head + 1) * ranks_per_kv]
            kv_cols.append(sum(share[:, first : first + HEAD_DIM] for share in shares))
    attn_rows = w_attn_out.shape[0]
    return (
        layer_out.astype(bf16).reshape(batch, block_len, model_width),
        grad_in.astype(bf16).reshape(batch, block_len, model_width),
        out_gain1,
        side_by_side(rest_cols, 0, q_width),
        jnp.concatenate(kv_cols, axis=1),
        out_grads[:attn_rows].astype(f32),
        side_by_side(z_cols, 0, z_width),
        side_by_side(x_cols, 0, x_width),
        side_by_side(rest_cols, bc_first, bc_width),
        side_by_side(rest_cols, dt_first, dt_width),
        out_conv.reshape(taps_rows, taps_width),
        out_heads[0],
        out_heads[1],
        out_heads[2],
        out_ssm_gain,
        out_grads[attn_rows:].astype(f32),
        out_gain2,
        side_by_side(ff_cols, 0, ff_width),
        side_by_side(ff_cols, ff_width, ff_width),
        grad_w_down.astype(f32),
    )


def solution(mesh):
    in_specs = (
        P("fsdp", "seq", None),
        P("fsdp", None),
        P("fsdp", "seq", None),
        P(("seq", "fsdp")),
        P(("seq", "fsdp"), None),
        P(("seq", "fsdp"), None),
        P(("seq", "fsdp"), None),
        P(("seq", "fsdp"), None),
        P(("seq", "fsdp"), None),
        P(("seq", "fsdp"), None),
        P(("seq", "fsdp"), None),
        P(("seq", "fsdp"), None),
        P(),
        P(),
        P(),
        P(("seq", "fsdp")),
        P(("seq", "fsdp"), None),
        P(("seq", "fsdp")),
        P(("seq", "fsdp"), None),
        P(("seq", "fsdp"), None),
        P(("seq", "fsdp"), None),
    )
    out_specs = (
        P("fsdp", "seq", None),
        P("fsdp", "seq", None),
        P(("seq", "fsdp")),
        P(("seq", "fsdp"), None),
        P(("seq", "fsdp"), None),
        P(("seq", "fsdp"), None),
        P(("seq", "fsdp"), None),
        P(("seq", "fsdp"), None),
        P(("seq", "fsdp"), None),
        P(("seq", "fsdp"), None),
        P(("seq", "fsdp"), None),
        P(),
        P(),
        P(),
        P(("seq", "fsdp")),
        P(("seq", "fsdp"), None),
        P(("seq", "fsdp")),
        P(("seq", "fsdp"), None),
        P(("seq", "fsdp"), None),
        P(("seq", "fsdp"), None),
    )
    step = functools.partial(body, mesh.shape["seq"], mesh.shape["fsdp"])
    return jax.shard_map(step, mesh=mesh, in_specs=in_specs, out_specs=out_specs, check_vma=False)
```

```python
import functools

import jax
import jax.numpy as jnp
from jax import lax
from jax.experimental import pallas as pl
from jax.experimental.layout import Layout, with_layout_constraint
from jax.experimental.pallas import tpu as pltpu
from jax.sharding import PartitionSpec as P

HEADS = 8
KV_HEADS = 2
HEAD_DIM = 128
SSM_DIM = 64
STATE = 256
BLOCK = 256
LANES = 128
KERNEL_VMEM = 56 * 1024 * 1024


epsilon = 1e-05
rope_base = 10000.0
masked_score = -1e30


def mat_product(left_op, right_op):
    return jnp.dot(left_op, right_op, preferred_element_type=jnp.float32)


def weight_grad(left_op, right_op):
    return lax.dot_general(
        left_op, right_op, (((0,), (0,)), ((), ())), preferred_element_type=jnp.float32
    )


def input_grad(grad_rows, weights):
    return lax.dot_general(
        grad_rows, weights, (((1,), (1,)), ((), ())), preferred_element_type=jnp.float32
    )


def dot_plain(left_op, right_op):
    return jnp.dot(left_op, right_op, preferred_element_type=jnp.float32)


def dot_ones(left_op, ones, terms):
    total = None
    for _ in range(terms):
        part = left_op.astype(jnp.bfloat16)
        product = dot_plain(part, ones)
        total = product if total is None else total + product
        left_op = left_op - part.astype(jnp.float32)
    return total


def ones_dot(ones, right_op, terms):
    total = None
    for _ in range(terms):
        part = right_op.astype(jnp.bfloat16)
        product = dot_plain(ones, part)
        total = product if total is None else total + product
        right_op = right_op - part.astype(jnp.float32)
    return total


def logistic(values):
    return 0.5 * jnp.tanh(0.5 * values) + 0.5


def dot_rows(left_op, right_op):
    return lax.dot_general(
        left_op, right_op, (((1,), (1,)), ((), ())), preferred_element_type=jnp.float32
    )


def dot_columns(left_op, right_op):
    return lax.dot_general(
        left_op, right_op, (((0,), (0,)), ((), ())), preferred_element_type=jnp.float32
    )


def iota_of(shape, axis):
    return lax.broadcasted_iota(jnp.int32, shape, axis)


def allowed_block(marks_ref, seg_row_ref, row_start, col_start, columns, diagonal):
    seg_col = marks_ref[pl.ds(row_start, BLOCK), 0:1]
    seg_row = seg_row_ref[0:1, pl.ds(col_start, columns)]
    same = seg_col == seg_row
    if diagonal:
        row_pos = row_start + iota_of((BLOCK, columns), 0)
        col_pos = col_start + iota_of((BLOCK, columns), 1)
        same = same & (row_pos >= col_pos)
    return same


def store_relative(order_ref, target, piece, row_start, column, values):
    rows, width = values.shape
    for part in range(rows // piece):
        place = row_start // piece + part
        start = pl.multiple_of(order_ref[place] * piece, piece)
        target[pl.ds(start, piece), column : column + width] = values[
            part * piece : (part + 1) * piece
        ]


def attention_load(pieces, order_ref, narrow_ref, cos_ref, sin_ref, q_s, k_s, v_s, q_width):
    length = narrow_ref.shape[0]
    piece = length // pieces
    for place in range(pieces):
        start = pl.multiple_of(order_ref[place] * piece, piece)
        rows = slice(place * piece, (place + 1) * piece)
        cosine = cos_ref[rows, :]
        sine = sin_ref[rows, :]
        for column in range(0, q_width + HEAD_DIM, HEAD_DIM):
            part = narrow_ref[pl.ds(start, piece), column : column + HEAD_DIM].astype(jnp.float32)
            turned = part * cosine + pltpu.roll(part, HEAD_DIM // 2, 1) * sine
            if column < q_width:
                q_s[rows, column : column + HEAD_DIM] = turned.astype(jnp.bfloat16)
            else:
                k_s[rows, :] = turned.astype(jnp.bfloat16)
        v_s[rows, :] = narrow_ref[
            pl.ds(start, piece), q_width + HEAD_DIM : q_width + 2 * HEAD_DIM
        ]


def attention_forward_kernel(
    q_width,
    pieces,
    order_ref,
    narrow_ref,
    cos_ref,
    sin_ref,
    marks_ref,
    seg_row_ref,
    out_ref,
    lse_ref,
    q_s,
    k_s,
    v_s,
):
    length = narrow_ref.shape[0]
    piece = length // pieces
    attention_load(pieces, order_ref, narrow_ref, cos_ref, sin_ref, q_s, k_s, v_s, q_width)
    for block in range(length // BLOCK):
        start = block * BLOCK
        columns = start + BLOCK
        allowed = allowed_block(marks_ref, seg_row_ref, start, 0, columns, True)
        for head in range(q_width // HEAD_DIM):
            lanes = slice(head * HEAD_DIM, (head + 1) * HEAD_DIM)
            scores = dot_rows(q_s[start : start + BLOCK, lanes], k_s[0:columns, :])
            scores = jnp.where(allowed, scores * HEAD_DIM ** (-0.5), masked_score)
            row_max = jnp.max(scores, axis=1, keepdims=True)
            exponent = jnp.exp(scores - row_max)
            total = jnp.sum(exponent, axis=1, keepdims=True)
            probs = (exponent * (1.0 / total)).astype(jnp.bfloat16)
            mixed = dot_plain(probs, v_s[0:columns, :]).astype(jnp.bfloat16)
            store_relative(order_ref, out_ref, piece, start, head * HEAD_DIM, mixed)
            lse_ref[start : start + BLOCK, head : head + 1] = row_max + jnp.log(total)


def attention_backward_kernel(
    q_width,
    pieces,
    order_ref,
    narrow_ref,
    grad_ref,
    cos_ref,
    sin_ref,
    marks_ref,
    seg_row_ref,
    lse_ref,
    out_ref,
    q_s,
    k_s,
    v_s,
    g_s,
    dk_s,
    dv_s,
):
    length = narrow_ref.shape[0]
    piece = length // pieces
    scale = HEAD_DIM ** (-0.5)
    attention_load(pieces, order_ref, narrow_ref, cos_ref, sin_ref, q_s, k_s, v_s, q_width)
    for place in range(pieces):
        rows = slice(place * piece, (place + 1) * piece)
        start = pl.multiple_of(order_ref[place] * piece, piece)
        g_s[rows, :] = grad_ref[pl.ds(start, piece), 0:q_width]
    dk_s[...] = jnp.zeros_like(dk_s)
    dv_s[...] = jnp.zeros_like(dv_s)
    for block in range(length // BLOCK):
        start = block * BLOCK
        columns = start + BLOCK
        rows = slice(start, columns)
        cosine = cos_ref[rows, :]
        sine = sin_ref[rows, :]
        allowed = allowed_block(marks_ref, seg_row_ref, start, 0, columns, True)
        for head in range(q_width // HEAD_DIM):
            lanes = slice(head * HEAD_DIM, (head + 1) * HEAD_DIM)
            q_blk = q_s[rows, lanes]
            g_blk = g_s[rows, lanes]
            scores = dot_rows(q_blk, k_s[0:columns, :])
            scores = jnp.where(allowed, scores * scale, masked_score)
            probs = jnp.exp(scores - lse_ref[rows, head : head + 1])
            grad_probs = dot_rows(g_blk, v_s[0:columns, :])
            inner = jnp.sum(grad_probs * probs, axis=1, keepdims=True)
            grad_scores = (probs * (grad_probs - inner)).astype(jnp.bfloat16)
            grad_q = dot_plain(grad_scores, k_s[0:columns, :]) * scale
            grad_q = grad_q * cosine - pltpu.roll(grad_q, HEAD_DIM // 2, 1) * sine
            store_relative(
                order_ref, out_ref, piece, start, head * HEAD_DIM, grad_q.astype(jnp.bfloat16)
            )
            dk_s[0:columns, :] += dot_columns(grad_scores, q_blk)
            dv_s[0:columns, :] += dot_columns(probs.astype(jnp.bfloat16), g_blk)
    for block in range(length // BLOCK):
        start = block * BLOCK
        rows = slice(start, start + BLOCK)
        grad_k = dk_s[rows, :] * scale
        grad_k = grad_k * cos_ref[rows, :] - pltpu.roll(grad_k, HEAD_DIM // 2, 1) * sin_ref[rows, :]
        store_relative(order_ref, out_ref, piece, start, q_width, grad_k.astype(jnp.bfloat16))
        store_relative(
            order_ref,
            out_ref,
            piece,
            start,
            q_width + HEAD_DIM,
            dv_s[rows, :].astype(jnp.bfloat16),
        )


def head_spread(width):
    heads = iota_of((LANES, width), 0)
    return (iota_of((LANES, width), 1) // SSM_DIM == heads).astype(jnp.float32).astype(jnp.bfloat16)


def head_gather(width):
    heads = iota_of((width, LANES), 1)
    return (iota_of((width, LANES), 0) // SSM_DIM == heads).astype(jnp.float32).astype(jnp.bfloat16)


def triangle(lower):
    rows = iota_of((BLOCK, BLOCK), 0)
    columns = iota_of((BLOCK, BLOCK), 1)
    return (rows >= columns if lower else rows <= columns).astype(jnp.float32).astype(jnp.bfloat16)


def softplus(values):
    return jnp.maximum(values, 0.0) + jnp.log1p(jnp.exp(-jnp.abs(values)))


def mark_columns(marks_ref, row_start, first):
    return [
        jnp.broadcast_to(marks_ref[pl.ds(row_start, BLOCK), first + tap : first + tap + 1], (BLOCK, LANES))
        for tap in range(3)
    ]


def conv_window(pad_ref, taps_ref, before, row_start, column):
    total = jnp.broadcast_to(taps_ref[4:5, column : column + LANES], (BLOCK, LANES))
    shifted = []
    for tap in range(4):
        rows = pad_ref[column // LANES, pl.ds(row_start + 5 + tap, BLOCK), :]
        if tap < 3:
            rows = rows * before[tap]
        shifted.append(rows)
        total = total + rows * taps_ref[tap : tap + 1, column : column + LANES]
    return total, shifted


def mixer_load(
    x_column,
    order_ref,
    narrow_ref,
    bc_ref,
    marks_ref,
    x_taps_ref,
    bc_taps_ref,
    heads_ref,
    x_pad,
    bc_pad,
    dt_s,
    a_s,
    a_row_s,
    a_wide,
    mixed_s,
    scaled_s,
    bc_s,
):
    length, width = mixed_s.shape
    count, _, bc_width = bc_ref.shape
    pieces = 2 * count
    piece = length // pieces
    dt_column = narrow_ref.shape[1] - LANES
    x_pad[:, 0:8, :] = jnp.zeros((width // LANES, 8, LANES), jnp.float32)
    bc_pad[:, 0:8, :] = jnp.zeros((2 * STATE // LANES, 8, LANES), jnp.float32)
    for place in range(pieces):
        start = pl.multiple_of(order_ref[place] * piece, piece)
        rows = slice(place * piece, (place + 1) * piece)
        padded = slice(8 + place * piece, 8 + (place + 1) * piece)
        for chunk in range(width // LANES):
            column = x_column + chunk * LANES
            x_pad[chunk, padded, :] = narrow_ref[
                pl.ds(start, piece), column : column + LANES
            ].astype(jnp.float32)
        for owner in range(count):
            source = order_ref[pieces + owner]
            owner_start = pl.multiple_of(
                order_ref[pieces + count + owner * pieces + place] * piece, piece
            )
            lane = owner * bc_width % LANES
            bc_pad[owner * bc_width // LANES, padded, lane : lane + bc_width] = bc_ref[
                source, pl.ds(owner_start, piece), :
            ].astype(jnp.float32)
        dt_s[rows, :] = narrow_ref[pl.ds(start, piece), dt_column : dt_column + LANES].astype(
            jnp.float32
        )
    spread = head_spread(width)
    lower = triangle(True)
    rate = jnp.exp(heads_ref[0:1, :])
    bias = heads_ref[1:2, :]

    def one_block(block, carry):
        start = pl.multiple_of(block * BLOCK, BLOCK)
        rows = pl.ds(start, BLOCK)
        step = softplus(dt_s[rows, :] + bias)
        decay_sum = ones_dot(lower, step * rate, 3) + carry
        a_s[rows, :] = decay_sum
        a_row_s[block] = decay_sum.T
        a_wide[rows, :] = dot_ones(decay_sum, spread, 3)
        step_wide = dot_ones(step, spread, 2)
        before = mark_columns(marks_ref, start, 1)
        for column in range(0, width, LANES):
            lanes = slice(column, column + LANES)
            total, _ = conv_window(x_pad, x_taps_ref, before, start, column)
            mixed = total * logistic(total)
            mixed_s[rows, lanes] = mixed
            scaled_s[rows, lanes] = (mixed * step_wide[:, lanes]).astype(jnp.bfloat16)
        for column in range(0, 2 * STATE, LANES):
            total, _ = conv_window(bc_pad, bc_taps_ref, before, start, column)
            bc_s[rows, column : column + LANES] = (total * logistic(total)).astype(
                jnp.bfloat16
            )
        return decay_sum[BLOCK - 1 : BLOCK, :]

    lax.fori_loop(0, length // BLOCK, one_block, jnp.zeros((1, LANES), jnp.float32))


def half_lanes(values, half):
    lane = iota_of(values.shape, 1)
    keep = lane < SSM_DIM if half == 0 else lane >= SSM_DIM
    return jnp.where(keep, values, jnp.zeros_like(values))


def diagonal_decay(a_s, a_row_s, block, start, head):
    gap = a_row_s[block, head : head + 1, :] - a_s[pl.ds(start, BLOCK), head : head + 1]
    return jnp.exp(jnp.minimum(gap, 0.0))


def mixer_forward_kernel(
    x_column,
    order_ref,
    narrow_ref,
    bc_ref,
    marks_ref,
    seg_row_ref,
    x_taps_ref,
    bc_taps_ref,
    heads_ref,
    out_ref,
    x_pad,
    bc_pad,
    dt_s,
    a_s,
    a_row_s,
    a_wide,
    mixed_s,
    scaled_s,
    bc_s,
    weight_s,
    inter_s,
    total_s,
):
    length, width = mixed_s.shape
    piece = length // (2 * bc_ref.shape[0])
    mixer_load(
        x_column,
        order_ref,
        narrow_ref,
        bc_ref,
        marks_ref,
        x_taps_ref,
        bc_taps_ref,
        heads_ref,
        x_pad,
        bc_pad,
        dt_s,
        a_s,
        a_row_s,
        a_wide,
        mixed_s,
        scaled_s,
        bc_s,
    )
    skip_wide = dot_ones(jnp.broadcast_to(heads_ref[2:3, :], (8, LANES)), head_spread(width), 3)

    def one_block(block, _):
        start = pl.multiple_of(block * BLOCK, BLOCK)
        rows = pl.ds(start, BLOCK)
        out_c = bc_s[rows, STATE : 2 * STATE]
        total_s[...] = jnp.zeros_like(total_s)
        first = a_wide[pl.ds(start, 8), :][0:1]

        def earlier(other, _):
            col_start = pl.multiple_of(other * BLOCK, BLOCK)
            columns = pl.ds(col_start, BLOCK)
            allowed = allowed_block(marks_ref, seg_row_ref, start, col_start, BLOCK, False)
            inter = dot_rows(out_c, bc_s[columns, 0:STATE])
            inter = jnp.where(allowed, inter, 0.0).astype(jnp.bfloat16)
            faded = scaled_s[columns, :].astype(jnp.float32) * jnp.exp(a_wide[columns, :] - first)
            total_s[...] += dot_plain(inter, faded.astype(jnp.bfloat16))
            return 0

        lax.fori_loop(0, block, earlier, 0)
        allowed = allowed_block(marks_ref, seg_row_ref, start, start, BLOCK, True)
        inter_s[...] = jnp.where(allowed, dot_rows(out_c, bc_s[rows, 0:STATE]), 0.0)
        for column in range(0, width, LANES):
            lanes = slice(column, column + LANES)
            scaled = scaled_s[rows, lanes]
            mixed = total_s[:, lanes] * jnp.exp(first[:, lanes] - a_wide[rows, lanes])
            for half in range(2):
                head = column // SSM_DIM + half
                decay = diagonal_decay(a_s, a_row_s, block, start, head)
                weights = (inter_s[...] * decay).astype(jnp.bfloat16)
                mixed = mixed + dot_plain(weights, half_lanes(scaled, half))
            mixed = mixed + skip_wide[0:1, lanes] * mixed_s[rows, lanes]
            weight_s[:, lanes] = mixed.astype(jnp.bfloat16)
        for part in range(BLOCK // piece):
            place = block * (BLOCK // piece) + part
            target = pl.multiple_of(order_ref[place] * piece, piece)
            out_ref[pl.ds(target, piece), :] = weight_s[part * piece : (part + 1) * piece, :]
        return 0

    lax.fori_loop(0, length // BLOCK, one_block, 0)


def mixer_backward_kernel(
    x_column,
    order_ref,
    narrow_ref,
    bc_ref,
    grad_ref,
    marks_ref,
    seg_row_ref,
    x_taps_ref,
    bc_taps_ref,
    heads_ref,
    gx_ref,
    gdt_ref,
    gbc_ref,
    gx_taps_ref,
    gbc_taps_ref,
    gheads_ref,
    x_pad,
    bc_pad,
    dt_s,
    a_s,
    a_row_s,
    a_wide,
    mixed_s,
    scaled_s,
    bc_s,
    grad_s,
    gscaled_s,
    gap_s,
    gbc_s,
    inter_s,
    gover_s,
    faded_s,
    gfaded_s,
    fade_s,
    edge_s,
    ahead_s,
    low_s,
):
    length, width = mixed_s.shape
    count, _, bc_width = bc_ref.shape
    pieces = 2 * count
    piece = length // pieces
    blocks = length // BLOCK
    mixer_load(
        x_column,
        order_ref,
        narrow_ref,
        bc_ref,
        marks_ref,
        x_taps_ref,
        bc_taps_ref,
        heads_ref,
        x_pad,
        bc_pad,
        dt_s,
        a_s,
        a_row_s,
        a_wide,
        mixed_s,
        scaled_s,
        bc_s,
    )
    for place in range(pieces):
        source = pl.multiple_of(order_ref[place] * piece, piece)
        grad_s[place * piece : (place + 1) * piece, :] = grad_ref[pl.ds(source, piece), :]
    gscaled_s[...] = jnp.zeros_like(gscaled_s)
    gap_s[...] = jnp.zeros_like(gap_s)
    gbc_s[...] = jnp.zeros_like(gbc_s)

    def one_block(block, _):
        start = pl.multiple_of(block * BLOCK, BLOCK)
        rows = pl.ds(start, BLOCK)
        out_c = bc_s[rows, STATE : 2 * STATE]
        allowed = allowed_block(marks_ref, seg_row_ref, start, start, BLOCK, True)
        inter_s[...] = jnp.where(allowed, dot_rows(out_c, bc_s[rows, 0:STATE]), 0.0)
        gover_s[...] = jnp.zeros_like(gover_s)
        for column in range(0, width, LANES):
            lanes = slice(column, column + LANES)
            scaled = scaled_s[rows, lanes]
            grad = grad_s[rows, lanes]
            row_side = jnp.zeros((BLOCK, LANES), jnp.float32)
            col_side = jnp.zeros((BLOCK, LANES), jnp.float32)
            for half in range(2):
                head = column // SSM_DIM + half
                decay = diagonal_decay(a_s, a_row_s, block, start, head)
                weights = (inter_s[...] * decay).astype(jnp.bfloat16)
                scaled_half = half_lanes(scaled, half)
                gover_s[...] += dot_rows(grad, scaled_half) * decay
                row_side = row_side + dot_plain(weights, scaled_half)
                col_side = col_side + dot_columns(weights, half_lanes(grad, half))
            gscaled_s[rows, lanes] += col_side
            gap_s[rows, lanes] += scaled.astype(jnp.float32) * col_side - grad.astype(
                jnp.float32
            ) * row_side
        gover = jnp.where(allowed, gover_s[...], 0.0).astype(jnp.bfloat16)
        gbc_s[rows, STATE : 2 * STATE] += dot_plain(gover, bc_s[rows, 0:STATE])
        gbc_s[rows, 0:STATE] += dot_columns(gover, out_c)
        first = a_wide[pl.ds(start, 8), :][0:1]
        gfaded_s[...] = (
            grad_s[rows, :].astype(jnp.float32) * jnp.exp(first - a_wide[rows, :])
        ).astype(jnp.bfloat16)

        def earlier(other, _):
            col_start = pl.multiple_of(other * BLOCK, BLOCK)
            columns = pl.ds(col_start, BLOCK)
            same = allowed_block(marks_ref, seg_row_ref, start, col_start, BLOCK, False)
            in_b = bc_s[columns, 0:STATE]
            inter = jnp.where(same, dot_rows(out_c, in_b), 0.0).astype(jnp.bfloat16)
            fade_s[...] = jnp.exp(a_wide[columns, :] - first)
            faded_s[...] = (scaled_s[columns, :].astype(jnp.float32) * fade_s[...]).astype(
                jnp.bfloat16
            )
            over = dot_rows(gfaded_s[...], faded_s[...])
            over = jnp.where(same, over, 0.0).astype(jnp.bfloat16)
            gbc_s[rows, STATE : 2 * STATE] += dot_plain(over, in_b)
            gbc_s[columns, 0:STATE] += dot_columns(over, out_c)
            gap_s[rows, :] -= gfaded_s[...].astype(jnp.float32) * dot_plain(inter, faded_s[...])
            col_side = dot_columns(inter, gfaded_s[...])
            gap_s[columns, :] += faded_s[...].astype(jnp.float32) * col_side
            gscaled_s[columns, :] += fade_s[...] * col_side
            return 0

        lax.fori_loop(0, block, earlier, 0)
        return 0

    lax.fori_loop(0, blocks, one_block, 0)

    spread = head_spread(width)
    gather = head_gather(width)
    upper = triangle(False)
    rate = jnp.exp(heads_ref[0:1, :])
    bias = heads_ref[1:2, :]
    skip_wide = dot_ones(jnp.broadcast_to(heads_ref[2:3, :], (8, LANES)), spread, 3)
    gx_taps_ref[...] = jnp.zeros_like(gx_taps_ref)
    gbc_taps_ref[...] = jnp.zeros_like(gbc_taps_ref)
    gheads_ref[...] = jnp.zeros_like(gheads_ref)
    edge_s[...] = jnp.zeros_like(edge_s)

    def conv_back(pad_ref, taps_ref, gtaps_ref, before, after, start, column, shift, gmixed):
        total, shifted = conv_window(pad_ref, taps_ref, before, start, column)
        sig = logistic(total)
        gtotal = gmixed * sig * (1.0 + total * (1.0 - sig))
        lanes = slice(column, column + LANES)
        for tap in range(4):
            gtaps_ref[tap : tap + 1, lanes] += jnp.sum(gtotal * shifted[tap], axis=0, keepdims=True)
        gtaps_ref[4:5, lanes] += jnp.sum(gtotal, axis=0, keepdims=True)
        wide = slice(shift + column, shift + column + LANES)
        chunk = (shift + column) // LANES
        ahead_s[chunk, 0:BLOCK, :] = gtotal
        ahead_s[chunk, BLOCK : BLOCK + 8, :] = edge_s[:, wide]
        edge_s[:, wide] = gtotal[0:8]
        result = gtotal * taps_ref[3:4, lanes]
        for tap in range(3):
            ahead = ahead_s[chunk, 3 - tap : 3 - tap + BLOCK, :] * after[tap]
            result = result + ahead * taps_ref[tap : tap + 1, lanes]
        return result.astype(jnp.bfloat16)

    def last_block(index, carry):
        block = blocks - 1 - index
        start = pl.multiple_of(block * BLOCK, BLOCK)
        rows = pl.ds(start, BLOCK)
        raw = dt_s[rows, :] + bias
        step = softplus(raw)
        gsum = ones_dot(upper, dot_ones(gap_s[rows, :], gather, 2), 3) + carry
        gstep = dot_ones(gscaled_s[rows, :] * mixed_s[rows, :], gather, 2) + gsum * rate
        graw = gstep * jax.nn.sigmoid(raw)
        gheads_ref[0:1, :] += jnp.sum(gsum * step * rate, axis=0, keepdims=True)
        gheads_ref[1:2, :] += jnp.sum(graw, axis=0, keepdims=True)
        low_s[:, width : width + LANES] = graw.astype(jnp.bfloat16)
        step_wide = dot_ones(step, spread, 2)
        skip_parts = []
        before = mark_columns(marks_ref, start, 1)
        after = mark_columns(marks_ref, start, 4)
        for column in range(0, width, LANES):
            lanes = slice(column, column + LANES)
            grad = grad_s[rows, lanes].astype(jnp.float32)
            skip_parts.append(jnp.sum(grad * mixed_s[rows, lanes], axis=0, keepdims=True))
            gmixed = skip_wide[0:1, lanes] * grad + gscaled_s[rows, lanes] * step_wide[:, lanes]
            low_s[:, lanes] = conv_back(
                x_pad, x_taps_ref, gx_taps_ref, before, after, start, column, 0, gmixed
            )
        skip_row = jnp.broadcast_to(jnp.concatenate(skip_parts, axis=1), (8, width))
        gheads_ref[2:3, :] += dot_ones(skip_row, gather, 2)[0:1]
        for column in range(0, 2 * STATE, LANES):
            lanes = slice(column, column + LANES)
            low_s[:, width + LANES + column : width + 2 * LANES + column] = conv_back(
                bc_pad,
                bc_taps_ref,
                gbc_taps_ref,
                before,
                after,
                start,
                column,
                width,
                gbc_s[rows, lanes],
            )
        for part in range(BLOCK // piece):
            place = block * (BLOCK // piece) + part
            target = pl.multiple_of(order_ref[place] * piece, piece)
            gx_ref[pl.ds(target, piece), :] = low_s[part * piece : (part + 1) * piece, 0:width]
            gdt_ref[pl.ds(target, piece), :] = low_s[
                part * piece : (part + 1) * piece, width : width + LANES
            ]
            for owner in range(count):
                first = width + LANES + owner * bc_width
                owner_start = pl.multiple_of(
                    order_ref[pieces + count + owner * pieces + place] * piece, piece
                )
                gbc_ref[order_ref[pieces + owner], pl.ds(owner_start, piece), :] = low_s[
                    part * piece : (part + 1) * piece, first : first + bc_width
                ]
        return gsum[0:1, :]

    lax.fori_loop(0, blocks, last_block, jnp.zeros((1, LANES), jnp.float32))


def local_call(kernel, outs, scratch, flops, operands):
    moved = sum(part.size * part.dtype.itemsize for part in operands)
    moved += sum(part.size * part.dtype.itemsize for part in outs)
    return pl.pallas_call(
        kernel,
        out_shape=outs,
        in_specs=[pl.BlockSpec(memory_space=pltpu.SMEM)]
        + [pl.BlockSpec(memory_space=pltpu.VMEM)] * (len(operands) - 1),
        out_specs=[pl.BlockSpec(memory_space=pltpu.VMEM)] * len(outs),
        scratch_shapes=scratch,
        compiler_params=pltpu.CompilerParams(vmem_limit_bytes=KERNEL_VMEM),
        cost_estimate=pl.CostEstimate(flops=flops, bytes_accessed=moved, transcendentals=0),
    )(*operands)


def array_of(shape, dtype):
    return jax.ShapeDtypeStruct(shape, dtype)


def attention_forward(q_width, pieces, order, narrow, cosine, sine, marks, seg_row):
    length = narrow.shape[0]
    low = jnp.bfloat16
    return local_call(
        functools.partial(attention_forward_kernel, q_width, pieces),
        [array_of((length, q_width), low), array_of((length, 8), jnp.float32)],
        [
            pltpu.VMEM((length, q_width), low),
            pltpu.VMEM((length, HEAD_DIM), low),
            pltpu.VMEM((length, HEAD_DIM), low),
        ],
        3 * length * length * q_width,
        (order, narrow, cosine, sine, marks, seg_row),
    )


def attention_backward(q_width, pieces, order, narrow, grad, cosine, sine, marks, seg_row, lse):
    length = narrow.shape[0]
    low = jnp.bfloat16
    return local_call(
        functools.partial(attention_backward_kernel, q_width, pieces),
        [array_of((length, q_width + 2 * HEAD_DIM), low)],
        [
            pltpu.VMEM((length, q_width), low),
            pltpu.VMEM((length, HEAD_DIM), low),
            pltpu.VMEM((length, HEAD_DIM), low),
            pltpu.VMEM((length, q_width), low),
            pltpu.VMEM((length, HEAD_DIM), jnp.float32),
            pltpu.VMEM((length, HEAD_DIM), jnp.float32),
        ],
        6 * length * length * q_width,
        (order, narrow, grad, cosine, sine, marks, seg_row, lse),
    )[0]


def mixer_scratch(length, width):
    low, full = jnp.bfloat16, jnp.float32
    return [
        pltpu.VMEM((width // LANES, length + 8, LANES), full),
        pltpu.VMEM((2 * STATE // LANES, length + 8, LANES), full),
        pltpu.VMEM((length, LANES), full),
        pltpu.VMEM((length, LANES), full),
        pltpu.VMEM((length // BLOCK, LANES, BLOCK), full),
        pltpu.VMEM((length, width), full),
        pltpu.VMEM((length, width), full),
        pltpu.VMEM((length, width), low),
        pltpu.VMEM((length, 2 * STATE), low),
    ]


def mixer_forward(x_column, width, order, narrow, bc, marks, seg_row, x_taps, bc_taps, heads):
    length = narrow.shape[0]
    low, full = jnp.bfloat16, jnp.float32
    return local_call(
        functools.partial(mixer_forward_kernel, x_column),
        [array_of((length, width), low)],
        mixer_scratch(length, width)
        + [
            pltpu.VMEM((BLOCK, width), low),
            pltpu.VMEM((BLOCK, BLOCK), full),
            pltpu.VMEM((BLOCK, width), full),
        ],
        4 * length * length * width,
        (order, narrow, bc, marks, seg_row, x_taps, bc_taps, heads),
    )[0]


def mixer_backward(x_column, width, order, narrow, bc, grad, marks, seg_row, x_taps, bc_taps, heads):
    length = narrow.shape[0]
    low, full = jnp.bfloat16, jnp.float32
    return local_call(
        functools.partial(mixer_backward_kernel, x_column),
        [
            array_of((length, width), low),
            array_of((length, LANES), low),
            array_of(bc.shape, low),
            array_of((8, width), full),
            array_of((8, 2 * STATE), full),
            array_of((8, LANES), full),
        ],
        mixer_scratch(length, width)
        + [
            pltpu.VMEM((length, width), low),
            pltpu.VMEM((length, width), full),
            pltpu.VMEM((length, width), full),
            pltpu.VMEM((length, 2 * STATE), full),
            pltpu.VMEM((BLOCK, BLOCK), full),
            pltpu.VMEM((BLOCK, BLOCK), full),
            pltpu.VMEM((BLOCK, width), low),
            pltpu.VMEM((BLOCK, width), low),
            pltpu.VMEM((BLOCK, width), full),
            pltpu.VMEM((8, width + 2 * STATE), full),
            pltpu.VMEM(((width + 2 * STATE) // LANES, BLOCK + 8, LANES), full),
            pltpu.VMEM((BLOCK, width + LANES + 2 * STATE), low),
        ],
        10 * length * length * width,
        (order, narrow, bc, grad, marks, seg_row, x_taps, bc_taps, heads),
    )


def document_marks(seg_row):
    length = seg_row.shape[0]
    before = jnp.pad(seg_row, (3, 0), constant_values=-1)
    after = jnp.pad(seg_row, (0, 3), constant_values=-1)
    columns = [seg_row.astype(jnp.float32)]
    for tap in range(3):
        columns.append((before[tap : tap + length] == seg_row).astype(jnp.float32))
    for tap in range(3):
        columns.append((after[3 - tap : 3 - tap + length] == seg_row).astype(jnp.float32))
    columns.append(jnp.zeros((length,), jnp.float32))
    return jnp.stack(columns, axis=1)


def rope_wide(length):
    half_dim = HEAD_DIM // 2
    frequency = rope_base ** (-jnp.arange(half_dim, dtype=jnp.float32) / half_dim)
    angles = jnp.arange(length, dtype=jnp.float32)[:, None] * frequency[None, :]
    cosine, sine = jnp.cos(angles), jnp.sin(angles)
    return jnp.concatenate([cosine, cosine], axis=1), jnp.concatenate([-sine, sine], axis=1)


def swap_seq(value, bit, count):
    return lax.ppermute(value, "seq", [(place, place ^ bit) for place in range(count)])


def seq_bits(count):
    bits = []
    bit = 1
    while bit < count:
        bits.append(bit)
        bit *= 2
    return bits


def block_order(bits):
    order = [0]
    for bit in bits:
        order = order + [place ^ bit for place in order]
    return order


def relative_order(count):
    bits = seq_bits(count)
    upper = [(0, block) for block in block_order(bits)]
    lower = [(1, block) for block in block_order(bits[::-1])]
    near = count // 2
    return upper[:near] + lower[:near] + upper[near:] + lower[near:]


def gather_first(rows, count):
    half = rows.shape[0] // 2
    bits = seq_bits(count)
    pieces = []
    for piece, order in ((rows[:half], bits), (rows[half:], bits[::-1])):
        for bit in order[:-1]:
            piece = jnp.concatenate([piece, swap_seq(piece, bit, count)], axis=0)
        pieces.append(piece)
    return pieces


def gather_last(pieces, count):
    bits = seq_bits(count)
    far = [swap_seq(piece, bit, count) for piece, bit in zip(pieces, (bits[-1], bits[0]))]
    return jnp.concatenate(pieces, axis=0), jnp.concatenate(far, axis=0)


def rows_gather(rows, count):
    return gather_last(gather_first(rows, count), count)


def scatter_first(far, count):
    half = far.shape[0] // 2
    bits = seq_bits(count)
    far = far.astype(jnp.bfloat16)
    return [
        swap_seq(far[first : first + half], order[-1], count)
        for first, order in ((0, bits), (half, bits[::-1]))
    ]


def scatter_second(near, came, count):
    half = near.shape[0] // 2
    bits = seq_bits(count)
    kept, arrived = [], []
    for first, order, add in ((0, bits, came[0]), (half, bits[::-1], came[1])):
        piece = near[first : first + half]
        for bit in order[:-1][::-1]:
            piece = piece + add.astype(jnp.float32)
            keep = piece.shape[0] // 2
            add = swap_seq(piece[keep:].astype(jnp.bfloat16), bit, count)
            piece = piece[:keep]
        kept.append(piece)
        arrived.append(add)
    return kept, arrived


def scatter_last(kept, arrived):
    return jnp.concatenate(
        [piece + add.astype(jnp.float32) for piece, add in zip(kept, arrived)], axis=0
    )


def rows_scatter(near, far, count):
    came = scatter_first(far, count)
    return scatter_last(*scatter_second(near, came, count))


def true_rows(rank, count):
    order = relative_order(count)
    blocks = jnp.arange(count, dtype=jnp.int32) ^ rank
    tables = [
        jnp.asarray([order.index((half, block)) for block in range(count)], jnp.int32)[blocks]
        for half in range(2)
    ]
    return jnp.stack(tables, axis=1).reshape(-1)


def seq_pieces(value, count):
    return [value] + [swap_seq(value, bit, count) for bit in range(1, count)]


def seq_sum(value, count):
    order = relative_order(count)
    total = value.reshape(2 * count, -1)
    for bit in range(1, count):
        came = swap_seq(value, bit, count).reshape(2 * count, -1)
        places = [order.index((half, block ^ bit)) for half, block in order]
        total = total + jnp.concatenate([came[place : place + 1] for place in places])
    return total.reshape(-1)


def norm_forward(rows, gain):
    scale = lax.rsqrt(jnp.mean(rows * rows, axis=-1, keepdims=True) + epsilon)
    return ((rows * scale * gain).astype(jnp.bfloat16), scale)


def norm_backward(rows, scale, gain, cotangent):
    weighted = cotangent * gain
    inner = jnp.mean(rows * weighted, axis=-1, keepdims=True)
    grad_rows = scale * weighted - rows * (scale * scale * scale * inner)
    return grad_rows


def columns_exchange(blocks):
    return lax.all_to_all(blocks, "seq", split_axis=0, concat_axis=0, tiled=True)


def rows_of_all(piece):
    return lax.all_gather(piece, "fsdp", axis=1, tiled=True).reshape(-1, piece.shape[2])


def columns_gather(blocks):
    return rows_of_all(columns_exchange(blocks))


def columns_to_owners(blocks):
    blocks = with_layout_constraint(blocks, Layout(major_to_minor=(0, 1, 2)))
    return lax.all_to_all(blocks, "seq", split_axis=0, concat_axis=0, tiled=True)


def rank_parts(arrived):
    return [arrived[place].astype(jnp.float32) for place in range(arrived.shape[0])]


def side_by_side(parts, first, width):
    return jnp.concatenate([part[:, first : first + width] for part in parts], axis=1)


def body(
    seq_count,
    fsdp_count,
    hidden_in,
    segments,
    out_grad,
    norm1_gain,
    w_query,
    w_keyval,
    w_attn_out,
    w_gate_z,
    w_ssm_x,
    w_ssm_bc,
    w_ssm_dt,
    conv_taps,
    a_log,
    dt_bias,
    skip_gain,
    ssm_gain,
    w_ssm_out,
    norm2_gain,
    w_ff_gate,
    w_ff_up,
    w_ff_down,
):
    f32, bf16 = jnp.float32, jnp.bfloat16
    batch, block_len, model_width = hidden_in.shape
    length = block_len * seq_count
    rank = lax.axis_index("seq")
    seg_row = segments[0]
    heads_local = HEADS // seq_count
    group_size = HEADS // KV_HEADS
    q_width = w_query.shape[1] // seq_count
    z_width = w_gate_z.shape[1] // seq_count
    x_width = w_ssm_x.shape[1] // seq_count
    bc_width = w_ssm_bc.shape[1] // seq_count
    dt_width = w_ssm_dt.shape[1] // seq_count
    ff_width = w_ff_gate.shape[1] // seq_count
    kv_total = w_keyval.shape[1] // 2
    heads_total = a_log.shape[0]
    dssm = w_ssm_x.shape[1]
    row_piece = w_query.shape[0]
    bc_pad = -bc_width % LANES
    dt_pad = -dt_width % LANES

    def pack(vector):
        parts = -(-vector.shape[0] // row_piece)
        padded = jnp.pad(vector, (0, parts * row_piece - vector.shape[0]))
        return [padded[part * row_piece : (part + 1) * row_piece] for part in range(parts)]

    def unpack(columns, length_each):
        spread = columns.reshape(columns.shape[0], -1, row_piece).transpose(1, 0, 2)
        return spread.reshape(spread.shape[0], -1)[:, :length_each].reshape(-1)

    extra_columns = [norm1_gain, norm2_gain] + pack(ssm_gain)
    ssm_pieces = len(extra_columns) - 2
    for tap in range(conv_taps.shape[1]):
        extra_columns += pack(conv_taps[:, tap])
    taps_pieces = (len(extra_columns) - 2 - ssm_pieces) // conv_taps.shape[1]
    extra_block = jnp.pad(
        jnp.stack(extra_columns, axis=1), ((0, 0), (0, dt_pad - len(extra_columns)))
    )
    free_first = q_width + 2 * HEAD_DIM + x_width + bc_width + bc_pad + dt_width
    sends = []
    for target in range(seq_count):
        kv_head = target * heads_local // group_size
        sends.append(
            jnp.concatenate(
                [
                    w_query[:, target * q_width : (target + 1) * q_width],
                    w_keyval[:, kv_head * HEAD_DIM : (kv_head + 1) * HEAD_DIM],
                    w_keyval[:, kv_total + kv_head * HEAD_DIM : kv_total + (kv_head + 1) * HEAD_DIM],
                    w_ssm_x[:, target * x_width : (target + 1) * x_width],
                    w_ssm_bc[:, target * bc_width : (target + 1) * bc_width],
                    jnp.zeros((row_piece, bc_pad), bf16),
                    w_ssm_dt[:, target * dt_width : (target + 1) * dt_width],
                    extra_block,
                ],
                axis=1,
            )
        )
    narrow_piece = columns_exchange(jnp.stack(sends))
    narrow_w = rows_of_all(narrow_piece)
    extras = lax.slice_in_dim(narrow_w, free_first, free_first + len(extra_columns), axis=1).T
    extras = extras.astype(f32)
    gain1, gain2 = extras[0], extras[1]
    taps_rows, taps_width = conv_taps.shape
    ssm_count = ssm_gain.shape[0]
    gain_ssm = unpack(extras[2 : 2 + ssm_pieces], ssm_count)
    gain_ssm = lax.dynamic_slice_in_dim(gain_ssm, rank * z_width, z_width, 0)
    taps = [
        unpack(extras[first : first + taps_pieces], taps_rows)
        for first in range(2 + ssm_pieces, len(extra_columns), taps_pieces)
    ]
    taps_rows8 = jnp.pad(jnp.stack(taps), ((0, 8 - taps_width), (0, 0)))
    x_taps = lax.dynamic_slice_in_dim(taps_rows8, rank * x_width, x_width, 1)
    bc_taps = taps_rows8[:, dssm:]
    head_rows = lax.dynamic_slice_in_dim(
        jnp.stack([a_log, dt_bias, skip_gain]), rank * dt_width, dt_width, 1
    )
    head_rows = jnp.pad(head_rows, ((0, 5), (0, dt_pad)))
    marks = document_marks(seg_row)
    seg_line = jnp.broadcast_to(seg_row.astype(f32)[None, :], (8, length))

    to_true = true_rows(rank, seq_count)
    ranks = jnp.arange(seq_count, dtype=jnp.int32)
    to_true = jnp.concatenate(
        [to_true, ranks ^ rank] + [true_rows(other, seq_count) for other in range(seq_count)]
    )
    pieces = 2 * seq_count

    narrow_piece, w_gate_z, w_ff_gate, w_ff_up, w_attn_out, w_ssm_out = (
        lax.optimization_barrier(
            (narrow_piece, w_gate_z, w_ff_gate, w_ff_up, w_attn_out, w_ssm_out)
        )
    )
    wide_piece = columns_exchange(
        jnp.stack(
            [
                jnp.concatenate(
                    [
                        w_gate_z[:, target * z_width : (target + 1) * z_width],
                        w_ff_gate[:, target * ff_width : (target + 1) * ff_width],
                        w_ff_up[:, target * ff_width : (target + 1) * ff_width],
                    ],
                    axis=1,
                )
                for target in range(seq_count)
            ]
        )
    )
    z_piece, ff_piece = wide_piece[:, :, :z_width], wide_piece[:, :, z_width:]
    z_w = rows_of_all(z_piece)
    out_piece = jnp.concatenate([w_attn_out, w_ssm_out], axis=0)
    z_piece, out_piece = lax.optimization_barrier((z_piece, out_piece))
    out_w = lax.all_gather(out_piece, "fsdp", axis=0)

    own_in = hidden_in.reshape(block_len, model_width)
    all_in = jnp.concatenate(rows_gather(own_in, seq_count), axis=0)
    cosine, sine = rope_wide(length)
    all_in, ff_piece, cosine, sine, marks, seg_line, to_true, out_grad = (
        lax.optimization_barrier(
            (all_in, ff_piece, cosine, sine, marks, seg_line, to_true, out_grad)
        )
    )
    grad_own = out_grad.reshape(block_len, model_width)
    grad_ff = gather_first(grad_own, seq_count)
    ff_w = rows_of_all(ff_piece)
    normed, _ = norm_forward(all_in.astype(f32), gain1)
    edges = [0]
    for width in (q_width, HEAD_DIM, HEAD_DIM, x_width, bc_width + bc_pad, dt_width + dt_pad):
        edges.append(edges[-1] + width)
    narrow = mat_product(normed, narrow_w).astype(bf16)
    bc_seq = jnp.stack(seq_pieces(narrow[:, edges[4] : edges[4] + bc_width], seq_count))
    attn_rel, lse_seq = attention_forward(
        q_width, pieces, to_true, narrow, cosine, sine, marks, seg_line
    )
    bc_seq, attn_rel, w_ff_down, grad_ff = lax.optimization_barrier(
        (bc_seq, attn_rel, w_ff_down, grad_ff)
    )
    grad_ff = gather_last(grad_ff, seq_count)
    down_w = lax.all_gather(w_ff_down, "fsdp", axis=0, tiled=True)
    mixer_args = (x_taps, bc_taps, head_rows)
    ssm_rel = mixer_forward(
        edges[3], x_width, to_true, narrow, bc_seq, marks, seg_line, *mixer_args
    )
    ssm_rel, z_w, grad_ff = lax.optimization_barrier((ssm_rel, z_w, grad_ff))
    ssm_rel = ssm_rel.astype(f32)
    attn_out_w = out_w[:, : w_attn_out.shape[0]].reshape(-1, model_width)
    ssm_out_w = out_w[:, w_attn_out.shape[0] :].reshape(-1, model_width)
    gate_z = mat_product(normed, z_w)
    gate_sig = jax.nn.sigmoid(gate_z)
    gate_silu = gate_z * gate_sig
    gated = ssm_rel * gate_silu
    gated, out_w = lax.optimization_barrier((gated, out_w))
    square_sum = seq_sum(jnp.sum(gated * gated, axis=1), seq_count)
    gated_scale = lax.rsqrt(square_sum / dssm + epsilon)[:, None]
    ssm_in = (gated * gated_scale * gain_ssm).astype(bf16)
    near = length // 2

    def out_product(first):
        rows = slice(first, first + near)
        return mat_product(attn_rel[rows], attn_out_w) + mat_product(ssm_in[rows], ssm_out_w)

    xin = own_in.astype(f32)
    middle = xin + rows_scatter(out_product(0), out_product(near), seq_count)

    own_normed2, scale2 = norm_forward(middle, gain2)
    normed2 = rows_gather(own_normed2, seq_count)

    def ff_forward(rows):
        gate_ff = mat_product(rows, ff_w[:, :ff_width])
        up_ff = mat_product(rows, ff_w[:, ff_width:])
        ff_sig = jax.nn.sigmoid(gate_ff)
        ff_silu = gate_ff * ff_sig
        return up_ff, ff_sig, ff_silu, (ff_silu * up_ff).astype(bf16), gate_ff

    def ff_backward(grad_rows, up_ff, ff_sig, ff_silu):
        grad_act = input_grad(grad_rows, down_w)
        grad_gate_ff = grad_act * up_ff * (ff_sig + ff_silu * (1.0 - ff_sig))
        grad_up_ff = grad_act * ff_silu
        return jnp.concatenate([grad_gate_ff.astype(bf16), grad_up_ff.astype(bf16)], axis=1)

    up_near, sig_near, silu_near, act_near, gate_near = ff_forward(normed2[0])
    normed2_far, act_near, up_near, gate_near = lax.optimization_barrier(
        (normed2[1], act_near, up_near, gate_near)
    )
    sig_near = jax.nn.sigmoid(gate_near)
    silu_near = gate_near * sig_near
    up_far, sig_far, silu_far, act_far, gate_far = ff_forward(normed2_far)
    act = jnp.concatenate([act_near, act_far], axis=0)
    grad_ff_all = jnp.concatenate(grad_ff, axis=0)
    normed2_all = jnp.concatenate([normed2[0], normed2_far], axis=0)
    act, grad_ff_all = lax.optimization_barrier((act, grad_ff_all))
    grad_w_down = weight_grad(act, grad_ff_all).astype(bf16)
    grad_ff_far, grad_w_down = lax.optimization_barrier((grad_ff[1], grad_w_down))
    grad_w_down = lax.psum_scatter(grad_w_down, "fsdp", scatter_dimension=0, tiled=True)
    pair_far = ff_backward(grad_ff_far, up_far, sig_far, silu_far)
    pair_far = lax.optimization_barrier(pair_far)
    normed2_grad_far = input_grad(pair_far, ff_w).astype(bf16)
    grad_ff_near, normed2_grad_far = lax.optimization_barrier((grad_ff[0], normed2_grad_far))
    pair_near = ff_backward(grad_ff_near, up_near, sig_near, silu_near)
    pair_near = lax.optimization_barrier(pair_near)
    normed2_grad_near = input_grad(pair_near, ff_w)
    grad_pair = jnp.concatenate([pair_near, pair_far], axis=0)
    grad_pair, normed2_all = lax.optimization_barrier((grad_pair, normed2_all))
    grad_w_ff = weight_grad(normed2_all, grad_pair).astype(bf16)
    grad_w_ff = lax.psum_scatter(
        grad_w_ff.reshape(seq_count, -1, 2 * ff_width), "fsdp", scatter_dimension=1, tiled=True
    )
    grad_normed2 = rows_scatter(normed2_grad_near, normed2_grad_far, seq_count)
    grad_normed2, grad_w_down = lax.optimization_barrier((grad_normed2, grad_w_down))
    grad_middle_norm = norm_backward(middle, scale2, gain2, grad_normed2)
    grad_middle = grad_own.astype(f32) + grad_middle_norm

    mix_near, mix_far = rows_gather(grad_middle.astype(bf16), seq_count)
    ff_near = mat_product(act[:near], down_w)
    ff_far = mat_product(act[near:], down_w).astype(bf16)
    mix_far, ff_near, ff_far = lax.optimization_barrier((mix_far, ff_near, ff_far))
    grad_mix = jnp.concatenate([mix_near, mix_far], axis=0)
    grad_attn = input_grad(grad_mix, attn_out_w).astype(bf16)
    grad_ssm_in = input_grad(grad_mix, ssm_out_w)
    grad_w_attn = weight_grad(attn_rel, grad_mix).astype(bf16)
    grad_w_ssm = weight_grad(ssm_in, grad_mix).astype(bf16)
    weighted = grad_ssm_in * gain_ssm
    inner = seq_sum(jnp.sum(gated * weighted, axis=1), seq_count)
    out_grads = jnp.concatenate(
        [
            grad_w_attn.reshape(fsdp_count, -1, model_width),
            grad_w_ssm.reshape(fsdp_count, -1, model_width),
        ],
        axis=1,
    )
    grad_qkv = attention_backward(
        q_width, pieces, to_true, narrow, grad_attn, cosine, sine, marks, seg_line, lse_seq
    )
    inner, out_grads = lax.optimization_barrier((inner, out_grads))
    out_grads = lax.psum_scatter(out_grads, "fsdp", scatter_dimension=0, tiled=True)[0]
    inner = inner[:, None] / dssm
    grad_gated = gated_scale * weighted - gated * (
        gated_scale * gated_scale * gated_scale * inner
    )
    grad_ssm = (grad_gated * gate_silu).astype(bf16)
    grad_z = (grad_gated * ssm_rel * (gate_sig + gate_silu * (1.0 - gate_sig))).astype(bf16)
    grad_zq = lax.optimization_barrier(jnp.concatenate([grad_z, grad_qkv], axis=1))
    grad_w_zq = weight_grad(normed, grad_zq).astype(bf16)
    grad_ssm, grad_w_zq, ff_far, grad_w_ff = lax.optimization_barrier(
        (grad_ssm, grad_w_zq, ff_far, grad_w_ff)
    )
    grad_w_zq = lax.psum_scatter(
        grad_w_zq.reshape(seq_count, -1, grad_zq.shape[1]),
        "fsdp",
        scatter_dimension=1,
        tiled=True,
    )
    ff_came = scatter_first(ff_far, seq_count)
    grad_x, grad_dt, grad_bc_part, grad_x_taps, grad_bc_taps, grad_heads = mixer_backward(
        edges[3], x_width, to_true, narrow, bc_seq, grad_ssm, marks, seg_line, *mixer_args
    )
    grad_w_ff, grad_bc_part = lax.optimization_barrier((grad_w_ff, grad_bc_part))
    ff_cols = columns_to_owners(grad_w_ff)
    grad_bc = grad_bc_part[0].astype(f32)
    for bit in range(1, seq_count):
        grad_bc = grad_bc + swap_seq(grad_bc_part[bit], bit, seq_count).astype(f32)
    grad_bc = grad_bc.astype(bf16)
    ff_near, grad_bc = lax.optimization_barrier((ff_near, grad_bc))
    ff_kept, ff_arrived = scatter_second(ff_near, ff_came, seq_count)
    bc_zeros = jnp.zeros((length, bc_pad), bf16)
    grad_rest = jnp.concatenate([grad_x, grad_bc, bc_zeros, grad_dt], axis=1)
    grad_rest, out_grads, ff_cols = lax.optimization_barrier((grad_rest, out_grads, ff_cols))
    per_device = (seq_count, fsdp_count, -1)
    x_conv = lax.dynamic_update_slice_in_dim(
        jnp.zeros((dssm, taps_width), f32), grad_x_taps[:taps_width].T, rank * x_width, 0
    )
    conv_grads = jnp.concatenate([x_conv, grad_bc_taps[:taps_width].T], axis=0).reshape(per_device)
    head_grads = lax.dynamic_update_slice(
        jnp.zeros((3, heads_total), f32),
        grad_heads[:3, :dt_width],
        (jnp.int32(0), rank * dt_width),
    )
    head_grads = jnp.broadcast_to(
        head_grads.reshape(1, 1, -1), (seq_count, fsdp_count, 3 * heads_total)
    )
    smalls = jnp.concatenate([conv_grads, head_grads], axis=2)
    small_count = smalls.shape[2]
    small_columns = -(-small_count // row_piece)
    smalls = jnp.pad(smalls, ((0, 0), (0, 0), (0, small_columns * row_piece - small_count)))
    smalls = smalls.reshape(model_width, small_columns)
    small_first = x_width + bc_width + bc_pad + dt_width
    small_room = grad_rest.shape[1] - small_first - small_columns
    smalls = jnp.pad(smalls, ((0, 0), (small_first, small_room)))
    grad_w_rest = (weight_grad(normed, grad_rest) + smalls).astype(bf16)
    grad_rest, grad_w_rest, grad_z, grad_qkv = lax.optimization_barrier(
        (grad_rest, grad_w_rest, grad_z, grad_qkv)
    )
    grad_w_rest = lax.psum_scatter(
        grad_w_rest.reshape(seq_count, -1, grad_rest.shape[1]),
        "fsdp",
        scatter_dimension=1,
        tiled=True,
    )

    def first_product(first):
        rows = slice(first, first + near)
        return (
            input_grad(grad_rest[rows], narrow_w[:, edges[3] :])
            + input_grad(grad_z[rows], z_w)
            + input_grad(grad_qkv[rows], narrow_w[:, : edges[3]])
        )

    grad_normed_far = first_product(near).astype(bf16)
    ff_kept, grad_normed_far = lax.optimization_barrier((ff_kept, grad_normed_far))
    layer_out = middle + scatter_last(ff_kept, ff_arrived)
    normed_came = scatter_first(grad_normed_far, seq_count)
    zq_cols = columns_to_owners(grad_w_zq)
    grad_normed_near, zq_cols = lax.optimization_barrier((first_product(0), zq_cols))
    normed_kept, normed_arrived = scatter_second(grad_normed_near, normed_came, seq_count)
    normed_kept, grad_w_rest = lax.optimization_barrier((normed_kept, grad_w_rest))
    grad_normed = scatter_last(normed_kept, normed_arrived)
    _, scale1 = norm_forward(xin, gain1)
    grad_in_norm = norm_backward(xin, scale1, gain1, grad_normed)
    grad_in = grad_middle + grad_in_norm

    ff_cols = rank_parts(ff_cols)
    zq_cols = rank_parts(zq_cols)
    rest_cols = rank_parts(columns_to_owners(grad_w_rest))
    bc_first = x_width
    dt_first = bc_first + bc_width + bc_pad
    small = sum(part[:, small_first : small_first + small_columns] for part in rest_cols)
    small = small.reshape(-1)[:small_count]
    taps_total = taps_rows * taps_width
    out_conv = small[:taps_total]
    out_heads = small[taps_total:].reshape(3, heads_total)
    ranks_per_kv = group_size // heads_local
    kv_cols = []
    for first in (z_width + edges[1], z_width + edges[2]):
        for head in range(KV_HEADS):
            shares = zq_cols[head * ranks_per_kv : (head + 1) * ranks_per_kv]
            kv_cols.append(sum(share[:, first : first + HEAD_DIM] for share in shares))
    attn_rows = w_attn_out.shape[0]
    grad_query = side_by_side(zq_cols, z_width, q_width)
    grad_keyval = jnp.concatenate(kv_cols, axis=1)
    grad_gate_z = side_by_side(zq_cols, 0, z_width)
    grad_ssm_x = side_by_side(rest_cols, 0, x_width)
    grad_ssm_bc = side_by_side(rest_cols, bc_first, bc_width)
    grad_ssm_dt = side_by_side(rest_cols, dt_first, dt_width)
    grad_ff_gate = side_by_side(ff_cols, 0, ff_width)
    grad_ff_up = side_by_side(ff_cols, ff_width, ff_width)
    grad_attn_out = out_grads[:attn_rows].astype(f32)
    grad_ssm_out = out_grads[attn_rows:].astype(f32)

    def gain_grad(gain, *pairs):
        total = sum(jnp.sum(weight.astype(f32) * grad, axis=1) for weight, grad in pairs)
        return total / gain.astype(f32)

    out_gain1 = gain_grad(
        norm1_gain,
        (w_query, grad_query),
        (w_keyval, grad_keyval),
        (w_gate_z, grad_gate_z),
        (w_ssm_x, grad_ssm_x),
        (w_ssm_bc, grad_ssm_bc),
        (w_ssm_dt, grad_ssm_dt),
    )
    out_gain2 = gain_grad(norm2_gain, (w_ff_gate, grad_ff_gate), (w_ff_up, grad_ff_up))
    out_ssm_gain = gain_grad(ssm_gain, (w_ssm_out, grad_ssm_out))
    return (
        layer_out.astype(bf16).reshape(batch, block_len, model_width),
        grad_in.astype(bf16).reshape(batch, block_len, model_width),
        out_gain1,
        grad_query,
        grad_keyval,
        grad_attn_out,
        grad_gate_z,
        grad_ssm_x,
        grad_ssm_bc,
        grad_ssm_dt,
        out_conv.reshape(taps_rows, taps_width),
        out_heads[0],
        out_heads[1],
        out_heads[2],
        out_ssm_gain,
        grad_ssm_out,
        out_gain2,
        grad_ff_gate,
        grad_ff_up,
        grad_w_down.astype(f32),
    )


def solution(mesh):
    in_specs = (
        P("fsdp", "seq", None),
        P("fsdp", None),
        P("fsdp", "seq", None),
        P(("seq", "fsdp")),
        P(("seq", "fsdp"), None),
        P(("seq", "fsdp"), None),
        P(("seq", "fsdp"), None),
        P(("seq", "fsdp"), None),
        P(("seq", "fsdp"), None),
        P(("seq", "fsdp"), None),
        P(("seq", "fsdp"), None),
        P(("seq", "fsdp"), None),
        P(),
        P(),
        P(),
        P(("seq", "fsdp")),
        P(("seq", "fsdp"), None),
        P(("seq", "fsdp")),
        P(("seq", "fsdp"), None),
        P(("seq", "fsdp"), None),
        P(("seq", "fsdp"), None),
    )
    out_specs = (
        P("fsdp", "seq", None),
        P("fsdp", "seq", None),
        P(("seq", "fsdp")),
        P(("seq", "fsdp"), None),
        P(("seq", "fsdp"), None),
        P(("seq", "fsdp"), None),
        P(("seq", "fsdp"), None),
        P(("seq", "fsdp"), None),
        P(("seq", "fsdp"), None),
        P(("seq", "fsdp"), None),
        P(("seq", "fsdp"), None),
        P(),
        P(),
        P(),
        P(("seq", "fsdp")),
        P(("seq", "fsdp"), None),
        P(("seq", "fsdp")),
        P(("seq", "fsdp"), None),
        P(("seq", "fsdp"), None),
        P(("seq", "fsdp"), None),
    )
    step = functools.partial(body, mesh.shape["seq"], mesh.shape["fsdp"])
    return jax.shard_map(step, mesh=mesh, in_specs=in_specs, out_specs=out_specs, check_vma=False)
```

```python
import functools

import jax
import jax.numpy as jnp
import numpy as np
from jax import lax
from jax.experimental import pallas as pl
from jax.experimental.layout import Layout, with_layout_constraint
from jax.experimental.pallas import tpu as pltpu
from jax.sharding import PartitionSpec as P

HEADS = 8
KV_HEADS = 2
HEAD_DIM = 128
SSM_DIM = 64
STATE = 256
BLOCK = 256
LANES = 128
KERNEL_VMEM = 56 * 1024 * 1024


epsilon = 1e-05
rope_base = 10000.0
masked_score = -1e30


def mat_product(left_op, right_op):
    return jnp.dot(left_op, right_op, preferred_element_type=jnp.float32)


def weight_grad(left_op, right_op):
    return lax.dot_general(
        left_op, right_op, (((0,), (0,)), ((), ())), preferred_element_type=jnp.float32
    )


def input_grad(grad_rows, weights):
    return lax.dot_general(
        grad_rows, weights, (((1,), (1,)), ((), ())), preferred_element_type=jnp.float32
    )


def dot_plain(left_op, right_op):
    return jnp.dot(left_op, right_op, preferred_element_type=jnp.float32)


def dot_ones(left_op, ones, terms):
    total = None
    for _ in range(terms):
        part = left_op.astype(jnp.bfloat16)
        product = dot_plain(part, ones)
        total = product if total is None else total + product
        left_op = left_op - part.astype(jnp.float32)
    return total


def ones_dot(ones, right_op, terms):
    total = None
    for _ in range(terms):
        part = right_op.astype(jnp.bfloat16)
        product = dot_plain(ones, part)
        total = product if total is None else total + product
        right_op = right_op - part.astype(jnp.float32)
    return total


def logistic(values):
    return 0.5 * jnp.tanh(0.5 * values) + 0.5


def dot_rows(left_op, right_op):
    return lax.dot_general(
        left_op, right_op, (((1,), (1,)), ((), ())), preferred_element_type=jnp.float32
    )


def dot_columns(left_op, right_op):
    return lax.dot_general(
        left_op, right_op, (((0,), (0,)), ((), ())), preferred_element_type=jnp.float32
    )


def iota_of(shape, axis):
    return lax.broadcasted_iota(jnp.int32, shape, axis)


def allowed_block(marks_ref, seg_row_ref, row_start, col_start, columns, diagonal):
    seg_col = marks_ref[pl.ds(row_start, BLOCK), 0:1]
    seg_row = seg_row_ref[0:1, pl.ds(col_start, columns)]
    same = seg_col == seg_row
    if diagonal:
        row_pos = row_start + iota_of((BLOCK, columns), 0)
        col_pos = col_start + iota_of((BLOCK, columns), 1)
        same = same & (row_pos >= col_pos)
    return same


def store_relative(order_ref, target, piece, row_start, column, values):
    rows, width = values.shape
    for part in range(rows // piece):
        place = row_start // piece + part
        start = pl.multiple_of(order_ref[place] * piece, piece)
        target[pl.ds(start, piece), column : column + width] = values[
            part * piece : (part + 1) * piece
        ]


def attention_load(pieces, order_ref, narrow_ref, cos_ref, sin_ref, q_s, k_s, v_s, q_width):
    length = narrow_ref.shape[0]
    piece = length // pieces
    for place in range(pieces):
        start = pl.multiple_of(order_ref[place] * piece, piece)
        rows = slice(place * piece, (place + 1) * piece)
        cosine = cos_ref[rows, :]
        sine = sin_ref[rows, :]
        for column in range(0, q_width + HEAD_DIM, HEAD_DIM):
            part = narrow_ref[pl.ds(start, piece), column : column + HEAD_DIM].astype(jnp.float32)
            turned = part * cosine + pltpu.roll(part, HEAD_DIM // 2, 1) * sine
            if column < q_width:
                q_s[rows, column : column + HEAD_DIM] = turned.astype(jnp.bfloat16)
            else:
                k_s[rows, :] = turned.astype(jnp.bfloat16)
        v_s[rows, :] = narrow_ref[
            pl.ds(start, piece), q_width + HEAD_DIM : q_width + 2 * HEAD_DIM
        ]


def attention_forward_kernel(
    q_width,
    pieces,
    order_ref,
    narrow_ref,
    cos_ref,
    sin_ref,
    marks_ref,
    seg_row_ref,
    out_ref,
    lse_ref,
    q_s,
    k_s,
    v_s,
):
    length = narrow_ref.shape[0]
    piece = length // pieces
    attention_load(pieces, order_ref, narrow_ref, cos_ref, sin_ref, q_s, k_s, v_s, q_width)
    for block in range(length // BLOCK):
        start = block * BLOCK
        columns = start + BLOCK
        allowed = allowed_block(marks_ref, seg_row_ref, start, 0, columns, True)
        for head in range(q_width // HEAD_DIM):
            lanes = slice(head * HEAD_DIM, (head + 1) * HEAD_DIM)
            scores = dot_rows(q_s[start : start + BLOCK, lanes], k_s[0:columns, :])
            scores = jnp.where(allowed, scores * HEAD_DIM ** (-0.5), masked_score)
            row_max = jnp.max(scores, axis=1, keepdims=True)
            exponent = jnp.exp(scores - row_max)
            total = jnp.sum(exponent, axis=1, keepdims=True)
            probs = (exponent * (1.0 / total)).astype(jnp.bfloat16)
            mixed = dot_plain(probs, v_s[0:columns, :]).astype(jnp.bfloat16)
            store_relative(order_ref, out_ref, piece, start, head * HEAD_DIM, mixed)
            lse_ref[start : start + BLOCK, head : head + 1] = row_max + jnp.log(total)


def attention_backward_kernel(
    q_width,
    pieces,
    order_ref,
    narrow_ref,
    grad_ref,
    cos_ref,
    sin_ref,
    marks_ref,
    seg_row_ref,
    lse_ref,
    out_ref,
    q_s,
    k_s,
    v_s,
    g_s,
    dk_s,
    dv_s,
):
    length = narrow_ref.shape[0]
    piece = length // pieces
    scale = HEAD_DIM ** (-0.5)
    attention_load(pieces, order_ref, narrow_ref, cos_ref, sin_ref, q_s, k_s, v_s, q_width)
    for place in range(pieces):
        rows = slice(place * piece, (place + 1) * piece)
        start = pl.multiple_of(order_ref[place] * piece, piece)
        g_s[rows, :] = grad_ref[pl.ds(start, piece), 0:q_width]
    dk_s[...] = jnp.zeros_like(dk_s)
    dv_s[...] = jnp.zeros_like(dv_s)
    for block in range(length // BLOCK):
        start = block * BLOCK
        columns = start + BLOCK
        rows = slice(start, columns)
        cosine = cos_ref[rows, :]
        sine = sin_ref[rows, :]
        allowed = allowed_block(marks_ref, seg_row_ref, start, 0, columns, True)
        for head in range(q_width // HEAD_DIM):
            lanes = slice(head * HEAD_DIM, (head + 1) * HEAD_DIM)
            q_blk = q_s[rows, lanes]
            g_blk = g_s[rows, lanes]
            scores = dot_rows(q_blk, k_s[0:columns, :])
            scores = jnp.where(allowed, scores * scale, masked_score)
            probs = jnp.exp(scores - lse_ref[rows, head : head + 1])
            grad_probs = dot_rows(g_blk, v_s[0:columns, :])
            inner = jnp.sum(grad_probs * probs, axis=1, keepdims=True)
            grad_scores = (probs * (grad_probs - inner)).astype(jnp.bfloat16)
            grad_q = dot_plain(grad_scores, k_s[0:columns, :]) * scale
            grad_q = grad_q * cosine - pltpu.roll(grad_q, HEAD_DIM // 2, 1) * sine
            store_relative(
                order_ref, out_ref, piece, start, head * HEAD_DIM, grad_q.astype(jnp.bfloat16)
            )
            dk_s[0:columns, :] += dot_columns(grad_scores, q_blk)
            dv_s[0:columns, :] += dot_columns(probs.astype(jnp.bfloat16), g_blk)
    for block in range(length // BLOCK):
        start = block * BLOCK
        rows = slice(start, start + BLOCK)
        grad_k = dk_s[rows, :] * scale
        grad_k = grad_k * cos_ref[rows, :] - pltpu.roll(grad_k, HEAD_DIM // 2, 1) * sin_ref[rows, :]
        store_relative(order_ref, out_ref, piece, start, q_width, grad_k.astype(jnp.bfloat16))
        store_relative(
            order_ref,
            out_ref,
            piece,
            start,
            q_width + HEAD_DIM,
            dv_s[rows, :].astype(jnp.bfloat16),
        )


def head_spread(width):
    heads = iota_of((LANES, width), 0)
    return (iota_of((LANES, width), 1) // SSM_DIM == heads).astype(jnp.float32).astype(jnp.bfloat16)


def head_gather(width):
    heads = iota_of((width, LANES), 1)
    return (iota_of((width, LANES), 0) // SSM_DIM == heads).astype(jnp.float32).astype(jnp.bfloat16)


def triangle(lower):
    rows = iota_of((BLOCK, BLOCK), 0)
    columns = iota_of((BLOCK, BLOCK), 1)
    return (rows >= columns if lower else rows <= columns).astype(jnp.float32).astype(jnp.bfloat16)


def softplus(values):
    return jnp.maximum(values, 0.0) + jnp.log1p(jnp.exp(-jnp.abs(values)))


def mark_columns(marks_ref, row_start, first):
    return [
        jnp.broadcast_to(marks_ref[pl.ds(row_start, BLOCK), first + tap : first + tap + 1], (BLOCK, LANES))
        for tap in range(3)
    ]


def conv_window(pad_ref, taps_ref, before, row_start, column):
    total = jnp.broadcast_to(taps_ref[4:5, column : column + LANES], (BLOCK, LANES))
    shifted = []
    for tap in range(4):
        rows = pad_ref[column // LANES, pl.ds(row_start + 5 + tap, BLOCK), :]
        if tap < 3:
            rows = rows * before[tap]
        shifted.append(rows)
        total = total + rows * taps_ref[tap : tap + 1, column : column + LANES]
    return total, shifted


def mixer_load(
    x_column,
    order_ref,
    narrow_ref,
    bc_ref,
    marks_ref,
    x_taps_ref,
    bc_taps_ref,
    heads_ref,
    x_pad,
    bc_pad,
    dt_s,
    a_s,
    a_row_s,
    a_wide,
    mixed_s,
    scaled_s,
    bc_s,
):
    length, width = mixed_s.shape
    count, _, bc_width = bc_ref.shape
    pieces = 2 * count
    piece = length // pieces
    dt_column = narrow_ref.shape[1] - LANES
    x_pad[:, 0:8, :] = jnp.zeros((width // LANES, 8, LANES), jnp.float32)
    bc_pad[:, 0:8, :] = jnp.zeros((2 * STATE // LANES, 8, LANES), jnp.float32)
    for place in range(pieces):
        start = pl.multiple_of(order_ref[place] * piece, piece)
        rows = slice(place * piece, (place + 1) * piece)
        padded = slice(8 + place * piece, 8 + (place + 1) * piece)
        for chunk in range(width // LANES):
            column = x_column + chunk * LANES
            x_pad[chunk, padded, :] = narrow_ref[
                pl.ds(start, piece), column : column + LANES
            ].astype(jnp.float32)
        for owner in range(count):
            source = order_ref[pieces + owner]
            owner_start = pl.multiple_of(
                order_ref[pieces + count + owner * pieces + place] * piece, piece
            )
            lane = owner * bc_width % LANES
            bc_pad[owner * bc_width // LANES, padded, lane : lane + bc_width] = bc_ref[
                source, pl.ds(owner_start, piece), :
            ].astype(jnp.float32)
        dt_s[rows, :] = narrow_ref[pl.ds(start, piece), dt_column : dt_column + LANES].astype(
            jnp.float32
        )
    spread = head_spread(width)
    lower = triangle(True)
    rate = jnp.exp(heads_ref[0:1, :])
    bias = heads_ref[1:2, :]

    def one_block(block, carry):
        start = pl.multiple_of(block * BLOCK, BLOCK)
        rows = pl.ds(start, BLOCK)
        step = softplus(dt_s[rows, :] + bias)
        decay_sum = ones_dot(lower, step * rate, 3) + carry
        a_s[rows, :] = decay_sum
        a_row_s[block] = decay_sum.T
        a_wide[rows, :] = dot_ones(decay_sum, spread, 3)
        step_wide = dot_ones(step, spread, 2)
        before = mark_columns(marks_ref, start, 1)
        for column in range(0, width, LANES):
            lanes = slice(column, column + LANES)
            total, _ = conv_window(x_pad, x_taps_ref, before, start, column)
            mixed = total * logistic(total)
            mixed_s[rows, lanes] = mixed
            scaled_s[rows, lanes] = (mixed * step_wide[:, lanes]).astype(jnp.bfloat16)
        for column in range(0, 2 * STATE, LANES):
            total, _ = conv_window(bc_pad, bc_taps_ref, before, start, column)
            bc_s[rows, column : column + LANES] = (total * logistic(total)).astype(
                jnp.bfloat16
            )
        return decay_sum[BLOCK - 1 : BLOCK, :]

    lax.fori_loop(0, length // BLOCK, one_block, jnp.zeros((1, LANES), jnp.float32))


def half_lanes(values, half):
    lane = iota_of(values.shape, 1)
    keep = lane < SSM_DIM if half == 0 else lane >= SSM_DIM
    return jnp.where(keep, values, jnp.zeros_like(values))


def diagonal_decay(a_s, a_row_s, block, start, head):
    gap = a_row_s[block, head : head + 1, :] - a_s[pl.ds(start, BLOCK), head : head + 1]
    return jnp.exp(jnp.minimum(gap, 0.0))


def mixer_forward_kernel(
    x_column,
    order_ref,
    narrow_ref,
    bc_ref,
    marks_ref,
    seg_row_ref,
    x_taps_ref,
    bc_taps_ref,
    heads_ref,
    out_ref,
    x_pad,
    bc_pad,
    dt_s,
    a_s,
    a_row_s,
    a_wide,
    mixed_s,
    scaled_s,
    bc_s,
    weight_s,
    inter_s,
    total_s,
):
    length, width = mixed_s.shape
    piece = length // (2 * bc_ref.shape[0])
    mixer_load(
        x_column,
        order_ref,
        narrow_ref,
        bc_ref,
        marks_ref,
        x_taps_ref,
        bc_taps_ref,
        heads_ref,
        x_pad,
        bc_pad,
        dt_s,
        a_s,
        a_row_s,
        a_wide,
        mixed_s,
        scaled_s,
        bc_s,
    )
    skip_wide = dot_ones(jnp.broadcast_to(heads_ref[2:3, :], (8, LANES)), head_spread(width), 3)

    def one_block(block, _):
        start = pl.multiple_of(block * BLOCK, BLOCK)
        rows = pl.ds(start, BLOCK)
        out_c = bc_s[rows, STATE : 2 * STATE]
        total_s[...] = jnp.zeros_like(total_s)
        first = a_wide[pl.ds(start, 8), :][0:1]

        def earlier(other, _):
            col_start = pl.multiple_of(other * BLOCK, BLOCK)
            columns = pl.ds(col_start, BLOCK)
            allowed = allowed_block(marks_ref, seg_row_ref, start, col_start, BLOCK, False)
            inter = dot_rows(out_c, bc_s[columns, 0:STATE])
            inter = jnp.where(allowed, inter, 0.0).astype(jnp.bfloat16)
            faded = scaled_s[columns, :].astype(jnp.float32) * jnp.exp(a_wide[columns, :] - first)
            total_s[...] += dot_plain(inter, faded.astype(jnp.bfloat16))
            return 0

        lax.fori_loop(0, block, earlier, 0)
        allowed = allowed_block(marks_ref, seg_row_ref, start, start, BLOCK, True)
        inter_s[...] = jnp.where(allowed, dot_rows(out_c, bc_s[rows, 0:STATE]), 0.0)
        for column in range(0, width, LANES):
            lanes = slice(column, column + LANES)
            scaled = scaled_s[rows, lanes]
            mixed = total_s[:, lanes] * jnp.exp(first[:, lanes] - a_wide[rows, lanes])
            for half in range(2):
                head = column // SSM_DIM + half
                decay = diagonal_decay(a_s, a_row_s, block, start, head)
                weights = (inter_s[...] * decay).astype(jnp.bfloat16)
                mixed = mixed + dot_plain(weights, half_lanes(scaled, half))
            mixed = mixed + skip_wide[0:1, lanes] * mixed_s[rows, lanes]
            weight_s[:, lanes] = mixed.astype(jnp.bfloat16)
        for part in range(BLOCK // piece):
            place = block * (BLOCK // piece) + part
            target = pl.multiple_of(order_ref[place] * piece, piece)
            out_ref[pl.ds(target, piece), :] = weight_s[part * piece : (part + 1) * piece, :]
        return 0

    lax.fori_loop(0, length // BLOCK, one_block, 0)


def mixer_backward_kernel(
    x_column,
    order_ref,
    narrow_ref,
    bc_ref,
    grad_ref,
    marks_ref,
    seg_row_ref,
    x_taps_ref,
    bc_taps_ref,
    heads_ref,
    gx_ref,
    gdt_ref,
    gbc_ref,
    gx_taps_ref,
    gbc_taps_ref,
    gheads_ref,
    x_pad,
    bc_pad,
    dt_s,
    a_s,
    a_row_s,
    a_wide,
    mixed_s,
    scaled_s,
    bc_s,
    grad_s,
    gscaled_s,
    gap_s,
    gbc_s,
    inter_s,
    gover_s,
    faded_s,
    gfaded_s,
    fade_s,
    edge_s,
    ahead_s,
    low_s,
):
    length, width = mixed_s.shape
    count, _, bc_width = bc_ref.shape
    pieces = 2 * count
    piece = length // pieces
    blocks = length // BLOCK
    mixer_load(
        x_column,
        order_ref,
        narrow_ref,
        bc_ref,
        marks_ref,
        x_taps_ref,
        bc_taps_ref,
        heads_ref,
        x_pad,
        bc_pad,
        dt_s,
        a_s,
        a_row_s,
        a_wide,
        mixed_s,
        scaled_s,
        bc_s,
    )
    for place in range(pieces):
        source = pl.multiple_of(order_ref[place] * piece, piece)
        grad_s[place * piece : (place + 1) * piece, :] = grad_ref[pl.ds(source, piece), :]
    gscaled_s[...] = jnp.zeros_like(gscaled_s)
    gap_s[...] = jnp.zeros_like(gap_s)
    gbc_s[...] = jnp.zeros_like(gbc_s)

    def one_block(block, _):
        start = pl.multiple_of(block * BLOCK, BLOCK)
        rows = pl.ds(start, BLOCK)
        out_c = bc_s[rows, STATE : 2 * STATE]
        allowed = allowed_block(marks_ref, seg_row_ref, start, start, BLOCK, True)
        inter_s[...] = jnp.where(allowed, dot_rows(out_c, bc_s[rows, 0:STATE]), 0.0)
        gover_s[...] = jnp.zeros_like(gover_s)
        for column in range(0, width, LANES):
            lanes = slice(column, column + LANES)
            scaled = scaled_s[rows, lanes]
            grad = grad_s[rows, lanes]
            row_side = jnp.zeros((BLOCK, LANES), jnp.float32)
            col_side = jnp.zeros((BLOCK, LANES), jnp.float32)
            for half in range(2):
                head = column // SSM_DIM + half
                decay = diagonal_decay(a_s, a_row_s, block, start, head)
                weights = (inter_s[...] * decay).astype(jnp.bfloat16)
                scaled_half = half_lanes(scaled, half)
                gover_s[...] += dot_rows(grad, scaled_half) * decay
                row_side = row_side + dot_plain(weights, scaled_half)
                col_side = col_side + dot_columns(weights, half_lanes(grad, half))
            gscaled_s[rows, lanes] += col_side
            gap_s[rows, lanes] += scaled.astype(jnp.float32) * col_side - grad.astype(
                jnp.float32
            ) * row_side
        gover = jnp.where(allowed, gover_s[...], 0.0).astype(jnp.bfloat16)
        gbc_s[rows, STATE : 2 * STATE] += dot_plain(gover, bc_s[rows, 0:STATE])
        gbc_s[rows, 0:STATE] += dot_columns(gover, out_c)
        first = a_wide[pl.ds(start, 8), :][0:1]
        gfaded_s[...] = (
            grad_s[rows, :].astype(jnp.float32) * jnp.exp(first - a_wide[rows, :])
        ).astype(jnp.bfloat16)

        def earlier(other, _):
            col_start = pl.multiple_of(other * BLOCK, BLOCK)
            columns = pl.ds(col_start, BLOCK)
            same = allowed_block(marks_ref, seg_row_ref, start, col_start, BLOCK, False)
            in_b = bc_s[columns, 0:STATE]
            inter = jnp.where(same, dot_rows(out_c, in_b), 0.0).astype(jnp.bfloat16)
            fade_s[...] = jnp.exp(a_wide[columns, :] - first)
            faded_s[...] = (scaled_s[columns, :].astype(jnp.float32) * fade_s[...]).astype(
                jnp.bfloat16
            )
            over = dot_rows(gfaded_s[...], faded_s[...])
            over = jnp.where(same, over, 0.0).astype(jnp.bfloat16)
            gbc_s[rows, STATE : 2 * STATE] += dot_plain(over, in_b)
            gbc_s[columns, 0:STATE] += dot_columns(over, out_c)
            gap_s[rows, :] -= gfaded_s[...].astype(jnp.float32) * dot_plain(inter, faded_s[...])
            col_side = dot_columns(inter, gfaded_s[...])
            gap_s[columns, :] += faded_s[...].astype(jnp.float32) * col_side
            gscaled_s[columns, :] += fade_s[...] * col_side
            return 0

        lax.fori_loop(0, block, earlier, 0)
        return 0

    lax.fori_loop(0, blocks, one_block, 0)

    spread = head_spread(width)
    gather = head_gather(width)
    upper = triangle(False)
    rate = jnp.exp(heads_ref[0:1, :])
    bias = heads_ref[1:2, :]
    skip_wide = dot_ones(jnp.broadcast_to(heads_ref[2:3, :], (8, LANES)), spread, 3)
    gx_taps_ref[...] = jnp.zeros_like(gx_taps_ref)
    gbc_taps_ref[...] = jnp.zeros_like(gbc_taps_ref)
    gheads_ref[...] = jnp.zeros_like(gheads_ref)
    edge_s[...] = jnp.zeros_like(edge_s)

    def conv_back(pad_ref, taps_ref, gtaps_ref, before, after, start, column, shift, gmixed):
        total, shifted = conv_window(pad_ref, taps_ref, before, start, column)
        sig = logistic(total)
        gtotal = gmixed * sig * (1.0 + total * (1.0 - sig))
        lanes = slice(column, column + LANES)
        for tap in range(4):
            gtaps_ref[tap : tap + 1, lanes] += jnp.sum(gtotal * shifted[tap], axis=0, keepdims=True)
        gtaps_ref[4:5, lanes] += jnp.sum(gtotal, axis=0, keepdims=True)
        wide = slice(shift + column, shift + column + LANES)
        chunk = (shift + column) // LANES
        ahead_s[chunk, 0:BLOCK, :] = gtotal
        ahead_s[chunk, BLOCK : BLOCK + 8, :] = edge_s[:, wide]
        edge_s[:, wide] = gtotal[0:8]
        result = gtotal * taps_ref[3:4, lanes]
        for tap in range(3):
            ahead = ahead_s[chunk, 3 - tap : 3 - tap + BLOCK, :] * after[tap]
            result = result + ahead * taps_ref[tap : tap + 1, lanes]
        return result.astype(jnp.bfloat16)

    def last_block(index, carry):
        block = blocks - 1 - index
        start = pl.multiple_of(block * BLOCK, BLOCK)
        rows = pl.ds(start, BLOCK)
        raw = dt_s[rows, :] + bias
        step = softplus(raw)
        gsum = ones_dot(upper, dot_ones(gap_s[rows, :], gather, 2), 3) + carry
        gstep = dot_ones(gscaled_s[rows, :] * mixed_s[rows, :], gather, 2) + gsum * rate
        graw = gstep * jax.nn.sigmoid(raw)
        gheads_ref[0:1, :] += jnp.sum(gsum * step * rate, axis=0, keepdims=True)
        gheads_ref[1:2, :] += jnp.sum(graw, axis=0, keepdims=True)
        low_s[:, width : width + LANES] = graw.astype(jnp.bfloat16)
        step_wide = dot_ones(step, spread, 2)
        skip_parts = []
        before = mark_columns(marks_ref, start, 1)
        after = mark_columns(marks_ref, start, 4)
        for column in range(0, width, LANES):
            lanes = slice(column, column + LANES)
            grad = grad_s[rows, lanes].astype(jnp.float32)
            skip_parts.append(jnp.sum(grad * mixed_s[rows, lanes], axis=0, keepdims=True))
            gmixed = skip_wide[0:1, lanes] * grad + gscaled_s[rows, lanes] * step_wide[:, lanes]
            low_s[:, lanes] = conv_back(
                x_pad, x_taps_ref, gx_taps_ref, before, after, start, column, 0, gmixed
            )
        skip_row = jnp.broadcast_to(jnp.concatenate(skip_parts, axis=1), (8, width))
        gheads_ref[2:3, :] += dot_ones(skip_row, gather, 2)[0:1]
        for column in range(0, 2 * STATE, LANES):
            lanes = slice(column, column + LANES)
            low_s[:, width + LANES + column : width + 2 * LANES + column] = conv_back(
                bc_pad,
                bc_taps_ref,
                gbc_taps_ref,
                before,
                after,
                start,
                column,
                width,
                gbc_s[rows, lanes],
            )
        for part in range(BLOCK // piece):
            place = block * (BLOCK // piece) + part
            target = pl.multiple_of(order_ref[place] * piece, piece)
            gx_ref[pl.ds(target, piece), :] = low_s[part * piece : (part + 1) * piece, 0:width]
            gdt_ref[pl.ds(target, piece), :] = low_s[
                part * piece : (part + 1) * piece, width : width + LANES
            ]
            for owner in range(count):
                first = width + LANES + owner * bc_width
                owner_start = pl.multiple_of(
                    order_ref[pieces + count + owner * pieces + place] * piece, piece
                )
                gbc_ref[order_ref[pieces + owner], pl.ds(owner_start, piece), :] = low_s[
                    part * piece : (part + 1) * piece, first : first + bc_width
                ]
        return gsum[0:1, :]

    lax.fori_loop(0, blocks, last_block, jnp.zeros((1, LANES), jnp.float32))


def local_call(kernel, outs, scratch, flops, operands):
    moved = sum(part.size * part.dtype.itemsize for part in operands)
    moved += sum(part.size * part.dtype.itemsize for part in outs)
    return pl.pallas_call(
        kernel,
        out_shape=outs,
        in_specs=[pl.BlockSpec(memory_space=pltpu.SMEM)]
        + [pl.BlockSpec(memory_space=pltpu.VMEM)] * (len(operands) - 1),
        out_specs=[pl.BlockSpec(memory_space=pltpu.VMEM)] * len(outs),
        scratch_shapes=scratch,
        compiler_params=pltpu.CompilerParams(vmem_limit_bytes=KERNEL_VMEM),
        cost_estimate=pl.CostEstimate(flops=flops, bytes_accessed=moved, transcendentals=0),
    )(*operands)


def array_of(shape, dtype):
    return jax.ShapeDtypeStruct(shape, dtype)


def attention_forward(q_width, pieces, order, narrow, cosine, sine, marks, seg_row):
    length = narrow.shape[0]
    low = jnp.bfloat16
    return local_call(
        functools.partial(attention_forward_kernel, q_width, pieces),
        [array_of((length, q_width), low), array_of((length, 8), jnp.float32)],
        [
            pltpu.VMEM((length, q_width), low),
            pltpu.VMEM((length, HEAD_DIM), low),
            pltpu.VMEM((length, HEAD_DIM), low),
        ],
        36 * length * length * q_width,
        (order, narrow, cosine, sine, marks, seg_row),
    )


def attention_backward(q_width, pieces, order, narrow, grad, cosine, sine, marks, seg_row, lse):
    length = narrow.shape[0]
    low = jnp.bfloat16
    return local_call(
        functools.partial(attention_backward_kernel, q_width, pieces),
        [array_of((length, q_width + 2 * HEAD_DIM), low)],
        [
            pltpu.VMEM((length, q_width), low),
            pltpu.VMEM((length, HEAD_DIM), low),
            pltpu.VMEM((length, HEAD_DIM), low),
            pltpu.VMEM((length, q_width), low),
            pltpu.VMEM((length, HEAD_DIM), jnp.float32),
            pltpu.VMEM((length, HEAD_DIM), jnp.float32),
        ],
        44 * length * length * q_width,
        (order, narrow, grad, cosine, sine, marks, seg_row, lse),
    )[0]


def mixer_scratch(length, width):
    low, full = jnp.bfloat16, jnp.float32
    return [
        pltpu.VMEM((width // LANES, length + 8, LANES), full),
        pltpu.VMEM((2 * STATE // LANES, length + 8, LANES), full),
        pltpu.VMEM((length, LANES), full),
        pltpu.VMEM((length, LANES), full),
        pltpu.VMEM((length // BLOCK, LANES, BLOCK), full),
        pltpu.VMEM((length, width), full),
        pltpu.VMEM((length, width), full),
        pltpu.VMEM((length, width), low),
        pltpu.VMEM((length, 2 * STATE), low),
    ]


def mixer_forward(x_column, width, order, narrow, bc, marks, seg_row, x_taps, bc_taps, heads):
    length = narrow.shape[0]
    low, full = jnp.bfloat16, jnp.float32
    return local_call(
        functools.partial(mixer_forward_kernel, x_column),
        [array_of((length, width), low)],
        mixer_scratch(length, width)
        + [
            pltpu.VMEM((BLOCK, width), low),
            pltpu.VMEM((BLOCK, BLOCK), full),
            pltpu.VMEM((BLOCK, width), full),
        ],
        28 * length * length * width,
        (order, narrow, bc, marks, seg_row, x_taps, bc_taps, heads),
    )[0]


def mixer_backward(x_column, width, order, narrow, bc, grad, marks, seg_row, x_taps, bc_taps, heads):
    length = narrow.shape[0]
    low, full = jnp.bfloat16, jnp.float32
    return local_call(
        functools.partial(mixer_backward_kernel, x_column),
        [
            array_of((length, width), low),
            array_of((length, LANES), low),
            array_of(bc.shape, low),
            array_of((8, width), full),
            array_of((8, 2 * STATE), full),
            array_of((8, LANES), full),
        ],
        mixer_scratch(length, width)
        + [
            pltpu.VMEM((length, width), low),
            pltpu.VMEM((length, width), full),
            pltpu.VMEM((length, width), full),
            pltpu.VMEM((length, 2 * STATE), full),
            pltpu.VMEM((BLOCK, BLOCK), full),
            pltpu.VMEM((BLOCK, BLOCK), full),
            pltpu.VMEM((BLOCK, width), low),
            pltpu.VMEM((BLOCK, width), low),
            pltpu.VMEM((BLOCK, width), full),
            pltpu.VMEM((8, width + 2 * STATE), full),
            pltpu.VMEM(((width + 2 * STATE) // LANES, BLOCK + 8, LANES), full),
            pltpu.VMEM((BLOCK, width + LANES + 2 * STATE), low),
        ],
        60 * length * length * width,
        (order, narrow, bc, grad, marks, seg_row, x_taps, bc_taps, heads),
    )


def document_marks(seg_row):
    length = seg_row.shape[0]
    before = jnp.pad(seg_row, (3, 0), constant_values=-1)
    after = jnp.pad(seg_row, (0, 3), constant_values=-1)
    columns = [seg_row.astype(jnp.float32)]
    for tap in range(3):
        columns.append((before[tap : tap + length] == seg_row).astype(jnp.float32))
    for tap in range(3):
        columns.append((after[3 - tap : 3 - tap + length] == seg_row).astype(jnp.float32))
    columns.append(jnp.zeros((length,), jnp.float32))
    return jnp.stack(columns, axis=1)


def rope_wide(length):
    half_dim = HEAD_DIM // 2
    frequency = rope_base ** (-jnp.arange(half_dim, dtype=jnp.float32) / half_dim)
    angles = jnp.arange(length, dtype=jnp.float32)[:, None] * frequency[None, :]
    cosine, sine = jnp.cos(angles), jnp.sin(angles)
    return jnp.concatenate([cosine, cosine], axis=1), jnp.concatenate([-sine, sine], axis=1)


def swap_seq(value, bit, count):
    return lax.ppermute(value, "seq", [(place, place ^ bit) for place in range(count)])


def seq_bits(count):
    bits = []
    bit = 1
    while bit < count:
        bits.append(bit)
        bit *= 2
    return bits


def block_order(bits):
    order = [0]
    for bit in bits:
        order = order + [place ^ bit for place in order]
    return order


def relative_order(count):
    bits = seq_bits(count)
    upper = [(0, block) for block in block_order(bits)]
    lower = [(1, block) for block in block_order(bits[::-1])]
    near = count // 2
    return upper[:near] + lower[:near] + upper[near:] + lower[near:]


def gather_first(rows, count):
    half = rows.shape[0] // 2
    bits = seq_bits(count)
    pieces = []
    for piece, order in ((rows[:half], bits), (rows[half:], bits[::-1])):
        for bit in order[:-1]:
            piece = jnp.concatenate([piece, swap_seq(piece, bit, count)], axis=0)
        pieces.append(piece)
    return pieces


def gather_last(pieces, count):
    bits = seq_bits(count)
    far = [swap_seq(piece, bit, count) for piece, bit in zip(pieces, (bits[-1], bits[0]))]
    return jnp.concatenate(pieces, axis=0), jnp.concatenate(far, axis=0)


def rows_gather(rows, count):
    return gather_last(gather_first(rows, count), count)


def scatter_first(far, count):
    half = far.shape[0] // 2
    bits = seq_bits(count)
    far = far.astype(jnp.bfloat16)
    return [
        swap_seq(far[first : first + half], order[-1], count)
        for first, order in ((0, bits), (half, bits[::-1]))
    ]


def scatter_second(near, came, count):
    half = near.shape[0] // 2
    bits = seq_bits(count)
    kept, arrived = [], []
    for first, order, add in ((0, bits, came[0]), (half, bits[::-1], came[1])):
        piece = near[first : first + half]
        for bit in order[:-1][::-1]:
            piece = piece + add.astype(jnp.float32)
            keep = piece.shape[0] // 2
            add = swap_seq(piece[keep:].astype(jnp.bfloat16), bit, count)
            piece = piece[:keep]
        kept.append(piece)
        arrived.append(add)
    return kept, arrived


def scatter_last(kept, arrived):
    return jnp.concatenate(
        [piece + add.astype(jnp.float32) for piece, add in zip(kept, arrived)], axis=0
    )


def rows_scatter(near, far, count):
    came = scatter_first(far, count)
    return scatter_last(*scatter_second(near, came, count))


def row_tables(count):
    order = relative_order(count)

    def places(rank):
        return [order.index((half, block ^ rank)) for block in range(count) for half in range(2)]

    everyone = [place for rank in range(count) for place in places(rank)]
    return np.asarray(
        [
            places(rank) + [other ^ rank for other in range(count)] + everyone
            for rank in range(count)
        ],
        np.int32,
    )


def seq_pieces(value, count):
    return [value] + [swap_seq(value, bit, count) for bit in range(1, count)]


def seq_sum(value, count):
    order = relative_order(count)
    total = value.reshape(2 * count, -1)
    for bit in range(1, count):
        came = swap_seq(value, bit, count).reshape(2 * count, -1)
        places = [order.index((half, block ^ bit)) for half, block in order]
        total = total + jnp.concatenate([came[place : place + 1] for place in places])
    return total.reshape(-1)


def norm_forward(rows, gain):
    scale = lax.rsqrt(jnp.mean(rows * rows, axis=-1, keepdims=True) + epsilon)
    return ((rows * scale * gain).astype(jnp.bfloat16), scale)


def norm_backward(rows, scale, gain, cotangent):
    weighted = cotangent * gain
    inner = jnp.mean(rows * weighted, axis=-1, keepdims=True)
    grad_rows = scale * weighted - rows * (scale * scale * scale * inner)
    return grad_rows


def columns_exchange(blocks):
    return lax.all_to_all(blocks, "seq", split_axis=0, concat_axis=0, tiled=True)


def rows_of_all(piece):
    return lax.all_gather(piece, "fsdp", axis=1, tiled=True).reshape(-1, piece.shape[2])


def columns_gather(blocks):
    return rows_of_all(columns_exchange(blocks))


def columns_to_owners(blocks):
    blocks = with_layout_constraint(blocks, Layout(major_to_minor=(0, 1, 2)))
    return lax.all_to_all(blocks, "seq", split_axis=0, concat_axis=0, tiled=True)


def rank_parts(arrived):
    return [arrived[place].astype(jnp.float32) for place in range(arrived.shape[0])]


def side_by_side(parts, first, width):
    return jnp.concatenate([part[:, first : first + width] for part in parts], axis=1)


def body(
    seq_count,
    fsdp_count,
    hidden_in,
    segments,
    out_grad,
    norm1_gain,
    w_query,
    w_keyval,
    w_attn_out,
    w_gate_z,
    w_ssm_x,
    w_ssm_bc,
    w_ssm_dt,
    conv_taps,
    a_log,
    dt_bias,
    skip_gain,
    ssm_gain,
    w_ssm_out,
    norm2_gain,
    w_ff_gate,
    w_ff_up,
    w_ff_down,
):
    f32, bf16 = jnp.float32, jnp.bfloat16
    batch, block_len, model_width = hidden_in.shape
    length = block_len * seq_count
    rank = lax.axis_index("seq")
    seg_row = segments[0]
    heads_local = HEADS // seq_count
    group_size = HEADS // KV_HEADS
    q_width = w_query.shape[1] // seq_count
    z_width = w_gate_z.shape[1] // seq_count
    x_width = w_ssm_x.shape[1] // seq_count
    bc_width = w_ssm_bc.shape[1] // seq_count
    dt_width = w_ssm_dt.shape[1] // seq_count
    ff_width = w_ff_gate.shape[1] // seq_count
    kv_total = w_keyval.shape[1] // 2
    heads_total = a_log.shape[0]
    dssm = w_ssm_x.shape[1]
    row_piece = w_query.shape[0]
    bc_pad = -bc_width % LANES
    dt_pad = -dt_width % LANES

    def pack(vector):
        parts = -(-vector.shape[0] // row_piece)
        padded = jnp.pad(vector, (0, parts * row_piece - vector.shape[0]))
        return [padded[part * row_piece : (part + 1) * row_piece] for part in range(parts)]

    def unpack(columns, length_each):
        spread = columns.reshape(columns.shape[0], -1, row_piece).transpose(1, 0, 2)
        return spread.reshape(spread.shape[0], -1)[:, :length_each].reshape(-1)

    extra_columns = [norm1_gain, norm2_gain] + pack(ssm_gain)
    ssm_pieces = len(extra_columns) - 2
    for tap in range(conv_taps.shape[1]):
        extra_columns += pack(conv_taps[:, tap])
    taps_pieces = (len(extra_columns) - 2 - ssm_pieces) // conv_taps.shape[1]
    extra_block = jnp.pad(
        jnp.stack(extra_columns, axis=1), ((0, 0), (0, dt_pad - len(extra_columns)))
    )
    free_first = q_width + 2 * HEAD_DIM + x_width + bc_width + bc_pad + dt_width
    sends = []
    for target in range(seq_count):
        kv_head = target * heads_local // group_size
        sends.append(
            jnp.concatenate(
                [
                    w_query[:, target * q_width : (target + 1) * q_width],
                    w_keyval[:, kv_head * HEAD_DIM : (kv_head + 1) * HEAD_DIM],
                    w_keyval[:, kv_total + kv_head * HEAD_DIM : kv_total + (kv_head + 1) * HEAD_DIM],
                    w_ssm_x[:, target * x_width : (target + 1) * x_width],
                    w_ssm_bc[:, target * bc_width : (target + 1) * bc_width],
                    jnp.zeros((row_piece, bc_pad), bf16),
                    w_ssm_dt[:, target * dt_width : (target + 1) * dt_width],
                    extra_block,
                ],
                axis=1,
            )
        )
    narrow_piece = columns_exchange(jnp.stack(sends))
    narrow_w = rows_of_all(narrow_piece)
    extras = lax.slice_in_dim(narrow_w, free_first, free_first + len(extra_columns), axis=1).T
    extras = extras.astype(f32)
    gain1, gain2 = extras[0], extras[1]
    taps_rows, taps_width = conv_taps.shape
    ssm_count = ssm_gain.shape[0]
    gain_ssm = unpack(extras[2 : 2 + ssm_pieces], ssm_count)
    gain_ssm = lax.dynamic_slice_in_dim(gain_ssm, rank * z_width, z_width, 0)
    taps = [
        unpack(extras[first : first + taps_pieces], taps_rows)
        for first in range(2 + ssm_pieces, len(extra_columns), taps_pieces)
    ]
    taps_rows8 = jnp.pad(jnp.stack(taps), ((0, 8 - taps_width), (0, 0)))
    x_taps = lax.dynamic_slice_in_dim(taps_rows8, rank * x_width, x_width, 1)
    bc_taps = taps_rows8[:, dssm:]
    head_rows = lax.dynamic_slice_in_dim(
        jnp.stack([a_log, dt_bias, skip_gain]), rank * dt_width, dt_width, 1
    )
    head_rows = jnp.pad(head_rows, ((0, 5), (0, dt_pad)))
    marks = document_marks(seg_row)
    seg_line = jnp.broadcast_to(seg_row.astype(f32)[None, :], (8, length))

    to_true = lax.dynamic_index_in_dim(jnp.asarray(row_tables(seq_count)), rank, 0, False)
    pieces = 2 * seq_count

    own_in = hidden_in.reshape(block_len, model_width)
    narrow_piece, own_in = lax.optimization_barrier((narrow_piece, own_in))
    all_in = jnp.concatenate(rows_gather(own_in, seq_count), axis=0)
    all_in, w_gate_z, w_ff_gate, w_ff_up, w_attn_out, w_ssm_out = lax.optimization_barrier(
        (all_in, w_gate_z, w_ff_gate, w_ff_up, w_attn_out, w_ssm_out)
    )
    wide_piece = columns_exchange(
        jnp.stack(
            [
                jnp.concatenate(
                    [
                        w_gate_z[:, target * z_width : (target + 1) * z_width],
                        w_ff_gate[:, target * ff_width : (target + 1) * ff_width],
                        w_ff_up[:, target * ff_width : (target + 1) * ff_width],
                    ],
                    axis=1,
                )
                for target in range(seq_count)
            ]
        )
    )
    z_piece, ff_piece = wide_piece[:, :, :z_width], wide_piece[:, :, z_width:]
    z_w = rows_of_all(z_piece)
    out_piece = jnp.concatenate([w_attn_out, w_ssm_out], axis=0)
    z_piece, out_piece = lax.optimization_barrier((z_piece, out_piece))
    out_w = lax.all_gather(out_piece, "fsdp", axis=0)

    cosine, sine = rope_wide(length)
    all_in, cosine, sine, marks, seg_line, to_true = lax.optimization_barrier(
        (all_in, cosine, sine, marks, seg_line, to_true)
    )
    ff_w = rows_of_all(ff_piece)
    normed, _ = norm_forward(all_in.astype(f32), gain1)
    edges = [0]
    for width in (q_width, HEAD_DIM, HEAD_DIM, x_width, bc_width + bc_pad, dt_width + dt_pad):
        edges.append(edges[-1] + width)
    narrow = mat_product(normed, narrow_w).astype(bf16)
    narrow, out_grad = lax.optimization_barrier((narrow, out_grad))
    grad_own = out_grad.reshape(block_len, model_width)
    grad_ff = gather_first(grad_own, seq_count)
    bc_seq = jnp.stack(seq_pieces(narrow[:, edges[4] : edges[4] + bc_width], seq_count))
    attn_rel, lse_seq = attention_forward(
        q_width, pieces, to_true, narrow, cosine, sine, marks, seg_line
    )
    bc_seq, attn_rel, w_ff_down, grad_ff = lax.optimization_barrier(
        (bc_seq, attn_rel, w_ff_down, grad_ff)
    )
    grad_ff = gather_last(grad_ff, seq_count)
    down_w = lax.all_gather(w_ff_down, "fsdp", axis=0, tiled=True)
    mixer_args = (x_taps, bc_taps, head_rows)
    ssm_rel = mixer_forward(
        edges[3], x_width, to_true, narrow, bc_seq, marks, seg_line, *mixer_args
    )
    ssm_rel, z_w, grad_ff = lax.optimization_barrier((ssm_rel, z_w, grad_ff))
    ssm_rel = ssm_rel.astype(f32)
    gate_z = mat_product(normed, z_w)
    gate_sig = jax.nn.sigmoid(gate_z)
    gate_silu = gate_z * gate_sig
    gated = ssm_rel * gate_silu
    square_sum = seq_sum(jnp.sum(gated * gated, axis=1), seq_count)
    gated_scale = lax.rsqrt(square_sum / dssm + epsilon)[:, None]
    ssm_in = (gated * gated_scale * gain_ssm).astype(bf16)
    ssm_in, out_w = lax.optimization_barrier((ssm_in, out_w))
    attn_out_w = out_w[:, : w_attn_out.shape[0]].reshape(-1, model_width)
    ssm_out_w = out_w[:, w_attn_out.shape[0] :].reshape(-1, model_width)
    near = length // 2

    def out_product(first):
        rows = slice(first, first + near)
        return mat_product(attn_rel[rows], attn_out_w) + mat_product(ssm_in[rows], ssm_out_w)

    xin = own_in.astype(f32)
    middle = xin + rows_scatter(out_product(0), out_product(near), seq_count)

    own_normed2, scale2 = norm_forward(middle, gain2)
    normed2 = rows_gather(own_normed2, seq_count)

    def ff_forward(rows):
        gate_ff = mat_product(rows, ff_w[:, :ff_width])
        up_ff = mat_product(rows, ff_w[:, ff_width:])
        ff_sig = jax.nn.sigmoid(gate_ff)
        ff_silu = gate_ff * ff_sig
        return up_ff, ff_sig, ff_silu, (ff_silu * up_ff).astype(bf16), gate_ff

    def ff_backward(grad_rows, up_ff, ff_sig, ff_silu):
        grad_act = input_grad(grad_rows, down_w)
        grad_gate_ff = grad_act * up_ff * (ff_sig + ff_silu * (1.0 - ff_sig))
        grad_up_ff = grad_act * ff_silu
        return jnp.concatenate([grad_gate_ff.astype(bf16), grad_up_ff.astype(bf16)], axis=1)

    up_near, sig_near, silu_near, act_near, gate_near = ff_forward(normed2[0])
    normed2_far, act_near, up_near, gate_near = lax.optimization_barrier(
        (normed2[1], act_near, up_near, gate_near)
    )
    sig_near = jax.nn.sigmoid(gate_near)
    silu_near = gate_near * sig_near
    up_far, sig_far, silu_far, act_far, gate_far = ff_forward(normed2_far)
    act = jnp.concatenate([act_near, act_far], axis=0)
    grad_ff_all = jnp.concatenate(grad_ff, axis=0)
    normed2_all = jnp.concatenate([normed2[0], normed2_far], axis=0)
    act, grad_ff_all = lax.optimization_barrier((act, grad_ff_all))
    grad_w_down = weight_grad(act, grad_ff_all).astype(bf16)
    grad_ff_far, grad_w_down = lax.optimization_barrier((grad_ff[1], grad_w_down))
    grad_w_down = lax.psum_scatter(grad_w_down, "fsdp", scatter_dimension=0, tiled=True)
    pair_far = ff_backward(grad_ff_far, up_far, sig_far, silu_far)
    pair_far = lax.optimization_barrier(pair_far)
    normed2_grad_far = input_grad(pair_far, ff_w).astype(bf16)
    grad_ff_near, normed2_grad_far = lax.optimization_barrier((grad_ff[0], normed2_grad_far))
    pair_near = ff_backward(grad_ff_near, up_near, sig_near, silu_near)
    pair_near = lax.optimization_barrier(pair_near)
    normed2_grad_near = input_grad(pair_near, ff_w)
    grad_pair = jnp.concatenate([pair_near, pair_far], axis=0)
    grad_pair, normed2_all = lax.optimization_barrier((grad_pair, normed2_all))
    grad_w_ff = weight_grad(normed2_all, grad_pair).astype(bf16)
    grad_w_ff = lax.psum_scatter(
        grad_w_ff.reshape(seq_count, -1, 2 * ff_width), "fsdp", scatter_dimension=1, tiled=True
    )
    grad_normed2 = rows_scatter(normed2_grad_near, normed2_grad_far, seq_count)
    grad_normed2, grad_w_down = lax.optimization_barrier((grad_normed2, grad_w_down))
    grad_middle_norm = norm_backward(middle, scale2, gain2, grad_normed2)
    grad_middle = grad_own.astype(f32) + grad_middle_norm

    mix_near, mix_far = rows_gather(grad_middle.astype(bf16), seq_count)
    ff_near = mat_product(act[:near], down_w)
    ff_far = mat_product(act[near:], down_w).astype(bf16)
    mix_far, ff_near, ff_far = lax.optimization_barrier((mix_far, ff_near, ff_far))
    grad_mix = jnp.concatenate([mix_near, mix_far], axis=0)
    grad_attn = input_grad(grad_mix, attn_out_w).astype(bf16)
    grad_ssm_in = input_grad(grad_mix, ssm_out_w)
    grad_w_attn = weight_grad(attn_rel, grad_mix).astype(bf16)
    grad_w_ssm = weight_grad(ssm_in, grad_mix).astype(bf16)
    weighted = grad_ssm_in * gain_ssm
    inner = seq_sum(jnp.sum(gated * weighted, axis=1), seq_count)
    out_grads = jnp.concatenate(
        [
            grad_w_attn.reshape(fsdp_count, -1, model_width),
            grad_w_ssm.reshape(fsdp_count, -1, model_width),
        ],
        axis=1,
    )
    grad_qkv = attention_backward(
        q_width, pieces, to_true, narrow, grad_attn, cosine, sine, marks, seg_line, lse_seq
    )
    inner, out_grads = lax.optimization_barrier((inner, out_grads))
    out_grads = lax.psum_scatter(out_grads, "fsdp", scatter_dimension=0, tiled=True)[0]
    inner = inner[:, None] / dssm
    grad_gated = gated_scale * weighted - gated * (
        gated_scale * gated_scale * gated_scale * inner
    )
    grad_ssm = (grad_gated * gate_silu).astype(bf16)
    grad_z = (grad_gated * ssm_rel * (gate_sig + gate_silu * (1.0 - gate_sig))).astype(bf16)
    grad_zq = lax.optimization_barrier(jnp.concatenate([grad_z, grad_qkv], axis=1))
    grad_w_zq = weight_grad(normed, grad_zq).astype(bf16)
    grad_ssm, grad_w_zq, ff_far, grad_w_ff = lax.optimization_barrier(
        (grad_ssm, grad_w_zq, ff_far, grad_w_ff)
    )
    grad_w_zq = lax.psum_scatter(
        grad_w_zq.reshape(seq_count, -1, grad_zq.shape[1]),
        "fsdp",
        scatter_dimension=1,
        tiled=True,
    )
    ff_came = scatter_first(ff_far, seq_count)
    grad_x, grad_dt, grad_bc_part, grad_x_taps, grad_bc_taps, grad_heads = mixer_backward(
        edges[3], x_width, to_true, narrow, bc_seq, grad_ssm, marks, seg_line, *mixer_args
    )
    grad_w_ff, grad_bc_part, ff_came = lax.optimization_barrier(
        (grad_w_ff, grad_bc_part, ff_came)
    )
    ff_cols = columns_to_owners(grad_w_ff)
    grad_bc = grad_bc_part[0].astype(f32)
    for bit in range(1, seq_count):
        grad_bc = grad_bc + swap_seq(grad_bc_part[bit], bit, seq_count).astype(f32)
    grad_bc = grad_bc.astype(bf16)
    ff_near, grad_bc = lax.optimization_barrier((ff_near, grad_bc))
    ff_kept, ff_arrived = scatter_second(ff_near, ff_came, seq_count)
    bc_zeros = jnp.zeros((length, bc_pad), bf16)
    grad_rest = jnp.concatenate([grad_x, grad_bc, bc_zeros, grad_dt], axis=1)
    grad_rest, out_grads, ff_cols = lax.optimization_barrier((grad_rest, out_grads, ff_cols))
    per_device = (seq_count, fsdp_count, -1)
    x_conv = lax.dynamic_update_slice_in_dim(
        jnp.zeros((dssm, taps_width), f32), grad_x_taps[:taps_width].T, rank * x_width, 0
    )
    conv_grads = jnp.concatenate([x_conv, grad_bc_taps[:taps_width].T], axis=0).reshape(per_device)
    head_grads = lax.dynamic_update_slice(
        jnp.zeros((3, heads_total), f32),
        grad_heads[:3, :dt_width],
        (jnp.int32(0), rank * dt_width),
    )
    head_grads = jnp.broadcast_to(
        head_grads.reshape(1, 1, -1), (seq_count, fsdp_count, 3 * heads_total)
    )
    smalls = jnp.concatenate([conv_grads, head_grads], axis=2)
    small_count = smalls.shape[2]
    small_columns = -(-small_count // row_piece)
    smalls = jnp.pad(smalls, ((0, 0), (0, 0), (0, small_columns * row_piece - small_count)))
    smalls = smalls.reshape(model_width, small_columns)
    small_first = x_width + bc_width + bc_pad + dt_width
    small_room = grad_rest.shape[1] - small_first - small_columns
    smalls = jnp.pad(smalls, ((0, 0), (small_first, small_room)))
    grad_w_rest = (weight_grad(normed, grad_rest) + smalls).astype(bf16)
    grad_rest, grad_w_rest, grad_z, grad_qkv, ff_arrived = lax.optimization_barrier(
        (grad_rest, grad_w_rest, grad_z, grad_qkv, ff_arrived)
    )
    grad_w_rest = lax.psum_scatter(
        grad_w_rest.reshape(seq_count, -1, grad_rest.shape[1]),
        "fsdp",
        scatter_dimension=1,
        tiled=True,
    )

    def first_product(first):
        rows = slice(first, first + near)
        return (
            input_grad(grad_rest[rows], narrow_w[:, edges[3] :])
            + input_grad(grad_z[rows], z_w)
            + input_grad(grad_qkv[rows], narrow_w[:, : edges[3]])
        )

    grad_normed_far = first_product(near).astype(bf16)
    zq_cols = columns_to_owners(grad_w_zq)
    grad_normed_far, grad_rest, grad_z, grad_qkv = lax.optimization_barrier(
        (grad_normed_far, grad_rest, grad_z, grad_qkv)
    )
    normed_came = scatter_first(grad_normed_far, seq_count)
    grad_normed_near, zq_cols = lax.optimization_barrier((first_product(0), zq_cols))
    normed_kept, normed_arrived = scatter_second(grad_normed_near, normed_came, seq_count)
    normed_kept, ff_kept, ff_cols, out_grads = lax.optimization_barrier(
        (normed_kept, ff_kept, ff_cols, out_grads)
    )
    layer_out = middle + scatter_last(ff_kept, ff_arrived)
    grad_normed = scatter_last(normed_kept, normed_arrived)
    _, scale1 = norm_forward(xin, gain1)
    grad_in_norm = norm_backward(xin, scale1, gain1, grad_normed)
    grad_in = (grad_middle + grad_in_norm).astype(bf16)
    grad_in, grad_w_rest = lax.optimization_barrier((grad_in, grad_w_rest))

    ff_cols = rank_parts(ff_cols)
    zq_cols = rank_parts(zq_cols)
    rest_cols = rank_parts(columns_to_owners(grad_w_rest))
    bc_first = x_width
    dt_first = bc_first + bc_width + bc_pad
    small = sum(part[:, small_first : small_first + small_columns] for part in rest_cols)
    small = small.reshape(-1)[:small_count]
    taps_total = taps_rows * taps_width
    out_conv = small[:taps_total]
    out_heads = small[taps_total:].reshape(3, heads_total)
    ranks_per_kv = group_size // heads_local
    kv_cols = []
    for first in (z_width + edges[1], z_width + edges[2]):
        for head in range(KV_HEADS):
            shares = zq_cols[head * ranks_per_kv : (head + 1) * ranks_per_kv]
            kv_cols.append(sum(share[:, first : first + HEAD_DIM] for share in shares))
    attn_rows = w_attn_out.shape[0]
    grad_query = side_by_side(zq_cols, z_width, q_width)
    grad_keyval = jnp.concatenate(kv_cols, axis=1)
    grad_gate_z = side_by_side(zq_cols, 0, z_width)
    grad_ssm_x = side_by_side(rest_cols, 0, x_width)
    grad_ssm_bc = side_by_side(rest_cols, bc_first, bc_width)
    grad_ssm_dt = side_by_side(rest_cols, dt_first, dt_width)
    grad_ff_gate = side_by_side(ff_cols, 0, ff_width)
    grad_ff_up = side_by_side(ff_cols, ff_width, ff_width)
    grad_attn_out = out_grads[:attn_rows].astype(f32)
    grad_ssm_out = out_grads[attn_rows:].astype(f32)

    def gain_grad(gain, *pairs):
        total = sum(jnp.sum(weight.astype(f32) * grad, axis=1) for weight, grad in pairs)
        return total / gain.astype(f32)

    out_gain1 = gain_grad(
        norm1_gain,
        (w_query, grad_query),
        (w_keyval, grad_keyval),
        (w_gate_z, grad_gate_z),
        (w_ssm_x, grad_ssm_x),
        (w_ssm_bc, grad_ssm_bc),
        (w_ssm_dt, grad_ssm_dt),
    )
    out_gain2 = gain_grad(norm2_gain, (w_ff_gate, grad_ff_gate), (w_ff_up, grad_ff_up))
    out_ssm_gain = gain_grad(ssm_gain, (w_ssm_out, grad_ssm_out))
    return (
        layer_out.astype(bf16).reshape(batch, block_len, model_width),
        grad_in.reshape(batch, block_len, model_width),
        out_gain1,
        grad_query,
        grad_keyval,
        grad_attn_out,
        grad_gate_z,
        grad_ssm_x,
        grad_ssm_bc,
        grad_ssm_dt,
        out_conv.reshape(taps_rows, taps_width),
        out_heads[0],
        out_heads[1],
        out_heads[2],
        out_ssm_gain,
        grad_ssm_out,
        out_gain2,
        grad_ff_gate,
        grad_ff_up,
        grad_w_down.astype(f32),
    )


def solution(mesh):
    in_specs = (
        P("fsdp", "seq", None),
        P("fsdp", None),
        P("fsdp", "seq", None),
        P(("seq", "fsdp")),
        P(("seq", "fsdp"), None),
        P(("seq", "fsdp"), None),
        P(("seq", "fsdp"), None),
        P(("seq", "fsdp"), None),
        P(("seq", "fsdp"), None),
        P(("seq", "fsdp"), None),
        P(("seq", "fsdp"), None),
        P(("seq", "fsdp"), None),
        P(),
        P(),
        P(),
        P(("seq", "fsdp")),
        P(("seq", "fsdp"), None),
        P(("seq", "fsdp")),
        P(("seq", "fsdp"), None),
        P(("seq", "fsdp"), None),
        P(("seq", "fsdp"), None),
    )
    out_specs = (
        P("fsdp", "seq", None),
        P("fsdp", "seq", None),
        P(("seq", "fsdp")),
        P(("seq", "fsdp"), None),
        P(("seq", "fsdp"), None),
        P(("seq", "fsdp"), None),
        P(("seq", "fsdp"), None),
        P(("seq", "fsdp"), None),
        P(("seq", "fsdp"), None),
        P(("seq", "fsdp"), None),
        P(("seq", "fsdp"), None),
        P(),
        P(),
        P(),
        P(("seq", "fsdp")),
        P(("seq", "fsdp"), None),
        P(("seq", "fsdp")),
        P(("seq", "fsdp"), None),
        P(("seq", "fsdp"), None),
        P(("seq", "fsdp"), None),
    )
    step = functools.partial(body, mesh.shape["seq"], mesh.shape["fsdp"])
    return jax.shard_map(step, mesh=mesh, in_specs=in_specs, out_specs=out_specs, check_vma=False)
```

```python
import functools

import jax
import jax.numpy as jnp
import numpy as np
from jax import lax
from jax.experimental import pallas as pl
from jax.experimental.layout import Layout, with_layout_constraint
from jax.experimental.pallas import tpu as pltpu
from jax.sharding import PartitionSpec as P

HEADS = 8
KV_HEADS = 2
HEAD_DIM = 128
SSM_DIM = 64
STATE = 256
BLOCK = 256
LANES = 128
MIB = 1024 * 1024


epsilon = 1e-05
rope_base = 10000.0
masked_score = -1e30


def mat_product(left_op, right_op):
    return jnp.dot(left_op, right_op, preferred_element_type=jnp.float32)


def weight_grad(left_op, right_op):
    return lax.dot_general(
        left_op, right_op, (((0,), (0,)), ((), ())), preferred_element_type=jnp.float32
    )


def input_grad(grad_rows, weights):
    return lax.dot_general(
        grad_rows, weights, (((1,), (1,)), ((), ())), preferred_element_type=jnp.float32
    )


def dot_plain(left_op, right_op):
    return jnp.dot(left_op, right_op, preferred_element_type=jnp.float32)


def dot_ones(left_op, ones, terms):
    total = None
    for _ in range(terms):
        part = left_op.astype(jnp.bfloat16)
        product = dot_plain(part, ones)
        total = product if total is None else total + product
        left_op = left_op - part.astype(jnp.float32)
    return total


def ones_dot(ones, right_op, terms):
    total = None
    for _ in range(terms):
        part = right_op.astype(jnp.bfloat16)
        product = dot_plain(ones, part)
        total = product if total is None else total + product
        right_op = right_op - part.astype(jnp.float32)
    return total


def logistic(values):
    return 0.5 * jnp.tanh(0.5 * values) + 0.5


def dot_rows(left_op, right_op):
    return lax.dot_general(
        left_op, right_op, (((1,), (1,)), ((), ())), preferred_element_type=jnp.float32
    )


def dot_columns(left_op, right_op):
    return lax.dot_general(
        left_op, right_op, (((0,), (0,)), ((), ())), preferred_element_type=jnp.float32
    )


def iota_of(shape, axis):
    return lax.broadcasted_iota(jnp.int32, shape, axis)


def allowed_block(marks_ref, seg_row_ref, row_start, col_start, columns, diagonal):
    seg_col = marks_ref[pl.ds(row_start, BLOCK), 0:1]
    seg_row = seg_row_ref[0:1, pl.ds(col_start, columns)]
    same = seg_col == seg_row
    if diagonal:
        row_pos = row_start + iota_of((BLOCK, columns), 0)
        col_pos = col_start + iota_of((BLOCK, columns), 1)
        same = same & (row_pos >= col_pos)
    return same


def store_relative(order_ref, target, piece, row_start, column, values):
    rows, width = values.shape
    for part in range(rows // piece):
        place = row_start // piece + part
        start = pl.multiple_of(order_ref[place] * piece, piece)
        target[pl.ds(start, piece), column : column + width] = values[
            part * piece : (part + 1) * piece
        ]


def attention_load(pieces, order_ref, narrow_ref, cos_ref, sin_ref, q_s, k_s, v_s, q_width):
    length = narrow_ref.shape[0]
    piece = length // pieces
    for place in range(pieces):
        start = pl.multiple_of(order_ref[place] * piece, piece)
        rows = slice(place * piece, (place + 1) * piece)
        cosine = cos_ref[rows, :]
        sine = sin_ref[rows, :]
        for column in range(0, q_width + HEAD_DIM, HEAD_DIM):
            part = narrow_ref[pl.ds(start, piece), column : column + HEAD_DIM].astype(jnp.float32)
            turned = part * cosine + pltpu.roll(part, HEAD_DIM // 2, 1) * sine
            if column < q_width:
                q_s[rows, column : column + HEAD_DIM] = turned.astype(jnp.bfloat16)
            else:
                k_s[rows, :] = turned.astype(jnp.bfloat16)
        v_s[rows, :] = narrow_ref[
            pl.ds(start, piece), q_width + HEAD_DIM : q_width + 2 * HEAD_DIM
        ]


def attention_forward_kernel(
    q_width,
    pieces,
    order_ref,
    narrow_ref,
    cos_ref,
    sin_ref,
    marks_ref,
    seg_row_ref,
    out_ref,
    lse_ref,
    q_s,
    k_s,
    v_s,
):
    length = narrow_ref.shape[0]
    piece = length // pieces
    attention_load(pieces, order_ref, narrow_ref, cos_ref, sin_ref, q_s, k_s, v_s, q_width)
    for block in range(length // BLOCK):
        start = block * BLOCK
        columns = start + BLOCK
        allowed = allowed_block(marks_ref, seg_row_ref, start, 0, columns, True)
        for head in range(q_width // HEAD_DIM):
            lanes = slice(head * HEAD_DIM, (head + 1) * HEAD_DIM)
            scores = dot_rows(q_s[start : start + BLOCK, lanes], k_s[0:columns, :])
            scores = jnp.where(allowed, scores * HEAD_DIM ** (-0.5), masked_score)
            row_max = jnp.max(scores, axis=1, keepdims=True)
            exponent = jnp.exp(scores - row_max)
            total = jnp.sum(exponent, axis=1, keepdims=True)
            probs = (exponent * (1.0 / total)).astype(jnp.bfloat16)
            mixed = dot_plain(probs, v_s[0:columns, :]).astype(jnp.bfloat16)
            store_relative(order_ref, out_ref, piece, start, head * HEAD_DIM, mixed)
            lse_ref[start : start + BLOCK, head : head + 1] = row_max + jnp.log(total)


def attention_backward_kernel(
    q_width,
    pieces,
    order_ref,
    narrow_ref,
    grad_ref,
    cos_ref,
    sin_ref,
    marks_ref,
    seg_row_ref,
    lse_ref,
    out_ref,
    q_s,
    k_s,
    v_s,
    g_s,
    dk_s,
    dv_s,
):
    length = narrow_ref.shape[0]
    piece = length // pieces
    scale = HEAD_DIM ** (-0.5)
    attention_load(pieces, order_ref, narrow_ref, cos_ref, sin_ref, q_s, k_s, v_s, q_width)
    for place in range(pieces):
        rows = slice(place * piece, (place + 1) * piece)
        start = pl.multiple_of(order_ref[place] * piece, piece)
        g_s[rows, :] = grad_ref[pl.ds(start, piece), 0:q_width]
    dk_s[...] = jnp.zeros_like(dk_s)
    dv_s[...] = jnp.zeros_like(dv_s)
    for block in range(length // BLOCK):
        start = block * BLOCK
        columns = start + BLOCK
        rows = slice(start, columns)
        cosine = cos_ref[rows, :]
        sine = sin_ref[rows, :]
        allowed = allowed_block(marks_ref, seg_row_ref, start, 0, columns, True)
        for head in range(q_width // HEAD_DIM):
            lanes = slice(head * HEAD_DIM, (head + 1) * HEAD_DIM)
            q_blk = q_s[rows, lanes]
            g_blk = g_s[rows, lanes]
            scores = dot_rows(q_blk, k_s[0:columns, :])
            scores = jnp.where(allowed, scores * scale, masked_score)
            probs = jnp.exp(scores - lse_ref[rows, head : head + 1])
            grad_probs = dot_rows(g_blk, v_s[0:columns, :])
            inner = jnp.sum(grad_probs * probs, axis=1, keepdims=True)
            grad_scores = (probs * (grad_probs - inner)).astype(jnp.bfloat16)
            grad_q = dot_plain(grad_scores, k_s[0:columns, :]) * scale
            grad_q = grad_q * cosine - pltpu.roll(grad_q, HEAD_DIM // 2, 1) * sine
            store_relative(
                order_ref, out_ref, piece, start, head * HEAD_DIM, grad_q.astype(jnp.bfloat16)
            )
            dk_s[0:columns, :] += dot_columns(grad_scores, q_blk)
            dv_s[0:columns, :] += dot_columns(probs.astype(jnp.bfloat16), g_blk)
    for block in range(length // BLOCK):
        start = block * BLOCK
        rows = slice(start, start + BLOCK)
        grad_k = dk_s[rows, :] * scale
        grad_k = grad_k * cos_ref[rows, :] - pltpu.roll(grad_k, HEAD_DIM // 2, 1) * sin_ref[rows, :]
        store_relative(order_ref, out_ref, piece, start, q_width, grad_k.astype(jnp.bfloat16))
        store_relative(
            order_ref,
            out_ref,
            piece,
            start,
            q_width + HEAD_DIM,
            dv_s[rows, :].astype(jnp.bfloat16),
        )


def head_spread(width):
    heads = iota_of((LANES, width), 0)
    return (iota_of((LANES, width), 1) // SSM_DIM == heads).astype(jnp.float32).astype(jnp.bfloat16)


def head_gather(width):
    heads = iota_of((width, LANES), 1)
    return (iota_of((width, LANES), 0) // SSM_DIM == heads).astype(jnp.float32).astype(jnp.bfloat16)


def triangle(lower):
    rows = iota_of((BLOCK, BLOCK), 0)
    columns = iota_of((BLOCK, BLOCK), 1)
    return (rows >= columns if lower else rows <= columns).astype(jnp.float32).astype(jnp.bfloat16)


def softplus(values):
    return jnp.maximum(values, 0.0) + jnp.log1p(jnp.exp(-jnp.abs(values)))


def mark_columns(marks_ref, row_start, first):
    return [
        jnp.broadcast_to(marks_ref[pl.ds(row_start, BLOCK), first + tap : first + tap + 1], (BLOCK, LANES))
        for tap in range(3)
    ]


def conv_window(pad_ref, taps_ref, before, row_start, column):
    total = jnp.broadcast_to(taps_ref[4:5, column : column + LANES], (BLOCK, LANES))
    shifted = []
    for tap in range(4):
        rows = pad_ref[column // LANES, pl.ds(row_start + 5 + tap, BLOCK), :]
        if tap < 3:
            rows = rows * before[tap]
        shifted.append(rows)
        total = total + rows * taps_ref[tap : tap + 1, column : column + LANES]
    return total, shifted


def mixer_load(
    x_column,
    order_ref,
    narrow_ref,
    bc_ref,
    marks_ref,
    x_taps_ref,
    bc_taps_ref,
    heads_ref,
    x_pad,
    bc_pad,
    dt_s,
    a_s,
    a_row_s,
    a_wide,
    mixed_s,
    scaled_s,
    bc_s,
):
    length, width = mixed_s.shape
    count, _, bc_width = bc_ref.shape
    pieces = 2 * count
    piece = length // pieces
    dt_column = narrow_ref.shape[1] - LANES
    x_pad[:, 0:8, :] = jnp.zeros((width // LANES, 8, LANES), jnp.float32)
    bc_pad[:, 0:8, :] = jnp.zeros((2 * STATE // LANES, 8, LANES), jnp.float32)
    for place in range(pieces):
        start = pl.multiple_of(order_ref[place] * piece, piece)
        rows = slice(place * piece, (place + 1) * piece)
        padded = slice(8 + place * piece, 8 + (place + 1) * piece)
        for chunk in range(width // LANES):
            column = x_column + chunk * LANES
            x_pad[chunk, padded, :] = narrow_ref[
                pl.ds(start, piece), column : column + LANES
            ].astype(jnp.float32)
        for owner in range(count):
            source = order_ref[pieces + owner]
            owner_start = pl.multiple_of(
                order_ref[pieces + count + owner * pieces + place] * piece, piece
            )
            lane = owner * bc_width % LANES
            bc_pad[owner * bc_width // LANES, padded, lane : lane + bc_width] = bc_ref[
                source, pl.ds(owner_start, piece), :
            ].astype(jnp.float32)
        dt_s[rows, :] = narrow_ref[pl.ds(start, piece), dt_column : dt_column + LANES].astype(
            jnp.float32
        )
    spread = head_spread(width)
    lower = triangle(True)
    rate = jnp.exp(heads_ref[0:1, :])
    bias = heads_ref[1:2, :]

    def one_block(block, carry):
        start = pl.multiple_of(block * BLOCK, BLOCK)
        rows = pl.ds(start, BLOCK)
        step = softplus(dt_s[rows, :] + bias)
        decay_sum = ones_dot(lower, step * rate, 3) + carry
        a_s[rows, :] = decay_sum
        a_row_s[block] = decay_sum.T
        a_wide[rows, :] = dot_ones(decay_sum, spread, 3)
        step_wide = dot_ones(step, spread, 2)
        before = mark_columns(marks_ref, start, 1)
        for column in range(0, width, LANES):
            lanes = slice(column, column + LANES)
            total, _ = conv_window(x_pad, x_taps_ref, before, start, column)
            mixed = total * logistic(total)
            mixed_s[rows, lanes] = mixed
            scaled_s[rows, lanes] = (mixed * step_wide[:, lanes]).astype(jnp.bfloat16)
        for column in range(0, 2 * STATE, LANES):
            total, _ = conv_window(bc_pad, bc_taps_ref, before, start, column)
            bc_s[rows, column : column + LANES] = (total * logistic(total)).astype(
                jnp.bfloat16
            )
        return decay_sum[BLOCK - 1 : BLOCK, :]

    lax.fori_loop(0, length // BLOCK, one_block, jnp.zeros((1, LANES), jnp.float32))


def half_lanes(values, half):
    lane = iota_of(values.shape, 1)
    keep = lane < SSM_DIM if half == 0 else lane >= SSM_DIM
    return jnp.where(keep, values, jnp.zeros_like(values))


def diagonal_decay(a_s, a_row_s, block, start, head):
    gap = a_row_s[block, head : head + 1, :] - a_s[pl.ds(start, BLOCK), head : head + 1]
    return jnp.exp(jnp.minimum(gap, 0.0))


def mixer_forward_kernel(
    x_column,
    order_ref,
    narrow_ref,
    bc_ref,
    marks_ref,
    seg_row_ref,
    x_taps_ref,
    bc_taps_ref,
    heads_ref,
    out_ref,
    x_pad,
    bc_pad,
    dt_s,
    a_s,
    a_row_s,
    a_wide,
    mixed_s,
    scaled_s,
    bc_s,
    weight_s,
    inter_s,
    total_s,
):
    length, width = mixed_s.shape
    piece = length // (2 * bc_ref.shape[0])
    mixer_load(
        x_column,
        order_ref,
        narrow_ref,
        bc_ref,
        marks_ref,
        x_taps_ref,
        bc_taps_ref,
        heads_ref,
        x_pad,
        bc_pad,
        dt_s,
        a_s,
        a_row_s,
        a_wide,
        mixed_s,
        scaled_s,
        bc_s,
    )
    skip_wide = dot_ones(jnp.broadcast_to(heads_ref[2:3, :], (8, LANES)), head_spread(width), 3)

    def one_block(block, _):
        start = pl.multiple_of(block * BLOCK, BLOCK)
        rows = pl.ds(start, BLOCK)
        out_c = bc_s[rows, STATE : 2 * STATE]
        total_s[...] = jnp.zeros_like(total_s)
        first = a_wide[pl.ds(start, 8), :][0:1]

        def earlier(other, _):
            col_start = pl.multiple_of(other * BLOCK, BLOCK)
            columns = pl.ds(col_start, BLOCK)
            allowed = allowed_block(marks_ref, seg_row_ref, start, col_start, BLOCK, False)
            inter = dot_rows(out_c, bc_s[columns, 0:STATE])
            inter = jnp.where(allowed, inter, 0.0).astype(jnp.bfloat16)
            faded = scaled_s[columns, :].astype(jnp.float32) * jnp.exp(a_wide[columns, :] - first)
            total_s[...] += dot_plain(inter, faded.astype(jnp.bfloat16))
            return 0

        lax.fori_loop(0, block, earlier, 0)
        allowed = allowed_block(marks_ref, seg_row_ref, start, start, BLOCK, True)
        inter_s[...] = jnp.where(allowed, dot_rows(out_c, bc_s[rows, 0:STATE]), 0.0)
        for column in range(0, width, LANES):
            lanes = slice(column, column + LANES)
            scaled = scaled_s[rows, lanes]
            mixed = total_s[:, lanes] * jnp.exp(first[:, lanes] - a_wide[rows, lanes])
            for half in range(2):
                head = column // SSM_DIM + half
                decay = diagonal_decay(a_s, a_row_s, block, start, head)
                weights = (inter_s[...] * decay).astype(jnp.bfloat16)
                mixed = mixed + dot_plain(weights, half_lanes(scaled, half))
            mixed = mixed + skip_wide[0:1, lanes] * mixed_s[rows, lanes]
            weight_s[:, lanes] = mixed.astype(jnp.bfloat16)
        for part in range(BLOCK // piece):
            place = block * (BLOCK // piece) + part
            target = pl.multiple_of(order_ref[place] * piece, piece)
            out_ref[pl.ds(target, piece), :] = weight_s[part * piece : (part + 1) * piece, :]
        return 0

    lax.fori_loop(0, length // BLOCK, one_block, 0)


def mixer_backward_kernel(
    x_column,
    order_ref,
    narrow_ref,
    bc_ref,
    grad_ref,
    marks_ref,
    seg_row_ref,
    x_taps_ref,
    bc_taps_ref,
    heads_ref,
    gx_ref,
    gdt_ref,
    gbc_ref,
    gx_taps_ref,
    gbc_taps_ref,
    gheads_ref,
    x_pad,
    bc_pad,
    dt_s,
    a_s,
    a_row_s,
    a_wide,
    mixed_s,
    scaled_s,
    bc_s,
    grad_s,
    gscaled_s,
    gap_s,
    gbc_s,
    inter_s,
    gover_s,
    faded_s,
    gfaded_s,
    fade_s,
    edge_s,
    ahead_s,
    low_s,
):
    length, width = mixed_s.shape
    count, _, bc_width = bc_ref.shape
    pieces = 2 * count
    piece = length // pieces
    blocks = length // BLOCK
    mixer_load(
        x_column,
        order_ref,
        narrow_ref,
        bc_ref,
        marks_ref,
        x_taps_ref,
        bc_taps_ref,
        heads_ref,
        x_pad,
        bc_pad,
        dt_s,
        a_s,
        a_row_s,
        a_wide,
        mixed_s,
        scaled_s,
        bc_s,
    )
    for place in range(pieces):
        source = pl.multiple_of(order_ref[place] * piece, piece)
        grad_s[place * piece : (place + 1) * piece, :] = grad_ref[pl.ds(source, piece), :]
    gscaled_s[...] = jnp.zeros_like(gscaled_s)
    gap_s[...] = jnp.zeros_like(gap_s)
    gbc_s[...] = jnp.zeros_like(gbc_s)

    def one_block(block, _):
        start = pl.multiple_of(block * BLOCK, BLOCK)
        rows = pl.ds(start, BLOCK)
        out_c = bc_s[rows, STATE : 2 * STATE]
        allowed = allowed_block(marks_ref, seg_row_ref, start, start, BLOCK, True)
        inter_s[...] = jnp.where(allowed, dot_rows(out_c, bc_s[rows, 0:STATE]), 0.0)
        gover_s[...] = jnp.zeros_like(gover_s)
        for column in range(0, width, LANES):
            lanes = slice(column, column + LANES)
            scaled = scaled_s[rows, lanes]
            grad = grad_s[rows, lanes]
            row_side = jnp.zeros((BLOCK, LANES), jnp.float32)
            col_side = jnp.zeros((BLOCK, LANES), jnp.float32)
            for half in range(2):
                head = column // SSM_DIM + half
                decay = diagonal_decay(a_s, a_row_s, block, start, head)
                weights = (inter_s[...] * decay).astype(jnp.bfloat16)
                scaled_half = half_lanes(scaled, half)
                gover_s[...] += dot_rows(grad, scaled_half) * decay
                row_side = row_side + dot_plain(weights, scaled_half)
                col_side = col_side + dot_columns(weights, half_lanes(grad, half))
            gscaled_s[rows, lanes] += col_side
            gap_s[rows, lanes] += scaled.astype(jnp.float32) * col_side - grad.astype(
                jnp.float32
            ) * row_side
        gover = jnp.where(allowed, gover_s[...], 0.0).astype(jnp.bfloat16)
        gbc_s[rows, STATE : 2 * STATE] += dot_plain(gover, bc_s[rows, 0:STATE])
        gbc_s[rows, 0:STATE] += dot_columns(gover, out_c)
        first = a_wide[pl.ds(start, 8), :][0:1]
        gfaded_s[...] = (
            grad_s[rows, :].astype(jnp.float32) * jnp.exp(first - a_wide[rows, :])
        ).astype(jnp.bfloat16)

        def earlier(other, _):
            col_start = pl.multiple_of(other * BLOCK, BLOCK)
            columns = pl.ds(col_start, BLOCK)
            same = allowed_block(marks_ref, seg_row_ref, start, col_start, BLOCK, False)
            in_b = bc_s[columns, 0:STATE]
            inter = jnp.where(same, dot_rows(out_c, in_b), 0.0).astype(jnp.bfloat16)
            fade_s[...] = jnp.exp(a_wide[columns, :] - first)
            faded_s[...] = (scaled_s[columns, :].astype(jnp.float32) * fade_s[...]).astype(
                jnp.bfloat16
            )
            over = dot_rows(gfaded_s[...], faded_s[...])
            over = jnp.where(same, over, 0.0).astype(jnp.bfloat16)
            gbc_s[rows, STATE : 2 * STATE] += dot_plain(over, in_b)
            gbc_s[columns, 0:STATE] += dot_columns(over, out_c)
            gap_s[rows, :] -= gfaded_s[...].astype(jnp.float32) * dot_plain(inter, faded_s[...])
            col_side = dot_columns(inter, gfaded_s[...])
            gap_s[columns, :] += faded_s[...].astype(jnp.float32) * col_side
            gscaled_s[columns, :] += fade_s[...] * col_side
            return 0

        lax.fori_loop(0, block, earlier, 0)
        return 0

    lax.fori_loop(0, blocks, one_block, 0)

    spread = head_spread(width)
    gather = head_gather(width)
    upper = triangle(False)
    rate = jnp.exp(heads_ref[0:1, :])
    bias = heads_ref[1:2, :]
    skip_wide = dot_ones(jnp.broadcast_to(heads_ref[2:3, :], (8, LANES)), spread, 3)
    gx_taps_ref[...] = jnp.zeros_like(gx_taps_ref)
    gbc_taps_ref[...] = jnp.zeros_like(gbc_taps_ref)
    gheads_ref[...] = jnp.zeros_like(gheads_ref)
    edge_s[...] = jnp.zeros_like(edge_s)

    def conv_back(pad_ref, taps_ref, gtaps_ref, before, after, start, column, shift, gmixed):
        total, shifted = conv_window(pad_ref, taps_ref, before, start, column)
        sig = logistic(total)
        gtotal = gmixed * sig * (1.0 + total * (1.0 - sig))
        lanes = slice(column, column + LANES)
        for tap in range(4):
            gtaps_ref[tap : tap + 1, lanes] += jnp.sum(gtotal * shifted[tap], axis=0, keepdims=True)
        gtaps_ref[4:5, lanes] += jnp.sum(gtotal, axis=0, keepdims=True)
        wide = slice(shift + column, shift + column + LANES)
        chunk = (shift + column) // LANES
        ahead_s[chunk, 0:BLOCK, :] = gtotal
        ahead_s[chunk, BLOCK : BLOCK + 8, :] = edge_s[:, wide]
        edge_s[:, wide] = gtotal[0:8]
        result = gtotal * taps_ref[3:4, lanes]
        for tap in range(3):
            ahead = ahead_s[chunk, 3 - tap : 3 - tap + BLOCK, :] * after[tap]
            result = result + ahead * taps_ref[tap : tap + 1, lanes]
        return result.astype(jnp.bfloat16)

    def last_block(index, carry):
        block = blocks - 1 - index
        start = pl.multiple_of(block * BLOCK, BLOCK)
        rows = pl.ds(start, BLOCK)
        raw = dt_s[rows, :] + bias
        step = softplus(raw)
        gsum = ones_dot(upper, dot_ones(gap_s[rows, :], gather, 2), 3) + carry
        gstep = dot_ones(gscaled_s[rows, :] * mixed_s[rows, :], gather, 2) + gsum * rate
        graw = gstep * jax.nn.sigmoid(raw)
        gheads_ref[0:1, :] += jnp.sum(gsum * step * rate, axis=0, keepdims=True)
        gheads_ref[1:2, :] += jnp.sum(graw, axis=0, keepdims=True)
        low_s[:, width : width + LANES] = graw.astype(jnp.bfloat16)
        step_wide = dot_ones(step, spread, 2)
        skip_parts = []
        before = mark_columns(marks_ref, start, 1)
        after = mark_columns(marks_ref, start, 4)
        for column in range(0, width, LANES):
            lanes = slice(column, column + LANES)
            grad = grad_s[rows, lanes].astype(jnp.float32)
            skip_parts.append(jnp.sum(grad * mixed_s[rows, lanes], axis=0, keepdims=True))
            gmixed = skip_wide[0:1, lanes] * grad + gscaled_s[rows, lanes] * step_wide[:, lanes]
            low_s[:, lanes] = conv_back(
                x_pad, x_taps_ref, gx_taps_ref, before, after, start, column, 0, gmixed
            )
        skip_row = jnp.broadcast_to(jnp.concatenate(skip_parts, axis=1), (8, width))
        gheads_ref[2:3, :] += dot_ones(skip_row, gather, 2)[0:1]
        for column in range(0, 2 * STATE, LANES):
            lanes = slice(column, column + LANES)
            low_s[:, width + LANES + column : width + 2 * LANES + column] = conv_back(
                bc_pad,
                bc_taps_ref,
                gbc_taps_ref,
                before,
                after,
                start,
                column,
                width,
                gbc_s[rows, lanes],
            )
        for part in range(BLOCK // piece):
            place = block * (BLOCK // piece) + part
            target = pl.multiple_of(order_ref[place] * piece, piece)
            gx_ref[pl.ds(target, piece), :] = low_s[part * piece : (part + 1) * piece, 0:width]
            gdt_ref[pl.ds(target, piece), :] = low_s[
                part * piece : (part + 1) * piece, width : width + LANES
            ]
            for owner in range(count):
                first = width + LANES + owner * bc_width
                owner_start = pl.multiple_of(
                    order_ref[pieces + count + owner * pieces + place] * piece, piece
                )
                gbc_ref[order_ref[pieces + owner], pl.ds(owner_start, piece), :] = low_s[
                    part * piece : (part + 1) * piece, first : first + bc_width
                ]
        return gsum[0:1, :]

    lax.fori_loop(0, blocks, last_block, jnp.zeros((1, LANES), jnp.float32))


def local_call(kernel, outs, scratch, flops, vmem, operands):
    moved = sum(part.size * part.dtype.itemsize for part in operands)
    moved += sum(part.size * part.dtype.itemsize for part in outs)
    return pl.pallas_call(
        kernel,
        out_shape=outs,
        in_specs=[pl.BlockSpec(memory_space=pltpu.SMEM)]
        + [pl.BlockSpec(memory_space=pltpu.VMEM)] * (len(operands) - 1),
        out_specs=[pl.BlockSpec(memory_space=pltpu.VMEM)] * len(outs),
        scratch_shapes=scratch,
        compiler_params=pltpu.CompilerParams(vmem_limit_bytes=vmem * MIB),
        cost_estimate=pl.CostEstimate(flops=flops, bytes_accessed=moved, transcendentals=0),
    )(*operands)


def array_of(shape, dtype):
    return jax.ShapeDtypeStruct(shape, dtype)


def attention_forward(q_width, pieces, order, narrow, cosine, sine, marks, seg_row):
    length = narrow.shape[0]
    low = jnp.bfloat16
    return local_call(
        functools.partial(attention_forward_kernel, q_width, pieces),
        [array_of((length, q_width), low), array_of((length, 8), jnp.float32)],
        [
            pltpu.VMEM((length, q_width), low),
            pltpu.VMEM((length, HEAD_DIM), low),
            pltpu.VMEM((length, HEAD_DIM), low),
        ],
        36 * length * length * q_width,
        22,
        (order, narrow, cosine, sine, marks, seg_row),
    )


def attention_backward(q_width, pieces, order, narrow, grad, cosine, sine, marks, seg_row, lse):
    length = narrow.shape[0]
    low = jnp.bfloat16
    return local_call(
        functools.partial(attention_backward_kernel, q_width, pieces),
        [array_of((length, q_width + 2 * HEAD_DIM), low)],
        [
            pltpu.VMEM((length, q_width), low),
            pltpu.VMEM((length, HEAD_DIM), low),
            pltpu.VMEM((length, HEAD_DIM), low),
            pltpu.VMEM((length, q_width), low),
            pltpu.VMEM((length, HEAD_DIM), jnp.float32),
            pltpu.VMEM((length, HEAD_DIM), jnp.float32),
        ],
        44 * length * length * q_width,
        24,
        (order, narrow, grad, cosine, sine, marks, seg_row, lse),
    )[0]


def mixer_scratch(length, width):
    low, full = jnp.bfloat16, jnp.float32
    return [
        pltpu.VMEM((width // LANES, length + 8, LANES), full),
        pltpu.VMEM((2 * STATE // LANES, length + 8, LANES), full),
        pltpu.VMEM((length, LANES), full),
        pltpu.VMEM((length, LANES), full),
        pltpu.VMEM((length // BLOCK, LANES, BLOCK), full),
        pltpu.VMEM((length, width), full),
        pltpu.VMEM((length, width), full),
        pltpu.VMEM((length, width), low),
        pltpu.VMEM((length, 2 * STATE), low),
    ]


def mixer_forward(x_column, width, order, narrow, bc, marks, seg_row, x_taps, bc_taps, heads):
    length = narrow.shape[0]
    low, full = jnp.bfloat16, jnp.float32
    return local_call(
        functools.partial(mixer_forward_kernel, x_column),
        [array_of((length, width), low)],
        mixer_scratch(length, width)
        + [
            pltpu.VMEM((BLOCK, width), low),
            pltpu.VMEM((BLOCK, BLOCK), full),
            pltpu.VMEM((BLOCK, width), full),
        ],
        28 * length * length * width,
        34,
        (order, narrow, bc, marks, seg_row, x_taps, bc_taps, heads),
    )[0]


def mixer_backward(x_column, width, order, narrow, bc, grad, marks, seg_row, x_taps, bc_taps, heads):
    length = narrow.shape[0]
    low, full = jnp.bfloat16, jnp.float32
    return local_call(
        functools.partial(mixer_backward_kernel, x_column),
        [
            array_of((length, width), low),
            array_of((length, LANES), low),
            array_of(bc.shape, low),
            array_of((8, width), full),
            array_of((8, 2 * STATE), full),
            array_of((8, LANES), full),
        ],
        mixer_scratch(length, width)
        + [
            pltpu.VMEM((length, width), low),
            pltpu.VMEM((length, width), full),
            pltpu.VMEM((length, width), full),
            pltpu.VMEM((length, 2 * STATE), full),
            pltpu.VMEM((BLOCK, BLOCK), full),
            pltpu.VMEM((BLOCK, BLOCK), full),
            pltpu.VMEM((BLOCK, width), low),
            pltpu.VMEM((BLOCK, width), low),
            pltpu.VMEM((BLOCK, width), full),
            pltpu.VMEM((8, width + 2 * STATE), full),
            pltpu.VMEM(((width + 2 * STATE) // LANES, BLOCK + 8, LANES), full),
            pltpu.VMEM((BLOCK, width + LANES + 2 * STATE), low),
        ],
        60 * length * length * width,
        50,
        (order, narrow, bc, grad, marks, seg_row, x_taps, bc_taps, heads),
    )


def document_marks(seg_row):
    length = seg_row.shape[0]
    before = jnp.pad(seg_row, (3, 0), constant_values=-1)
    after = jnp.pad(seg_row, (0, 3), constant_values=-1)
    columns = [seg_row.astype(jnp.float32)]
    for tap in range(3):
        columns.append((before[tap : tap + length] == seg_row).astype(jnp.float32))
    for tap in range(3):
        columns.append((after[3 - tap : 3 - tap + length] == seg_row).astype(jnp.float32))
    columns.append(jnp.zeros((length,), jnp.float32))
    return jnp.stack(columns, axis=1)


def rope_wide(length):
    half_dim = HEAD_DIM // 2
    frequency = rope_base ** (-jnp.arange(half_dim, dtype=jnp.float32) / half_dim)
    angles = jnp.arange(length, dtype=jnp.float32)[:, None] * frequency[None, :]
    cosine, sine = jnp.cos(angles), jnp.sin(angles)
    return jnp.concatenate([cosine, cosine], axis=1), jnp.concatenate([-sine, sine], axis=1)


def swap_seq(value, bit, count):
    return lax.ppermute(value, "seq", [(place, place ^ bit) for place in range(count)])


def seq_bits(count):
    bits = []
    bit = 1
    while bit < count:
        bits.append(bit)
        bit *= 2
    return bits


def block_order(bits):
    order = [0]
    for bit in bits:
        order = order + [place ^ bit for place in order]
    return order


def relative_order(count):
    bits = seq_bits(count)
    upper = [(0, block) for block in block_order(bits)]
    lower = [(1, block) for block in block_order(bits[::-1])]
    near = count // 2
    return upper[:near] + lower[:near] + upper[near:] + lower[near:]


def gather_first(rows, count):
    half = rows.shape[0] // 2
    bits = seq_bits(count)
    pieces = []
    for piece, order in ((rows[:half], bits), (rows[half:], bits[::-1])):
        for bit in order[:-1]:
            piece = jnp.concatenate([piece, swap_seq(piece, bit, count)], axis=0)
        pieces.append(piece)
    return pieces


def gather_last(pieces, count):
    bits = seq_bits(count)
    far = [swap_seq(piece, bit, count) for piece, bit in zip(pieces, (bits[-1], bits[0]))]
    return jnp.concatenate(pieces, axis=0), jnp.concatenate(far, axis=0)


def rows_gather(rows, count):
    return gather_last(gather_first(rows, count), count)


def scatter_first(far, count):
    half = far.shape[0] // 2
    bits = seq_bits(count)
    far = far.astype(jnp.bfloat16)
    return [
        swap_seq(far[first : first + half], order[-1], count)
        for first, order in ((0, bits), (half, bits[::-1]))
    ]


def scatter_second(near, came, count):
    half = near.shape[0] // 2
    bits = seq_bits(count)
    kept, arrived = [], []
    for first, order, add in ((0, bits, came[0]), (half, bits[::-1], came[1])):
        piece = near[first : first + half]
        for bit in order[:-1][::-1]:
            piece = piece + add.astype(jnp.float32)
            keep = piece.shape[0] // 2
            add = swap_seq(piece[keep:].astype(jnp.bfloat16), bit, count)
            piece = piece[:keep]
        kept.append(piece)
        arrived.append(add)
    return kept, arrived


def scatter_last(kept, arrived):
    return jnp.concatenate(
        [piece + add.astype(jnp.float32) for piece, add in zip(kept, arrived)], axis=0
    )


def rows_scatter(near, far, count):
    came = scatter_first(far, count)
    return scatter_last(*scatter_second(near, came, count))


def row_tables(count):
    order = relative_order(count)

    def places(rank):
        return [order.index((half, block ^ rank)) for block in range(count) for half in range(2)]

    everyone = [place for rank in range(count) for place in places(rank)]
    return np.asarray(
        [
            places(rank) + [other ^ rank for other in range(count)] + everyone
            for rank in range(count)
        ],
        np.int32,
    )


def seq_pieces(value, count):
    return [value] + [swap_seq(value, bit, count) for bit in range(1, count)]


def seq_sum(value, count):
    order = relative_order(count)
    total = value.reshape(2 * count, -1)
    for bit in range(1, count):
        came = swap_seq(value, bit, count).reshape(2 * count, -1)
        places = [order.index((half, block ^ bit)) for half, block in order]
        total = total + jnp.concatenate([came[place : place + 1] for place in places])
    return total.reshape(-1)


def norm_forward(rows, gain):
    scale = lax.rsqrt(jnp.mean(rows * rows, axis=-1, keepdims=True) + epsilon)
    return ((rows * scale * gain).astype(jnp.bfloat16), scale)


def norm_backward(rows, scale, gain, cotangent):
    weighted = cotangent * gain
    inner = jnp.mean(rows * weighted, axis=-1, keepdims=True)
    grad_rows = scale * weighted - rows * (scale * scale * scale * inner)
    return grad_rows


def columns_exchange(blocks):
    return lax.all_to_all(blocks, "seq", split_axis=0, concat_axis=0, tiled=True)


def rows_of_all(piece):
    return lax.all_gather(piece, "fsdp", axis=1, tiled=True).reshape(-1, piece.shape[2])


def columns_gather(blocks):
    return rows_of_all(columns_exchange(blocks))


def columns_to_owners(blocks):
    blocks = with_layout_constraint(blocks, Layout(major_to_minor=(0, 1, 2)))
    return lax.all_to_all(blocks, "seq", split_axis=0, concat_axis=0, tiled=True)


def rank_parts(arrived):
    return [arrived[place].astype(jnp.float32) for place in range(arrived.shape[0])]


def side_by_side(parts, first, width):
    return jnp.concatenate([part[:, first : first + width] for part in parts], axis=1)


def body(
    seq_count,
    fsdp_count,
    hidden_in,
    segments,
    out_grad,
    norm1_gain,
    w_query,
    w_keyval,
    w_attn_out,
    w_gate_z,
    w_ssm_x,
    w_ssm_bc,
    w_ssm_dt,
    conv_taps,
    a_log,
    dt_bias,
    skip_gain,
    ssm_gain,
    w_ssm_out,
    norm2_gain,
    w_ff_gate,
    w_ff_up,
    w_ff_down,
):
    f32, bf16 = jnp.float32, jnp.bfloat16
    batch, block_len, model_width = hidden_in.shape
    length = block_len * seq_count
    rank = lax.axis_index("seq")
    seg_row = segments[0]
    heads_local = HEADS // seq_count
    group_size = HEADS // KV_HEADS
    q_width = w_query.shape[1] // seq_count
    z_width = w_gate_z.shape[1] // seq_count
    x_width = w_ssm_x.shape[1] // seq_count
    bc_width = w_ssm_bc.shape[1] // seq_count
    dt_width = w_ssm_dt.shape[1] // seq_count
    ff_width = w_ff_gate.shape[1] // seq_count
    kv_total = w_keyval.shape[1] // 2
    heads_total = a_log.shape[0]
    dssm = w_ssm_x.shape[1]
    row_piece = w_query.shape[0]
    bc_pad = -bc_width % LANES
    dt_pad = -dt_width % LANES

    def pack(vector):
        parts = -(-vector.shape[0] // row_piece)
        padded = jnp.pad(vector, (0, parts * row_piece - vector.shape[0]))
        return [padded[part * row_piece : (part + 1) * row_piece] for part in range(parts)]

    def unpack(columns, length_each):
        spread = columns.reshape(columns.shape[0], -1, row_piece).transpose(1, 0, 2)
        return spread.reshape(spread.shape[0], -1)[:, :length_each].reshape(-1)

    extra_columns = [norm1_gain, norm2_gain] + pack(ssm_gain)
    ssm_pieces = len(extra_columns) - 2
    for tap in range(conv_taps.shape[1]):
        extra_columns += pack(conv_taps[:, tap])
    taps_pieces = (len(extra_columns) - 2 - ssm_pieces) // conv_taps.shape[1]
    extra_block = jnp.pad(
        jnp.stack(extra_columns, axis=1), ((0, 0), (0, dt_pad - len(extra_columns)))
    )
    free_first = q_width + 2 * HEAD_DIM + x_width + bc_width + bc_pad + dt_width
    sends = []
    for target in range(seq_count):
        kv_head = target * heads_local // group_size
        sends.append(
            jnp.concatenate(
                [
                    w_query[:, target * q_width : (target + 1) * q_width],
                    w_keyval[:, kv_head * HEAD_DIM : (kv_head + 1) * HEAD_DIM],
                    w_keyval[:, kv_total + kv_head * HEAD_DIM : kv_total + (kv_head + 1) * HEAD_DIM],
                    w_ssm_x[:, target * x_width : (target + 1) * x_width],
                    w_ssm_bc[:, target * bc_width : (target + 1) * bc_width],
                    jnp.zeros((row_piece, bc_pad), bf16),
                    w_ssm_dt[:, target * dt_width : (target + 1) * dt_width],
                    extra_block,
                ],
                axis=1,
            )
        )
    narrow_piece = columns_exchange(jnp.stack(sends))
    narrow_w = rows_of_all(narrow_piece)
    extras = lax.slice_in_dim(narrow_w, free_first, free_first + len(extra_columns), axis=1).T
    extras = extras.astype(f32)
    gain1, gain2 = extras[0], extras[1]
    taps_rows, taps_width = conv_taps.shape
    ssm_count = ssm_gain.shape[0]
    gain_ssm = unpack(extras[2 : 2 + ssm_pieces], ssm_count)
    gain_ssm = lax.dynamic_slice_in_dim(gain_ssm, rank * z_width, z_width, 0)
    taps = [
        unpack(extras[first : first + taps_pieces], taps_rows)
        for first in range(2 + ssm_pieces, len(extra_columns), taps_pieces)
    ]
    taps_rows8 = jnp.pad(jnp.stack(taps), ((0, 8 - taps_width), (0, 0)))
    x_taps = lax.dynamic_slice_in_dim(taps_rows8, rank * x_width, x_width, 1)
    bc_taps = taps_rows8[:, dssm:]
    head_rows = lax.dynamic_slice_in_dim(
        jnp.stack([a_log, dt_bias, skip_gain]), rank * dt_width, dt_width, 1
    )
    head_rows = jnp.pad(head_rows, ((0, 5), (0, dt_pad)))
    marks = document_marks(seg_row)
    seg_line = jnp.broadcast_to(seg_row.astype(f32)[None, :], (8, length))

    to_true = lax.dynamic_index_in_dim(jnp.asarray(row_tables(seq_count)), rank, 0, False)
    pieces = 2 * seq_count

    own_in = hidden_in.reshape(block_len, model_width)
    narrow_piece, own_in = lax.optimization_barrier((narrow_piece, own_in))
    all_in = jnp.concatenate(rows_gather(own_in, seq_count), axis=0)
    all_in, w_gate_z, w_ff_gate, w_ff_up, w_attn_out, w_ssm_out = lax.optimization_barrier(
        (all_in, w_gate_z, w_ff_gate, w_ff_up, w_attn_out, w_ssm_out)
    )
    wide_piece = columns_exchange(
        jnp.stack(
            [
                jnp.concatenate(
                    [
                        w_gate_z[:, target * z_width : (target + 1) * z_width],
                        w_ff_gate[:, target * ff_width : (target + 1) * ff_width],
                        w_ff_up[:, target * ff_width : (target + 1) * ff_width],
                    ],
                    axis=1,
                )
                for target in range(seq_count)
            ]
        )
    )
    z_piece, ff_piece = wide_piece[:, :, :z_width], wide_piece[:, :, z_width:]
    z_w = rows_of_all(z_piece)
    out_piece = jnp.concatenate([w_attn_out, w_ssm_out], axis=0)
    z_piece, out_piece = lax.optimization_barrier((z_piece, out_piece))
    out_w = lax.all_gather(out_piece, "fsdp", axis=0)

    cosine, sine = rope_wide(length)
    all_in, cosine, sine, marks, seg_line, to_true = lax.optimization_barrier(
        (all_in, cosine, sine, marks, seg_line, to_true)
    )
    ff_w = rows_of_all(ff_piece)
    normed, _ = norm_forward(all_in.astype(f32), gain1)
    edges = [0]
    for width in (q_width, HEAD_DIM, HEAD_DIM, x_width, bc_width + bc_pad, dt_width + dt_pad):
        edges.append(edges[-1] + width)
    narrow = mat_product(normed, narrow_w).astype(bf16)
    narrow, out_grad = lax.optimization_barrier((narrow, out_grad))
    grad_own = out_grad.reshape(block_len, model_width)
    grad_ff = gather_first(grad_own, seq_count)
    bc_seq = jnp.stack(seq_pieces(narrow[:, edges[4] : edges[4] + bc_width], seq_count))
    attn_rel, lse_seq = attention_forward(
        q_width, pieces, to_true, narrow, cosine, sine, marks, seg_line
    )
    bc_seq, attn_rel, w_ff_down, grad_ff = lax.optimization_barrier(
        (bc_seq, attn_rel, w_ff_down, grad_ff)
    )
    grad_ff = gather_last(grad_ff, seq_count)
    down_w = lax.all_gather(w_ff_down, "fsdp", axis=0, tiled=True)
    mixer_args = (x_taps, bc_taps, head_rows)
    ssm_rel = mixer_forward(
        edges[3], x_width, to_true, narrow, bc_seq, marks, seg_line, *mixer_args
    )
    ssm_rel, z_w, grad_ff = lax.optimization_barrier((ssm_rel, z_w, grad_ff))
    ssm_rel = ssm_rel.astype(f32)
    gate_z = mat_product(normed, z_w)
    gate_sig = jax.nn.sigmoid(gate_z)
    gate_silu = gate_z * gate_sig
    gated = ssm_rel * gate_silu
    square_sum = seq_sum(jnp.sum(gated * gated, axis=1), seq_count)
    gated_scale = lax.rsqrt(square_sum / dssm + epsilon)[:, None]
    ssm_in = (gated * gated_scale * gain_ssm).astype(bf16)
    ssm_in, out_w = lax.optimization_barrier((ssm_in, out_w))
    attn_out_w = out_w[:, : w_attn_out.shape[0]].reshape(-1, model_width)
    ssm_out_w = out_w[:, w_attn_out.shape[0] :].reshape(-1, model_width)
    near = length // 2

    def out_product(first):
        rows = slice(first, first + near)
        return mat_product(attn_rel[rows], attn_out_w) + mat_product(ssm_in[rows], ssm_out_w)

    xin = own_in.astype(f32)
    middle = xin + rows_scatter(out_product(0), out_product(near), seq_count)

    own_normed2, scale2 = norm_forward(middle, gain2)
    normed2 = rows_gather(own_normed2, seq_count)

    def ff_forward(rows):
        gate_ff = mat_product(rows, ff_w[:, :ff_width])
        up_ff = mat_product(rows, ff_w[:, ff_width:])
        ff_sig = jax.nn.sigmoid(gate_ff)
        ff_silu = gate_ff * ff_sig
        return up_ff, ff_sig, ff_silu, (ff_silu * up_ff).astype(bf16), gate_ff

    def ff_backward(grad_rows, up_ff, ff_sig, ff_silu):
        grad_act = input_grad(grad_rows, down_w)
        grad_gate_ff = grad_act * up_ff * (ff_sig + ff_silu * (1.0 - ff_sig))
        grad_up_ff = grad_act * ff_silu
        return jnp.concatenate([grad_gate_ff.astype(bf16), grad_up_ff.astype(bf16)], axis=1)

    up_near, sig_near, silu_near, act_near, gate_near = ff_forward(normed2[0])
    normed2_far, act_near, up_near, gate_near = lax.optimization_barrier(
        (normed2[1], act_near, up_near, gate_near)
    )
    sig_near = jax.nn.sigmoid(gate_near)
    silu_near = gate_near * sig_near
    up_far, sig_far, silu_far, act_far, gate_far = ff_forward(normed2_far)
    act = jnp.concatenate([act_near, act_far], axis=0)
    grad_ff_all = jnp.concatenate(grad_ff, axis=0)
    normed2_all = jnp.concatenate([normed2[0], normed2_far], axis=0)
    act, grad_ff_all = lax.optimization_barrier((act, grad_ff_all))
    grad_w_down = weight_grad(act, grad_ff_all).astype(bf16)
    grad_ff_far, grad_w_down = lax.optimization_barrier((grad_ff[1], grad_w_down))
    grad_w_down = lax.psum_scatter(grad_w_down, "fsdp", scatter_dimension=0, tiled=True)
    pair_far = ff_backward(grad_ff_far, up_far, sig_far, silu_far)
    pair_far = lax.optimization_barrier(pair_far)
    normed2_grad_far = input_grad(pair_far, ff_w).astype(bf16)
    grad_ff_near, normed2_grad_far = lax.optimization_barrier((grad_ff[0], normed2_grad_far))
    pair_near = ff_backward(grad_ff_near, up_near, sig_near, silu_near)
    pair_near = lax.optimization_barrier(pair_near)
    normed2_grad_near = input_grad(pair_near, ff_w)
    grad_pair = jnp.concatenate([pair_near, pair_far], axis=0)
    grad_pair, normed2_all = lax.optimization_barrier((grad_pair, normed2_all))
    grad_w_ff = weight_grad(normed2_all, grad_pair).astype(bf16)
    grad_w_ff = lax.psum_scatter(
        grad_w_ff.reshape(seq_count, -1, 2 * ff_width), "fsdp", scatter_dimension=1, tiled=True
    )
    grad_normed2 = rows_scatter(normed2_grad_near, normed2_grad_far, seq_count)
    grad_normed2, grad_w_down = lax.optimization_barrier((grad_normed2, grad_w_down))
    grad_middle_norm = norm_backward(middle, scale2, gain2, grad_normed2)
    grad_middle = grad_own.astype(f32) + grad_middle_norm

    mix_near, mix_far = rows_gather(grad_middle.astype(bf16), seq_count)
    ff_near = mat_product(act[:near], down_w)
    ff_far = mat_product(act[near:], down_w).astype(bf16)
    mix_far, ff_near, ff_far = lax.optimization_barrier((mix_far, ff_near, ff_far))
    grad_mix = jnp.concatenate([mix_near, mix_far], axis=0)
    grad_attn = input_grad(grad_mix, attn_out_w).astype(bf16)
    grad_ssm_in = input_grad(grad_mix, ssm_out_w)
    grad_w_attn = weight_grad(attn_rel, grad_mix).astype(bf16)
    grad_w_ssm = weight_grad(ssm_in, grad_mix).astype(bf16)
    weighted = grad_ssm_in * gain_ssm
    inner = seq_sum(jnp.sum(gated * weighted, axis=1), seq_count)
    out_grads = jnp.concatenate(
        [
            grad_w_attn.reshape(fsdp_count, -1, model_width),
            grad_w_ssm.reshape(fsdp_count, -1, model_width),
        ],
        axis=1,
    )
    grad_qkv = attention_backward(
        q_width, pieces, to_true, narrow, grad_attn, cosine, sine, marks, seg_line, lse_seq
    )
    inner, out_grads = lax.optimization_barrier((inner, out_grads))
    out_grads = lax.psum_scatter(out_grads, "fsdp", scatter_dimension=0, tiled=True)[0]
    inner = inner[:, None] / dssm
    grad_gated = gated_scale * weighted - gated * (
        gated_scale * gated_scale * gated_scale * inner
    )
    grad_ssm = (grad_gated * gate_silu).astype(bf16)
    grad_z = (grad_gated * ssm_rel * (gate_sig + gate_silu * (1.0 - gate_sig))).astype(bf16)
    grad_zq = lax.optimization_barrier(jnp.concatenate([grad_z, grad_qkv], axis=1))
    grad_w_zq = weight_grad(normed, grad_zq).astype(bf16)
    grad_ssm, grad_w_zq, ff_far, grad_w_ff = lax.optimization_barrier(
        (grad_ssm, grad_w_zq, ff_far, grad_w_ff)
    )
    grad_w_zq = lax.psum_scatter(
        grad_w_zq.reshape(seq_count, -1, grad_zq.shape[1]),
        "fsdp",
        scatter_dimension=1,
        tiled=True,
    )
    ff_came = scatter_first(ff_far, seq_count)
    grad_x, grad_dt, grad_bc_part, grad_x_taps, grad_bc_taps, grad_heads = mixer_backward(
        edges[3], x_width, to_true, narrow, bc_seq, grad_ssm, marks, seg_line, *mixer_args
    )
    grad_w_ff, grad_bc_part, ff_came = lax.optimization_barrier(
        (grad_w_ff, grad_bc_part, ff_came)
    )
    ff_cols = columns_to_owners(grad_w_ff)
    grad_bc = grad_bc_part[0].astype(f32)
    for bit in range(1, seq_count):
        grad_bc = grad_bc + swap_seq(grad_bc_part[bit], bit, seq_count).astype(f32)
    grad_bc = grad_bc.astype(bf16)
    ff_near, grad_bc = lax.optimization_barrier((ff_near, grad_bc))
    ff_kept, ff_arrived = scatter_second(ff_near, ff_came, seq_count)
    bc_zeros = jnp.zeros((length, bc_pad), bf16)
    grad_rest = jnp.concatenate([grad_x, grad_bc, bc_zeros, grad_dt], axis=1)
    grad_rest, out_grads, ff_cols = lax.optimization_barrier((grad_rest, out_grads, ff_cols))
    per_device = (seq_count, fsdp_count, -1)
    x_conv = lax.dynamic_update_slice_in_dim(
        jnp.zeros((dssm, taps_width), f32), grad_x_taps[:taps_width].T, rank * x_width, 0
    )
    conv_grads = jnp.concatenate([x_conv, grad_bc_taps[:taps_width].T], axis=0).reshape(per_device)
    head_grads = lax.dynamic_update_slice(
        jnp.zeros((3, heads_total), f32),
        grad_heads[:3, :dt_width],
        (jnp.int32(0), rank * dt_width),
    )
    head_grads = jnp.broadcast_to(
        head_grads.reshape(1, 1, -1), (seq_count, fsdp_count, 3 * heads_total)
    )
    smalls = jnp.concatenate([conv_grads, head_grads], axis=2)
    small_count = smalls.shape[2]
    small_columns = -(-small_count // row_piece)
    smalls = jnp.pad(smalls, ((0, 0), (0, 0), (0, small_columns * row_piece - small_count)))
    smalls = smalls.reshape(model_width, small_columns)
    small_first = x_width + bc_width + bc_pad + dt_width
    small_room = grad_rest.shape[1] - small_first - small_columns
    smalls = jnp.pad(smalls, ((0, 0), (small_first, small_room)))
    grad_w_rest = (weight_grad(normed, grad_rest) + smalls).astype(bf16)
    grad_rest, grad_w_rest, grad_z, grad_qkv, ff_arrived = lax.optimization_barrier(
        (grad_rest, grad_w_rest, grad_z, grad_qkv, ff_arrived)
    )
    grad_w_rest = lax.psum_scatter(
        grad_w_rest.reshape(seq_count, -1, grad_rest.shape[1]),
        "fsdp",
        scatter_dimension=1,
        tiled=True,
    )

    def first_product(first):
        rows = slice(first, first + near)
        return (
            input_grad(grad_rest[rows], narrow_w[:, edges[3] :])
            + input_grad(grad_z[rows], z_w)
            + input_grad(grad_qkv[rows], narrow_w[:, : edges[3]])
        )

    grad_normed_far = first_product(near).astype(bf16)
    zq_cols = columns_to_owners(grad_w_zq)
    grad_normed_far, grad_rest, grad_z, grad_qkv = lax.optimization_barrier(
        (grad_normed_far, grad_rest, grad_z, grad_qkv)
    )
    normed_came = scatter_first(grad_normed_far, seq_count)
    grad_normed_near, zq_cols = lax.optimization_barrier((first_product(0), zq_cols))
    normed_kept, normed_arrived = scatter_second(grad_normed_near, normed_came, seq_count)
    normed_kept, ff_kept, ff_cols, out_grads = lax.optimization_barrier(
        (normed_kept, ff_kept, ff_cols, out_grads)
    )
    layer_out = middle + scatter_last(ff_kept, ff_arrived)
    grad_normed = scatter_last(normed_kept, normed_arrived)
    _, scale1 = norm_forward(xin, gain1)
    grad_in_norm = norm_backward(xin, scale1, gain1, grad_normed)
    grad_in = (grad_middle + grad_in_norm).astype(bf16)
    grad_in, grad_w_rest = lax.optimization_barrier((grad_in, grad_w_rest))

    ff_cols = rank_parts(ff_cols)
    zq_cols = rank_parts(zq_cols)
    rest_cols = rank_parts(columns_to_owners(grad_w_rest))
    bc_first = x_width
    dt_first = bc_first + bc_width + bc_pad
    small = sum(part[:, small_first : small_first + small_columns] for part in rest_cols)
    small = small.reshape(-1)[:small_count]
    taps_total = taps_rows * taps_width
    out_conv = small[:taps_total]
    out_heads = small[taps_total:].reshape(3, heads_total)
    ranks_per_kv = group_size // heads_local
    kv_cols = []
    for first in (z_width + edges[1], z_width + edges[2]):
        for head in range(KV_HEADS):
            shares = zq_cols[head * ranks_per_kv : (head + 1) * ranks_per_kv]
            kv_cols.append(sum(share[:, first : first + HEAD_DIM] for share in shares))
    attn_rows = w_attn_out.shape[0]
    grad_query = side_by_side(zq_cols, z_width, q_width)
    grad_keyval = jnp.concatenate(kv_cols, axis=1)
    grad_gate_z = side_by_side(zq_cols, 0, z_width)
    grad_ssm_x = side_by_side(rest_cols, 0, x_width)
    grad_ssm_bc = side_by_side(rest_cols, bc_first, bc_width)
    grad_ssm_dt = side_by_side(rest_cols, dt_first, dt_width)
    grad_ff_gate = side_by_side(ff_cols, 0, ff_width)
    grad_ff_up = side_by_side(ff_cols, ff_width, ff_width)
    grad_attn_out = out_grads[:attn_rows].astype(f32)
    grad_ssm_out = out_grads[attn_rows:].astype(f32)

    def gain_grad(gain, *pairs):
        total = sum(jnp.sum(weight.astype(f32) * grad, axis=1) for weight, grad in pairs)
        return total / gain.astype(f32)

    out_gain1 = gain_grad(
        norm1_gain,
        (w_query, grad_query),
        (w_keyval, grad_keyval),
        (w_gate_z, grad_gate_z),
        (w_ssm_x, grad_ssm_x),
        (w_ssm_bc, grad_ssm_bc),
        (w_ssm_dt, grad_ssm_dt),
    )
    out_gain2 = gain_grad(norm2_gain, (w_ff_gate, grad_ff_gate), (w_ff_up, grad_ff_up))
    out_ssm_gain = gain_grad(ssm_gain, (w_ssm_out, grad_ssm_out))
    return (
        layer_out.astype(bf16).reshape(batch, block_len, model_width),
        grad_in.reshape(batch, block_len, model_width),
        out_gain1,
        grad_query,
        grad_keyval,
        grad_attn_out,
        grad_gate_z,
        grad_ssm_x,
        grad_ssm_bc,
        grad_ssm_dt,
        out_conv.reshape(taps_rows, taps_width),
        out_heads[0],
        out_heads[1],
        out_heads[2],
        out_ssm_gain,
        grad_ssm_out,
        out_gain2,
        grad_ff_gate,
        grad_ff_up,
        grad_w_down.astype(f32),
    )


def solution(mesh):
    in_specs = (
        P("fsdp", "seq", None),
        P("fsdp", None),
        P("fsdp", "seq", None),
        P(("seq", "fsdp")),
        P(("seq", "fsdp"), None),
        P(("seq", "fsdp"), None),
        P(("seq", "fsdp"), None),
        P(("seq", "fsdp"), None),
        P(("seq", "fsdp"), None),
        P(("seq", "fsdp"), None),
        P(("seq", "fsdp"), None),
        P(("seq", "fsdp"), None),
        P(),
        P(),
        P(),
        P(("seq", "fsdp")),
        P(("seq", "fsdp"), None),
        P(("seq", "fsdp")),
        P(("seq", "fsdp"), None),
        P(("seq", "fsdp"), None),
        P(("seq", "fsdp"), None),
    )
    out_specs = (
        P("fsdp", "seq", None),
        P("fsdp", "seq", None),
        P(("seq", "fsdp")),
        P(("seq", "fsdp"), None),
        P(("seq", "fsdp"), None),
        P(("seq", "fsdp"), None),
        P(("seq", "fsdp"), None),
        P(("seq", "fsdp"), None),
        P(("seq", "fsdp"), None),
        P(("seq", "fsdp"), None),
        P(("seq", "fsdp"), None),
        P(),
        P(),
        P(),
        P(("seq", "fsdp")),
        P(("seq", "fsdp"), None),
        P(("seq", "fsdp")),
        P(("seq", "fsdp"), None),
        P(("seq", "fsdp"), None),
        P(("seq", "fsdp"), None),
    )
    step = functools.partial(body, mesh.shape["seq"], mesh.shape["fsdp"])
    return jax.shard_map(step, mesh=mesh, in_specs=in_specs, out_specs=out_specs, check_vma=False)
```
